512 devices in a mesh: modes: 4 (over y_lo), elems: 128 (over z, y_hi, x, core).
Axes of the slice: x: 4, y: 8 (y_hi: 2, y_lo: 4; y = y_hi * 4 + y_lo), z: 8, core: 2. Of those that a mesh axis runs over, the one named last changes fastest.
Arguments:
- state: float32 [512, 3, 2, 64, 512], P('elems', None, None, None, 'modes'), may hold values from -3 to 3
- adjoint_end: float32 [512, 3, 2, 64, 512], P('elems', None, None, None, 'modes'), may hold values from -6 to 6
- observed: bfloat16 [512, 3, 2, 64, 512], P('elems', None, None, None, 'modes'), may hold values from -3 to 3
- spacing: float32 [512, 2], P('elems'), may hold values from 0.5 to 2
- radial_slot: int32 [128, 4], P('elems'), may hold values from 0 to 3, each once within a row
Outputs:
- next_state: float32 [512, 3, 2, 64, 512], P('elems', None, None, None, 'modes')
- adjoint_start: float32 [512, 3, 2, 64, 512], P('elems', None, None, None, 'modes')
The draws below stay inside these ranges and needn't reach their ends.
Inputs may be any that keep to these rules, and one draw needn't show every extreme that they name: `radial_slot`: each row lists every radial row 0 to 3 once.
All inputs are finite; a program needn't handle non-finite values.
Results may differ from the reference program's by a relative error of at most 0.017.
Values may be sent and summed in bfloat16 or wider, within the bound.
A program may use at most 64 MiB of HBM per device.

```python
import math
import jax
import jax.numpy as jnp
import numpy as np
from jax import lax

MODES = 512
GLL = 8
ER = 4
SLABS = 128
ELEMS = 512


def level_of(key, extent, cuts, smallest, top_value):
    def one(axis_at, shards_of):
        steps = jax.random.uniform(jax.random.fold_in(jax.random.fold_in(key, 6), axis_at), (shards_of,), jnp.float32, smallest / len(cuts), top_value / len(cuts))
        return jnp.repeat(jnp.exp(steps), extent[axis_at] // shards_of).reshape((-1,) + (1,) * (len(extent) - axis_at - 1))

    gain = one(*cuts[0])
    for cut in cuts[1:]:
        gain = gain * one(*cut)
    return gain


def normal_values(stream_key, extent, scale, bound, cuts=(), kind=jnp.bfloat16):
    entries = jax.random.normal(stream_key, extent, jnp.float32) * scale
    if len(cuts) > 0:
        entries = level_of(stream_key, extent, cuts, -0.22, 0.18) * entries
    return jnp.clip(entries, min=-bound, max=bound).astype(kind)


def setup_inputs(seed: int = 0) -> dict:
    key_of = jax.random.split(jax.random.key(seed), 6)
    state = normal_values(key_of[0], (ELEMS, 3, 2, GLL * GLL, MODES), 0.5, 3.0, ((0, 128), (4, 4)), jnp.float32)
    adjoint_end = normal_values(key_of[1], (ELEMS, 3, 2, GLL * GLL, MODES), 1.0, 6.0, ((0, 128), (4, 4)), jnp.float32)
    observed = normal_values(key_of[2], (ELEMS, 3, 2, GLL * GLL, MODES), 0.5, 3.0, ((0, 128), (4, 4)))
    spacing = jnp.clip(jnp.exp(math.log(2.0) - 1.3862944 * jax.random.uniform(key_of[3], (ELEMS, 2), jnp.float32) ** level_of(key_of[3], (ELEMS, 2), ((0, 128),), -0.2, 0.2)), 0.5, 2.0)
    radial_slot = jax.vmap(lambda own: jax.random.permutation(own, ER))(jax.random.split(key_of[4], SLABS)).reshape((SLABS, ER)).astype(jnp.int32)
    return {"state": state, "adjoint_end": adjoint_end, "observed": observed, "spacing": spacing, "radial_slot": radial_slot}


time_step = 0.01
viscosity = 0.05
wave_scale = 4.0
exact_precision = lax.Precision.HIGHEST
pair_order = ((0, 0), (0, 1), (0, 2), (1, 1), (1, 2), (2, 2))
pair_index = ((0, 1, 2), (1, 3, 4), (2, 4, 5))


def legendre_table(points, quad_count):
    columns = [points * 0.0 + 1.0, points]
    for degree in range(2, quad_count):
        columns.append(((2 * degree - 1) * points * columns[-1] - (degree - 1) * columns[-2]) / degree)
    return np.stack(columns, axis=1)


def gll_tables(quad_count):
    degree = quad_count - 1
    points = -np.cos(np.pi * np.arange(quad_count) / degree)
    for repeat in range(60):
        vander = legendre_table(points, quad_count)
        points = points - (points * vander[:, degree] - vander[:, degree - 1]) / (quad_count * vander[:, degree])
    vander = legendre_table(points, quad_count)
    edge_value = vander[:, degree]
    weights = 2.0 / (degree * quad_count * edge_value * edge_value)
    diagonal_mask = np.arange(quad_count)[:, None] == np.arange(quad_count)[None, :]
    differ = np.where(diagonal_mask, 1.0, points[:, None] - points[None, :])
    derivative = np.where(diagonal_mask, 0.0, edge_value[:, None] / (edge_value[None, :] * differ))
    derivative[0, 0] = -degree * quad_count / 4.0
    derivative[degree, degree] = degree * quad_count / 4.0
    return weights, derivative


def fourier_tables(mode_total, plane_total):
    product = np.outer(np.arange(mode_total), np.arange(plane_total)) % plane_total
    angles = 2.0 * np.pi * product / plane_total
    factor = np.where(np.arange(mode_total) == 0, 1.0, 2.0)[:, None]
    synthesis = np.stack((factor * np.cos(angles), -factor * np.sin(angles)))
    analysis_field = np.stack((np.cos(angles), -np.sin(angles))) / plane_total
    return synthesis, np.transpose(analysis_field, (2, 0, 1))


def quad_weights(spacing, weights):
    area = spacing[:, 0] * spacing[:, 1] * 0.25
    return (area[:, None, None] * weights[:, None] * weights[None, :])[:, None, None, :, :, None]


def along_first(matrix, values):
    return jnp.einsum('xa,ecpabm->ecpxbm', matrix, values, precision=exact_precision)


def along_second(matrix, values):
    return jnp.einsum('yb,ecpabm->ecpaym', matrix, values, precision=exact_precision)


def span_derivative(values, wave_num):
    return jnp.stack((-wave_num * values[:, :, 1], wave_num * values[:, :, 0]), axis=2)


def side_scales(spacing):
    scale_x = (2.0 / spacing[:, 0])[:, None, None, None, None, None]
    scale_y = (2.0 / spacing[:, 1])[:, None, None, None, None, None]
    return scale_x, scale_y


def viscous_term(values, spacing, weights, derivative, wave_num):
    quad_wts = quad_weights(spacing, weights)
    scale_x, scale_y = side_scales(spacing)
    grad_x = scale_x * along_first(derivative, values)
    grad_y = scale_y * along_second(derivative, values)
    lateral = scale_x * along_first(derivative.T, quad_wts * grad_x) + scale_y * along_second(derivative.T, quad_wts * grad_y)
    return -viscosity * (lateral + wave_num * wave_num * quad_wts * values)


def advect_term(pair_vals, spacing, weights, derivative, wave_num):
    quad_wts = quad_weights(spacing, weights)
    scale_x, scale_y = side_scales(spacing)
    flux_x = jnp.stack([pair_vals[:, pair_pos] for pair_pos in pair_index[0]], axis=1)
    flux_y = jnp.stack([pair_vals[:, pair_pos] for pair_pos in pair_index[1]], axis=1)
    flux_z = jnp.stack([pair_vals[:, pair_pos] for pair_pos in pair_index[2]], axis=1)
    lateral = scale_x * along_first(derivative.T, quad_wts * flux_x) + scale_y * along_second(derivative.T, quad_wts * flux_y)
    return lateral - quad_wts * span_derivative(flux_z, wave_num)


def pair_cotangent(psi_vals, spacing, weights, derivative, wave_num):
    quad_wts = quad_weights(spacing, weights)
    scale_x, scale_y = side_scales(spacing)
    cot_table = (quad_wts * scale_x * along_first(derivative, psi_vals),
                 quad_wts * scale_y * along_second(derivative, psi_vals),
                 quad_wts * span_derivative(psi_vals, wave_num))
    pair_list = [cot_table[left_idx][:, right_idx] + cot_table[right_idx][:, left_idx] for left_idx, right_idx in pair_order]
    return jnp.stack(pair_list, axis=1)


def product_pairs(planes):
    return jnp.stack([planes[:, left_idx] * planes[:, right_idx] for left_idx, right_idx in pair_order], axis=1)


def combine_pairs(spread_modes, planes):
    outputs = []
    for comp_idx in range(3):
        total = spread_modes[:, pair_index[comp_idx][0]] * planes[:, 0]
        total = total + spread_modes[:, pair_index[comp_idx][1]] * planes[:, 1]
        total = total + spread_modes[:, pair_index[comp_idx][2]] * planes[:, 2]
        outputs.append(total)
    return jnp.stack(outputs, axis=1)


def radial_sum(grid_vals, elem_axis, b_axis):
    layer_count = grid_vals.shape[b_axis]
    row_count = grid_vals.shape[elem_axis]
    top_layer = lax.slice_in_dim(grid_vals, layer_count - 1, layer_count, axis=b_axis)
    low_layer = lax.slice_in_dim(grid_vals, 0, 1, axis=b_axis)
    zero_row = jnp.zeros_like(lax.slice_in_dim(top_layer, 0, 1, axis=elem_axis))
    from_above = jnp.concatenate((lax.slice_in_dim(low_layer, 1, row_count, axis=elem_axis), zero_row), axis=elem_axis)
    from_below = jnp.concatenate((zero_row, lax.slice_in_dim(top_layer, 0, row_count - 1, axis=elem_axis)), axis=elem_axis)
    middle = lax.slice_in_dim(grid_vals, 1, layer_count - 1, axis=b_axis)
    return jnp.concatenate((low_layer + from_below, middle, top_layer + from_above), axis=b_axis)


def assemble_global(values, radial_slot):
    onehot = (radial_slot[:, :, None] == jnp.arange(ER, dtype=jnp.int32)[None, None, :]).astype(jnp.float32)
    grid_vals = jnp.einsum('sjr,sjcpabm->srcpabm', onehot, values, precision=exact_precision)
    grid_vals = radial_sum(grid_vals, 1, 5)
    first_layer = grid_vals[:, :, :, :, 0:1]
    last_layer = grid_vals[:, :, :, :, GLL - 1:GLL]
    new_first = first_layer + jnp.roll(last_layer, 1, axis=0)
    new_last = last_layer + jnp.roll(first_layer, -1, axis=0)
    grid_vals = jnp.concatenate((new_first, grid_vals[:, :, :, :, 1:GLL - 1], new_last), axis=4)
    return jnp.einsum('sjr,srcpabm->sjcpabm', onehot, grid_vals, precision=exact_precision)


def to_planes(low_vals, synthesis):
    flat = low_vals.reshape(low_vals.shape[0], low_vals.shape[1], 2, GLL * GLL, MODES)
    return jnp.einsum('ecpnm,pmq->ecnq', flat.astype(jnp.float32), synthesis.astype(jnp.float32), precision=exact_precision)


def reference(state, adjoint_end, observed, spacing, radial_slot):
    weights_np, deriv_np = gll_tables(GLL)
    synth_np, analysis_np = fourier_tables(MODES, 3 * MODES)
    weights = jnp.asarray(weights_np, jnp.float32)
    derivative = jnp.asarray(deriv_np, jnp.float32)
    synthesis = jnp.asarray(synth_np, jnp.float32).astype(jnp.bfloat16)
    analysis_field = jnp.asarray(analysis_np, jnp.float32).astype(jnp.bfloat16)
    wave_num = wave_scale * jnp.arange(MODES, dtype=jnp.float32) / MODES
    shaped = (SLABS, ER, 3, 2, GLL, GLL, MODES)
    blocks = state.reshape(shaped)
    geometry = spacing.reshape(SLABS, ER, 2)

    def forward_block(pieces):
        block_vals, geom_vals = pieces
        planes = to_planes(block_vals.astype(jnp.bfloat16), synthesis)
        pair_physical_values = product_pairs(planes).astype(jnp.bfloat16)
        pair_spectral_coefficients = jnp.einsum('abry,yuw->aburw', pair_physical_values.astype(jnp.float32), analysis_field.astype(jnp.float32), precision=exact_precision).astype(jnp.bfloat16)
        pair_spectral_coefficients = pair_spectral_coefficients.reshape(ER, 6, 2, GLL, GLL, MODES)
        advect = advect_term(pair_spectral_coefficients.astype(jnp.float32), geom_vals, weights, derivative, wave_num).astype(jnp.bfloat16)
        quad_wts = quad_weights(geom_vals, weights)
        return quad_wts * block_vals + time_step * (viscous_term(block_vals, geom_vals, weights, derivative, wave_num) + advect.astype(jnp.float32))

    numerator = lax.map(forward_block, (blocks, geometry))
    quad_all = quad_weights(spacing, weights).reshape(SLABS, ER, 1, 1, GLL, GLL, 1)
    mass = assemble_global(quad_all, radial_slot)
    wall_rows = (radial_slot == 0).astype(jnp.float32)[:, :, None, None, None, None, None]
    wall_cols = (jnp.arange(GLL, dtype=jnp.int32) == 0).astype(jnp.float32)[None, None, None, None, None, :, None]
    wall_mask = 1.0 - wall_rows * wall_cols
    next_state = wall_mask * assemble_global(numerator, radial_slot) / mass
    forcing = adjoint_end.reshape(shaped) + (next_state - observed.reshape(shaped).astype(jnp.float32))
    psi_field = assemble_global(wall_mask * forcing / mass, radial_slot)

    def adjoint_block(pieces):
        block_vals, psi_vals, geom_vals = pieces
        planes = to_planes(block_vals.astype(jnp.bfloat16), synthesis)
        psi_low = psi_vals.astype(jnp.bfloat16)
        pair_adjoint_values = pair_cotangent(psi_low.astype(jnp.float32), geom_vals, weights, derivative, wave_num).astype(jnp.bfloat16)
        pair_adjoint_values = pair_adjoint_values.reshape(ER, 6, 2, GLL * GLL, MODES)
        spread_modes = jnp.einsum('voyjg,zyg->vojz', pair_adjoint_values.astype(jnp.float32), analysis_field.astype(jnp.float32), precision=exact_precision)
        planes_cot = combine_pairs(spread_modes, planes).astype(jnp.bfloat16)
        adjoint_adv = jnp.einsum('ecnq,pmq->ecpnm', planes_cot.astype(jnp.float32), synthesis.astype(jnp.float32), precision=exact_precision).astype(jnp.bfloat16)
        adjoint_adv = adjoint_adv.reshape(ER, 3, 2, GLL, GLL, MODES)
        quad_wts = quad_weights(geom_vals, weights)
        return quad_wts * psi_vals + time_step * (viscous_term(psi_vals, geom_vals, weights, derivative, wave_num) + adjoint_adv.astype(jnp.float32))

    adjoint_start = lax.map(adjoint_block, (blocks, psi_field, geometry))
    return next_state.reshape(state.shape), adjoint_start.reshape(state.shape)
```

```python
import jax
import jax.numpy as jnp
import numpy as np
from jax import lax
from jax.experimental import pallas as pl
from jax.experimental.pallas import tpu as pltpu
from jax.sharding import PartitionSpec as P

GLL = 8
NODES = GLL * GLL
ROWS = 4
time_step = 0.01
viscosity = 0.05
wave_scale = 4.0
pair_order = ((0, 0), (0, 1), (0, 2), (1, 1), (1, 2), (2, 2))
pair_index = ((0, 1, 2), (1, 3, 4), (2, 4, 5))
F32 = jnp.float32
LOW = jnp.bfloat16
MESH = pl.DeviceIdType.MESH


def legendre_table(points, quad_count):
    columns = [points * 0.0 + 1.0, points]
    for degree in range(2, quad_count):
        columns.append(
            ((2 * degree - 1) * points * columns[-1] - (degree - 1) * columns[-2]) / degree
        )
    return np.stack(columns, axis=1)


def gll_tables(quad_count):
    degree = quad_count - 1
    points = -np.cos(np.pi * np.arange(quad_count) / degree)
    for repeat in range(60):
        vander = legendre_table(points, quad_count)
        points = points - (points * vander[:, degree] - vander[:, degree - 1]) / (
            quad_count * vander[:, degree]
        )
    vander = legendre_table(points, quad_count)
    edge_value = vander[:, degree]
    weights = 2.0 / (degree * quad_count * edge_value * edge_value)
    diagonal_mask = np.arange(quad_count)[:, None] == np.arange(quad_count)[None, :]
    differ = np.where(diagonal_mask, 1.0, points[:, None] - points[None, :])
    derivative = np.where(diagonal_mask, 0.0, edge_value[:, None] / (edge_value[None, :] * differ))
    derivative[0, 0] = -degree * quad_count / 4.0
    derivative[degree, degree] = degree * quad_count / 4.0
    return (weights, derivative)


def half_tables(modes, planes):
    half = planes // 2
    turns = np.outer(np.arange(modes), 2 * np.arange(half) + 1) % (2 * planes)
    angles = np.pi * turns / planes
    factor = np.where(np.arange(modes) == 0, 1.0, 2.0)[:, None]
    synth = np.stack((factor * np.cos(angles), -factor * np.sin(angles)))
    analysis = np.stack((np.cos(angles), -np.sin(angles))) * (2.0 / planes)
    return synth, np.transpose(analysis, (0, 2, 1))


def node_tables():
    weights, deriv = gll_tables(GLL)
    wdiag = np.diag(weights)
    back = deriv.T @ wdiag
    ahead = wdiag @ deriv
    stiff = deriv.T @ wdiag @ deriv
    zero = np.zeros((NODES, NODES))
    fwd = (
        np.concatenate((np.kron(back, wdiag), np.kron(wdiag, back), np.kron(stiff, wdiag)), 1),
        np.concatenate((zero, zero, np.kron(wdiag, stiff)), 1),
    )
    adj = (
        np.concatenate((np.kron(ahead, wdiag), np.kron(wdiag, ahead), np.kron(stiff, wdiag)), 0),
        np.concatenate((zero, zero, np.kron(wdiag, stiff)), 0),
    )
    return np.stack(fwd), np.stack(adj), np.kron(weights, weights)


def step_kernel(
    groups,
    slabs,
    state_ref, adj_ref, obs_ref, spacing_ref, slot_ref, synth_ref, anal_ref, fwd_ref, bwd_ref, w2_ref,
    next_ref, start_ref,
    state_v, adj_v, obs_v, synth_v, anal_v, fwd_v, bwd_v, w2_v,
    send_v, state_r, forcing_r, next_r, start_r, quad_v, scale_v, mult_v,
    even_v, odd_v, prod_v, modal_v, num_v, psi_v, cot_v, spread_v, pcot_v,
    edge_send, edge_recv, mass_send, mass_recv, out_v,
    load_sem, send_sem, recv_sem, esend_sem, erecv_sem, msend_sem, mrecv_sem, out_sem,
):
    member = lax.axis_index("modes")
    slab = lax.axis_index("elems")
    low_slab = lax.rem(slab + slabs - 1, slabs)
    high_slab = lax.rem(slab + 1, slabs)
    partners = (lax.rem(member + 2, 4), 3 - member, member + 1 - 2 * lax.rem(member, 2))
    modes = groups * 128
    recv = (state_r, forcing_r, next_r, start_r)

    loads = [
        pltpu.make_async_copy(src, dst, load_sem.at[i])
        for i, (src, dst) in enumerate(
            (
                (state_ref, state_v), (adj_ref, adj_v), (obs_ref, obs_v), (w2_ref, w2_v),
                (fwd_ref, fwd_v), (synth_ref, synth_v), (anal_ref, anal_v), (bwd_ref, bwd_v),
            )
        )
    ]
    for load in loads:
        load.start()

    barrier = pltpu.get_barrier_semaphore()
    for partner in partners:
        pl.semaphore_signal(barrier, inc=1, device_id={"modes": partner}, device_id_type=MESH)
    for near in (low_slab, high_slab):
        pl.semaphore_signal(barrier, inc=1, device_id={"elems": near}, device_id_type=MESH)

    slots = [slot_ref[0, j] for j in range(ROWS)]

    def flat(block):
        return block.reshape(6 * NODES, 128)

    def elem_of(row):
        place = jnp.int32(0)
        for j in range(1, ROWS):
            place = jnp.where(slots[j] == row, j, place)
        return place

    def swap(phase, partner):
        return pltpu.make_async_remote_copy(
            src_ref=send_v.at[phase, partner],
            dst_ref=recv[phase].at[member],
            send_sem=send_sem.at[phase, partner],
            recv_sem=recv_sem.at[phase, member],
            device_id={"modes": partner},
            device_id_type=MESH,
        )

    def swapped(phase, partner):
        return pltpu.make_async_remote_copy(
            src_ref=send_v.at[phase, partner],
            dst_ref=recv[phase].at[partner],
            send_sem=send_sem.at[phase, partner],
            recv_sem=recv_sem.at[phase, partner],
            device_id={"modes": partner},
            device_id_type=MESH,
        )

    loads[0].wait()
    pl.semaphore_wait(barrier, 5)
    for partner in partners:
        send_v[0, partner] = flat(state_v[elem_of(partner)]).astype(LOW)
        swap(0, partner).start()
    state_r[member] = flat(state_v[elem_of(member)]).astype(LOW)

    loads[3].wait()
    own = elem_of(member)
    above = elem_of(jnp.minimum(member + 1, ROWS - 1))
    below = elem_of(jnp.maximum(member - 1, 0))

    def area(elem):
        return spacing_ref[elem, 0] * spacing_ref[elem, 1] * 0.25

    side_x = spacing_ref[own, 0]
    side_y = spacing_ref[own, 1]
    full = (NODES, 128)
    layer = lax.rem(lax.broadcasted_iota(jnp.int32, full, 0), GLL)
    has_above = jnp.logical_and(layer == GLL - 1, member < ROWS - 1)
    has_below = jnp.logical_and(layer == 0, member > 0)
    w2 = w2_v[...]
    quad = w2 * area(own)
    quad_v[...] = quad
    mass = quad + jnp.where(has_above, w2 * area(above), 0.0)
    mass = mass + jnp.where(has_below, w2 * area(below), 0.0)
    scale_v[...] = mass
    mass_send[0] = mass[NODES - GLL :]
    mass_send[1] = mass[:GLL]

    def mass_copy(way):
        return pltpu.make_async_remote_copy(
            src_ref=mass_send.at[way],
            dst_ref=mass_recv.at[way],
            send_sem=msend_sem.at[way],
            recv_sem=mrecv_sem.at[way],
            device_id={"elems": (high_slab, low_slab)[way]},
            device_id_type=MESH,
        )

    mass_copy(0).start()
    mass_copy(1).start()
    copies = jnp.where(jnp.logical_or(has_above, has_below), 2.0, 1.0).astype(F32)
    node_a = lax.broadcasted_iota(jnp.int32, full, 0) // GLL
    mult_v[...] = jnp.where(jnp.logical_or(node_a == 0, node_a == GLL - 1), 2.0 * copies, copies)

    loads[1].wait()
    loads[2].wait()
    for partner in partners:
        elem = elem_of(partner)
        send_v[1, partner] = flat(adj_v[elem] - obs_v[elem].astype(F32)).astype(LOW)
    forcing_r[member] = flat(adj_v[own] - obs_v[own].astype(F32)).astype(LOW)

    mass_copy(0).wait()
    mass_copy(1).wait()
    scale_v[:GLL, :] = scale_v[:GLL, :] + mass_recv[0]
    scale_v[NODES - GLL :, :] = scale_v[NODES - GLL :, :] + mass_recv[1]
    at_wall = jnp.logical_and(layer == 0, member == 0)
    scale_v[...] = jnp.where(at_wall, 0.0, 1.0) / scale_v[...]

    loads[4].wait()
    loads[7].wait()
    lane = lax.broadcasted_iota(jnp.int32, (NODES, 3 * NODES), 1)
    ratio = jnp.full((NODES, 3 * NODES), side_y) / jnp.full((NODES, 3 * NODES), side_x)
    coef = jnp.where(
        lane < NODES, 0.5 * side_y, jnp.where(lane < 2 * NODES, 0.5 * side_x, -viscosity * ratio)
    )
    fwd_mat = (time_step * (fwd_v[0] * coef - fwd_v[1] * (viscosity / ratio))).astype(LOW)
    line = lax.broadcasted_iota(jnp.int32, (3 * NODES, NODES), 0)
    ratio = jnp.full((3 * NODES, NODES), side_y) / jnp.full((3 * NODES, NODES), side_x)
    coef = jnp.where(
        line < NODES, 0.5 * side_y, jnp.where(line < 2 * NODES, 0.5 * side_x, -viscosity * ratio)
    )
    bwd_mat = (bwd_v[0] * coef - bwd_v[1] * (viscosity / ratio)).astype(LOW)

    for partner in partners:
        swap(0, partner).wait_send()
        swap(1, partner).start()
    for partner in partners:
        swapped(0, partner).wait_recv()

    def rows_of(index, count=NODES):
        return pl.ds(index * count, count)

    def gathered(phase, i):
        return jnp.concatenate([recv[phase][q, rows_of(i), :] for q in range(groups)], axis=1)

    def wide(block):
        return jnp.concatenate([block] * groups, axis=1)

    def field(buf, i):
        return jnp.concatenate([buf[rows_of(6 * q + i), :] for q in range(groups)], axis=1)

    def set_field(buf, i, value):
        for q in range(groups):
            buf[rows_of(6 * q + i), :] = value[:, q * 128 : (q + 1) * 128]

    mode_ids = lax.broadcasted_iota(jnp.int32, (NODES, modes), 1)
    wave = mode_ids.astype(F32) * (wave_scale / modes)

    loads[5].wait()
    even_v[...] = jnp.dot(
        jnp.concatenate([gathered(0, 2 * c) for c in range(3)], axis=0),
        synth_v[0],
        preferred_element_type=F32,
    )
    odd_v[...] = jnp.dot(
        jnp.concatenate([gathered(0, 2 * c + 1) for c in range(3)], axis=0),
        synth_v[1],
        preferred_element_type=F32,
    )

    for q, (left, right) in enumerate(pair_order):
        el, ol = even_v[rows_of(left), :], odd_v[rows_of(left), :]
        er, orr = even_v[rows_of(right), :], odd_v[rows_of(right), :]
        prod_v[0, rows_of(q), :] = (el * er + ol * orr).astype(LOW)
        prod_v[1, rows_of(q), :] = (el * orr + ol * er).astype(LOW)
    loads[6].wait()
    for p in range(2):
        modal_v[p] = jnp.dot(prod_v[p], anal_v[p], preferred_element_type=F32).astype(LOW)

    for c in range(3):
        for p in range(2):
            values = gathered(0, 2 * c + p)
            stack = jnp.concatenate(
                [
                    modal_v[p, rows_of(pair_index[0][c]), :],
                    modal_v[p, rows_of(pair_index[1][c]), :],
                    values,
                ],
                axis=0,
            )
            flux_z = modal_v[1 - p, rows_of(pair_index[2][c]), :].astype(F32)
            turn = (-time_step if p == 1 else time_step) * wave
            local = (1.0 - time_step * viscosity * wave * wave) * values.astype(F32)
            set_field(
                num_v,
                2 * c + p,
                jnp.dot(fwd_mat, stack, preferred_element_type=F32)
                + wide(quad_v[...]) * (local + turn * flux_z),
            )

    edge_rows = 6 * GLL * groups

    def assemble(which, buf):
        def edge_copy(way):
            if way == 0:
                target = {"modes": jnp.minimum(member + 1, ROWS - 1)}
            elif way == 1:
                target = {"modes": jnp.maximum(member - 1, 0)}
            else:
                target = {"elems": (high_slab, low_slab)[way - 2]}
            return pltpu.make_async_remote_copy(
                src_ref=edge_send.at[which, way],
                dst_ref=edge_recv.at[which, way],
                send_sem=esend_sem.at[which, way],
                recv_sem=erecv_sem.at[which, way],
                device_id=target,
                device_id_type=MESH,
            )

        top = pl.ds(GLL - 1, edge_rows, stride=GLL)
        low = pl.ds(0, edge_rows, stride=GLL)

        @pl.when(member < ROWS - 1)
        def _():
            edge_send[which, 0] = buf[top, :].astype(LOW)
            edge_copy(0).start()

        @pl.when(member > 0)
        def _():
            edge_send[which, 1] = buf[low, :].astype(LOW)
            edge_copy(1).start()

        @pl.when(member > 0)
        def _():
            edge_copy(0).wait_recv()
            buf[low, :] = buf[low, :] + edge_recv[which, 0].astype(F32)

        @pl.when(member < ROWS - 1)
        def _():
            edge_copy(1).wait_recv()
            buf[top, :] = buf[top, :] + edge_recv[which, 1].astype(F32)

        for way, start in ((2, NODES - GLL), (3, 0)):
            edge_send[which, way] = jnp.concatenate(
                [buf[pl.ds(i * NODES + start, GLL), :] for i in range(6 * groups)], axis=0
            ).astype(LOW)
            edge_copy(way).start()
        for way, start in ((2, 0), (3, NODES - GLL)):
            edge_copy(way).wait_recv()
            came = edge_recv[which, way].astype(F32)
            for i in range(6 * groups):
                rows = pl.ds(i * NODES + start, GLL)
                buf[rows, :] = buf[rows, :] + came[i * GLL : (i + 1) * GLL]
        for way in (2, 3):
            edge_copy(way).wait_send()

        @pl.when(member < ROWS - 1)
        def _():
            edge_copy(0).wait_send()

        @pl.when(member > 0)
        def _():
            edge_copy(1).wait_send()

    assemble(0, num_v)
    for q in range(groups):
        for i in range(6):
            value = scale_v[...] * num_v[rows_of(6 * q + i), :]
            num_v[rows_of(6 * q + i), :] = value
            send_v[2, q, rows_of(i), :] = value.astype(LOW)
    for partner in partners:
        swap(1, partner).wait_send()
        swap(2, partner).start()
    next_r[member] = send_v[2, member]

    for partner in partners:
        swapped(1, partner).wait_recv()
    for q in range(groups):
        for i in range(6):
            psi_v[rows_of(6 * q + i), :] = scale_v[...] * forcing_r[q, rows_of(i), :].astype(F32)
    assemble(1, psi_v)
    for i in range(6 * groups):
        psi_v[rows_of(i), :] = psi_v[rows_of(i), :] + mult_v[...] * (
            scale_v[...] * num_v[rows_of(i), :]
        )

    norm = jnp.where(mode_ids == 0, 1.0 / (3.0 * modes), 0.5 / (3.0 * modes)).astype(F32)
    for p in range(2):
        lateral = []
        for c in range(3):
            psi = field(psi_v, 2 * c + p)
            other = field(psi_v, 2 * c + 1 - p)
            grads = jnp.dot(bwd_mat, psi.astype(LOW), preferred_element_type=F32)
            set_field(
                num_v,
                2 * c + p,
                wide(quad_v[...]) * ((1.0 - time_step * viscosity * wave * wave) * psi)
                + time_step * grads[2 * NODES :],
            )
            turn = -wave if p == 0 else wave
            lateral.append((grads[:NODES], grads[NODES : 2 * NODES], wide(quad_v[...]) * (turn * other)))
        for q, (left, right) in enumerate(pair_order):
            cot = lateral[right][left] + lateral[left][right]
            cot_v[p, rows_of(q), :] = (norm * cot).astype(LOW)

    for p in range(2):
        spread_v[p] = jnp.dot(cot_v[p], synth_v[p], preferred_element_type=F32)
    for c in range(3):
        even = jnp.zeros((NODES, even_v.shape[1]), F32)
        odd = jnp.zeros((NODES, even_v.shape[1]), F32)
        for d in range(3):
            se = spread_v[0, rows_of(pair_index[c][d]), :]
            so = spread_v[1, rows_of(pair_index[c][d]), :]
            ed, od = even_v[rows_of(d), :], odd_v[rows_of(d), :]
            even = even + (se * ed + so * od)
            odd = odd + (se * od + so * ed)
        pcot_v[0, rows_of(c), :] = even.astype(LOW)
        pcot_v[1, rows_of(c), :] = odd.astype(LOW)
    gain = jnp.where(mode_ids == 0, 3.0 * modes * time_step, 6.0 * modes * time_step).astype(F32)
    for p in range(2):
        back = jnp.dot(pcot_v[p], anal_v[p], preferred_element_type=F32)
        for c in range(3):
            low = (
                field(num_v, 2 * c + p) + gain * back[c * NODES : (c + 1) * NODES]
            ).astype(LOW)
            for q in range(groups):
                send_v[3, q, rows_of(2 * c + p), :] = low[:, q * 128 : (q + 1) * 128]
    for partner in partners:
        swap(2, partner).wait_send()
        swap(3, partner).start()
    start_r[member] = send_v[3, member]

    stores = []
    for which, target in ((0, next_ref), (1, start_ref)):
        for partner in partners:
            swapped(2 + which, partner).wait_recv()
        for j in range(ROWS):
            out_v[which, j] = recv[2 + which][slots[j]].astype(F32).reshape(3, 2, NODES, 128)
        store = pltpu.make_async_copy(out_v.at[which], target, out_sem.at[which])
        store.start()
        stores.append(store)
    for store in stores:
        store.wait()
    for partner in partners:
        swap(3, partner).wait_send()


def on_device(state, adjoint_end, observed, spacing, radial_slot):
    groups = lax.axis_size("modes")
    slabs = lax.axis_size("elems")
    modes = groups * state.shape[4]
    half = 3 * modes // 2
    synth, analysis = half_tables(modes, 3 * modes)
    fwd, bwd, w2 = node_tables()
    any_spec = pl.BlockSpec(memory_space=pl.ANY)
    smem_spec = pl.BlockSpec(memory_space=pltpu.SMEM)
    local = state.shape
    block = (6 * NODES, 128)
    vm = pltpu.VMEM
    sem = pltpu.SemaphoreType.DMA

    def run(*args):
        step_kernel(groups, slabs, *args)

    return pl.pallas_call(
        run,
        out_shape=(jax.ShapeDtypeStruct(local, F32), jax.ShapeDtypeStruct(local, F32)),
        in_specs=[any_spec] * 3 + [smem_spec] * 2 + [any_spec] * 5,
        out_specs=(any_spec, any_spec),
        scratch_shapes=[
            vm(local, F32), vm(local, F32), vm(local, LOW),
            vm((2, modes, half), LOW), vm((2, half, modes), LOW),
            vm((2, NODES, 3 * NODES), F32), vm((2, 3 * NODES, NODES), F32), vm((NODES, 128), F32),
            vm((4, ROWS) + block, LOW), *[vm((ROWS,) + block, LOW)] * 4,
            vm((NODES, 128), F32), vm((NODES, 128), F32), vm((NODES, 128), F32),
            vm((3 * NODES, half), F32), vm((3 * NODES, half), F32),
            vm((2, 6 * NODES, half), LOW), vm((2, 6 * NODES, modes), LOW),
            vm((6 * NODES * groups, 128), F32), vm((6 * NODES * groups, 128), F32),
            vm((2, 6 * NODES, modes), LOW), vm((2, 6 * NODES, half), F32),
            vm((2, 3 * NODES, half), LOW),
            vm((2, 4, 6 * GLL * groups, 128), LOW), vm((2, 4, 6 * GLL * groups, 128), LOW),
            vm((2, GLL, 128), F32), vm((2, GLL, 128), F32),
            vm((2,) + local, F32),
            sem((8,)), sem((4, ROWS)), sem((4, ROWS)), sem((2, 4)), sem((2, 4)),
            sem((2,)), sem((2,)), sem((2,)),
        ],
        compiler_params=pltpu.CompilerParams(
            collective_id=0, has_side_effects=True, vmem_limit_bytes=48 * 1024 * 1024
        ),
        cost_estimate=pl.CostEstimate(
            flops=1900000000, bytes_accessed=7000000, transcendentals=0
        ),
    )(
        state, adjoint_end, observed, spacing, radial_slot,
        jnp.asarray(synth, F32).astype(LOW), jnp.asarray(analysis, F32).astype(LOW),
        jnp.asarray(fwd, F32), jnp.asarray(bwd, F32),
        jnp.asarray(np.broadcast_to(w2[:, None], (NODES, 128)), F32),
    )


def solution(mesh):
    in_specs = (
        P("elems", None, None, None, "modes"),
        P("elems", None, None, None, "modes"),
        P("elems", None, None, None, "modes"),
        P("elems", None),
        P("elems", None),
    )
    out_specs = (P("elems", None, None, None, "modes"), P("elems", None, None, None, "modes"))
    return jax.shard_map(
        on_device, mesh=mesh, in_specs=in_specs, out_specs=out_specs, check_vma=False
    )
```

```python
import jax
import jax.numpy as jnp
import numpy as np
from jax import lax
from jax.experimental import pallas as pl
from jax.experimental.pallas import tpu as pltpu
from jax.sharding import PartitionSpec as P

GLL = 8
NODES = GLL * GLL
ROWS = 4
time_step = 0.01
viscosity = 0.05
wave_scale = 4.0
pair_order = ((0, 0), (0, 1), (0, 2), (1, 1), (1, 2), (2, 2))
pair_index = ((0, 1, 2), (1, 3, 4), (2, 4, 5))
F32 = jnp.float32
LOW = jnp.bfloat16
MESH = pl.DeviceIdType.MESH


def legendre_table(points, quad_count):
    columns = [points * 0.0 + 1.0, points]
    for degree in range(2, quad_count):
        columns.append(
            ((2 * degree - 1) * points * columns[-1] - (degree - 1) * columns[-2]) / degree
        )
    return np.stack(columns, axis=1)


def gll_tables(quad_count):
    degree = quad_count - 1
    points = -np.cos(np.pi * np.arange(quad_count) / degree)
    for repeat in range(60):
        vander = legendre_table(points, quad_count)
        points = points - (points * vander[:, degree] - vander[:, degree - 1]) / (
            quad_count * vander[:, degree]
        )
    vander = legendre_table(points, quad_count)
    edge_value = vander[:, degree]
    weights = 2.0 / (degree * quad_count * edge_value * edge_value)
    diagonal_mask = np.arange(quad_count)[:, None] == np.arange(quad_count)[None, :]
    differ = np.where(diagonal_mask, 1.0, points[:, None] - points[None, :])
    derivative = np.where(diagonal_mask, 0.0, edge_value[:, None] / (edge_value[None, :] * differ))
    derivative[0, 0] = -degree * quad_count / 4.0
    derivative[degree, degree] = degree * quad_count / 4.0
    return (weights, derivative)


def half_tables(modes, planes):
    half = planes // 2
    turns = np.outer(np.arange(modes), 2 * np.arange(half) + 1) % (2 * planes)
    angles = np.pi * turns / planes
    factor = np.where(np.arange(modes) == 0, 1.0, 2.0)[:, None]
    synth = np.stack((factor * np.cos(angles), -factor * np.sin(angles)))
    analysis = np.stack((np.cos(angles), -np.sin(angles))) * (2.0 / planes)
    return synth, np.transpose(analysis, (0, 2, 1))


def node_tables():
    weights, deriv = gll_tables(GLL)
    wdiag = np.diag(weights)
    back = deriv.T @ wdiag
    ahead = wdiag @ deriv
    stiff = deriv.T @ wdiag @ deriv
    zero = np.zeros((NODES, NODES))
    fwd = (
        np.concatenate((np.kron(back, wdiag), np.kron(wdiag, back), np.kron(stiff, wdiag)), 1),
        np.concatenate((zero, zero, np.kron(wdiag, stiff)), 1),
    )
    adj = (
        np.concatenate((np.kron(ahead, wdiag), np.kron(wdiag, ahead), np.kron(stiff, wdiag)), 0),
        np.concatenate((zero, zero, np.kron(wdiag, stiff)), 0),
    )
    return np.stack(fwd), np.stack(adj), np.kron(weights, weights)


def step_kernel(
    groups,
    slabs,
    state_ref, adj_ref, obs_ref, spacing_h, slot_h, synth_ref, anal_ref, fwd_ref, bwd_ref, w2_ref,
    next_o, start_o,
    spacing_ref, slot_ref, state_v, adj_v, obs_v, synth_v, anal_v, fwd_v, bwd_v, w2_v,
    send_v, state_r, forcing_r, next_r, start_r, quad_v, scale_v, mult_v,
    even_v, odd_v, prod_v, modal_v, num_v, psi_v, cot_v, spread_v, pcot_v,
    edge_send, edge_recv, mass_send, mass_recv,
    load_sem, send_sem, recv_sem, esend_sem, erecv_sem, msend_sem, mrecv_sem,
):
    member = lax.axis_index("modes")
    slab = lax.axis_index("elems")
    low_slab = lax.rem(slab + slabs - 1, slabs)
    high_slab = lax.rem(slab + 1, slabs)
    partners = (lax.rem(member + 2, 4), 3 - member, member + 1 - 2 * lax.rem(member, 2))
    modes = groups * 128
    recv = (state_r, forcing_r, next_r, start_r)

    loads = [
        pltpu.make_async_copy(src, dst, load_sem.at[i])
        for i, (src, dst) in enumerate(
            [(slot_h, slot_ref), (spacing_h, spacing_ref)]
            + [(state_ref.at[j], state_v.at[j]) for j in range(ROWS)]
            + [
                (adj_ref, adj_v), (obs_ref, obs_v), (w2_ref, w2_v),
                (fwd_ref, fwd_v), (synth_ref, synth_v), (anal_ref, anal_v), (bwd_ref, bwd_v),
            ]
        )
    ]
    adj_load, obs_load, w2_load, fwd_load, synth_load, anal_load, bwd_load = loads[2 + ROWS :]
    for load in loads:
        load.start()

    barrier = pltpu.get_barrier_semaphore()
    for partner in partners:
        pl.semaphore_signal(barrier, inc=1, device_id={"modes": partner}, device_id_type=MESH)
    for near in (low_slab, high_slab):
        pl.semaphore_signal(barrier, inc=1, device_id={"elems": near}, device_id_type=MESH)

    loads[0].wait()
    loads[1].wait()
    slots = [slot_ref[0, j] for j in range(ROWS)]

    def rows_of(index, count=NODES):
        return pl.ds(index * count, count)

    def flat(block):
        return block.reshape(6 * NODES, 128)

    def elem_of(row):
        place = jnp.int32(0)
        for j in range(1, ROWS):
            place = jnp.where(slots[j] == row, j, place)
        return place

    whole = (0, 6 * NODES)
    phases = ((0,) + whole, (1, 0, 4 * NODES), (1, 4 * NODES, 6 * NODES), (2,) + whole, (3,) + whole)

    def swap(phase, partner, arrival=False):
        which, begin, end = phases[phase]
        rows = pl.ds(begin, end - begin)
        slot = partner if arrival else member
        return pltpu.make_async_remote_copy(
            src_ref=send_v.at[which, partner, rows],
            dst_ref=recv[which].at[slot, rows],
            send_sem=send_sem.at[phase, partner],
            recv_sem=recv_sem.at[phase, slot],
            device_id={"modes": partner},
            device_id_type=MESH,
        )

    def start(phase):
        for partner in partners:
            swap(phase, partner).start()

    def sent(phase):
        for partner in partners:
            swap(phase, partner).wait_send()

    def arrived(phase):
        for partner in partners:
            swap(phase, partner, arrival=True).wait_recv()

    for load in loads[2 : 2 + ROWS]:
        load.wait()
    for row in range(ROWS):
        send_v[0, row] = flat(state_v[elem_of(row)]).astype(LOW)
    pl.semaphore_wait(barrier, 5)
    start(0)
    state_r[member] = send_v[0, member]

    w2_load.wait()
    own = elem_of(member)
    above = elem_of(jnp.minimum(member + 1, ROWS - 1))
    below = elem_of(jnp.maximum(member - 1, 0))

    def area(elem):
        return spacing_ref[0, elem] * spacing_ref[1, elem] * 0.25

    side_x = spacing_ref[0, own]
    side_y = spacing_ref[1, own]
    full = (NODES, 128)
    layer = lax.rem(lax.broadcasted_iota(jnp.int32, full, 0), GLL)
    has_above = jnp.logical_and(layer == GLL - 1, member < ROWS - 1)
    has_below = jnp.logical_and(layer == 0, member > 0)
    w2 = w2_v[...]
    quad = w2 * area(own)
    quad_v[...] = quad
    mass = quad + jnp.where(has_above, w2 * area(above), 0.0)
    mass = mass + jnp.where(has_below, w2 * area(below), 0.0)
    scale_v[...] = mass
    mass_send[0] = mass[NODES - GLL :]
    mass_send[1] = mass[:GLL]

    def mass_copy(way):
        return pltpu.make_async_remote_copy(
            src_ref=mass_send.at[way],
            dst_ref=mass_recv.at[way],
            send_sem=msend_sem.at[way],
            recv_sem=mrecv_sem.at[way],
            device_id={"elems": (high_slab, low_slab)[way]},
            device_id_type=MESH,
        )

    mass_copy(0).start()
    mass_copy(1).start()
    copies = jnp.where(jnp.logical_or(has_above, has_below), 2.0, 1.0).astype(F32)
    node_a = lax.broadcasted_iota(jnp.int32, full, 0) // GLL
    mult_v[...] = jnp.where(jnp.logical_or(node_a == 0, node_a == GLL - 1), 2.0 * copies, copies)

    edge_rows = 6 * GLL * groups
    top = pl.ds(GLL - 1, edge_rows, stride=GLL)
    low = pl.ds(0, edge_rows, stride=GLL)

    def edge_copy(which, way):
        if way == 0:
            target = {"modes": jnp.minimum(member + 1, ROWS - 1)}
        elif way == 1:
            target = {"modes": jnp.maximum(member - 1, 0)}
        else:
            target = {"elems": (high_slab, low_slab)[way - 2]}
        return pltpu.make_async_remote_copy(
            src_ref=edge_send.at[which, way],
            dst_ref=edge_recv.at[which, way],
            send_sem=esend_sem.at[which, way],
            recv_sem=erecv_sem.at[which, way],
            device_id=target,
            device_id_type=MESH,
        )

    def send_around(which, buf):
        for way, begin in ((2, NODES - GLL), (3, 0)):
            edge_send[which, way] = jnp.concatenate(
                [buf[pl.ds(i * NODES + begin, GLL), :] for i in range(6 * groups)], axis=0
            ).astype(LOW)
            edge_copy(which, way).start()

    def add_around(which, buf):
        for way, begin in ((2, 0), (3, NODES - GLL)):
            edge_copy(which, way).wait_recv()
            came = edge_recv[which, way].astype(F32)
            for i in range(6 * groups):
                rows = pl.ds(i * NODES + begin, GLL)
                buf[rows, :] = buf[rows, :] + came[i * GLL : (i + 1) * GLL]

    def around_sent(which):
        for way in (2, 3):
            edge_copy(which, way).wait_send()

    adj_load.wait()
    obs_load.wait()
    for row in range(ROWS):
        elem = elem_of(row)
        psi_v[rows_of(row, 6 * NODES), :] = flat(adj_v[elem] - obs_v[elem].astype(F32))
    for row in range(ROWS - 1):
        lower = pl.ds(row * 6 * NODES + GLL - 1, 6 * GLL, stride=GLL)
        upper = pl.ds((row + 1) * 6 * NODES, 6 * GLL, stride=GLL)
        both = psi_v[lower, :] + psi_v[upper, :]
        psi_v[lower, :] = both
        psi_v[upper, :] = both
    send_around(0, psi_v)

    mass_copy(0).wait()
    mass_copy(1).wait()
    scale_v[:GLL, :] = scale_v[:GLL, :] + mass_recv[0]
    scale_v[NODES - GLL :, :] = scale_v[NODES - GLL :, :] + mass_recv[1]
    at_wall = jnp.logical_and(layer == 0, member == 0)
    scale_v[...] = jnp.where(at_wall, 0.0, 1.0) / scale_v[...]

    add_around(0, psi_v)
    for row in range(ROWS):
        send_v[1, row] = psi_v[rows_of(row, 6 * NODES), :].astype(LOW)
    forcing_r[member] = send_v[1, member]
    sent(0)
    start(1)

    fwd_load.wait()
    bwd_load.wait()
    lane = lax.broadcasted_iota(jnp.int32, (NODES, 3 * NODES), 1)
    ratio = jnp.full((NODES, 3 * NODES), side_y) / jnp.full((NODES, 3 * NODES), side_x)
    coef = jnp.where(
        lane < NODES, 0.5 * side_y, jnp.where(lane < 2 * NODES, 0.5 * side_x, -viscosity * ratio)
    )
    fwd_mat = (time_step * (fwd_v[0] * coef - fwd_v[1] * (viscosity / ratio))).astype(LOW)
    line = lax.broadcasted_iota(jnp.int32, (3 * NODES, NODES), 0)
    ratio = jnp.full((3 * NODES, NODES), side_y) / jnp.full((3 * NODES, NODES), side_x)
    coef = jnp.where(
        line < NODES, 0.5 * side_y, jnp.where(line < 2 * NODES, 0.5 * side_x, -viscosity * ratio)
    )
    bwd_mat = (bwd_v[0] * coef - bwd_v[1] * (viscosity / ratio)).astype(LOW)

    arrived(0)

    def gathered(phase, i):
        return jnp.concatenate([recv[phase][q, rows_of(i), :] for q in range(groups)], axis=1)

    def wide(block):
        return jnp.concatenate([block] * groups, axis=1)

    def field(buf, i):
        return jnp.concatenate([buf[rows_of(6 * q + i), :] for q in range(groups)], axis=1)

    def set_field(buf, i, value):
        for q in range(groups):
            buf[rows_of(6 * q + i), :] = value[:, q * 128 : (q + 1) * 128]

    mode_ids = lax.broadcasted_iota(jnp.int32, (NODES, modes), 1)
    wave = mode_ids.astype(F32) * (wave_scale / modes)

    synth_load.wait()
    even_v[...] = jnp.dot(
        jnp.concatenate([gathered(0, 2 * c) for c in range(3)], axis=0),
        synth_v[0],
        preferred_element_type=F32,
    )
    odd_v[...] = jnp.dot(
        jnp.concatenate([gathered(0, 2 * c + 1) for c in range(3)], axis=0),
        synth_v[1],
        preferred_element_type=F32,
    )

    for q, (left, right) in enumerate(pair_order):
        el, ol = even_v[rows_of(left), :], odd_v[rows_of(left), :]
        er, orr = even_v[rows_of(right), :], odd_v[rows_of(right), :]
        prod_v[0, rows_of(q), :] = (el * er + ol * orr).astype(LOW)
        prod_v[1, rows_of(q), :] = (el * orr + ol * er).astype(LOW)
    anal_load.wait()
    for p in range(2):
        modal_v[p] = jnp.dot(prod_v[p], anal_v[p], preferred_element_type=F32).astype(LOW)

    for c in range(3):
        for p in range(2):
            values = gathered(0, 2 * c + p)
            stack = jnp.concatenate(
                [
                    modal_v[p, rows_of(pair_index[0][c]), :],
                    modal_v[p, rows_of(pair_index[1][c]), :],
                    values,
                ],
                axis=0,
            )
            flux_z = modal_v[1 - p, rows_of(pair_index[2][c]), :].astype(F32)
            turn = (-time_step if p == 1 else time_step) * wave
            local = (1.0 - time_step * viscosity * wave * wave) * values.astype(F32)
            set_field(
                num_v,
                2 * c + p,
                jnp.dot(fwd_mat, stack, preferred_element_type=F32)
                + wide(quad_v[...]) * (local + turn * flux_z),
            )

    send_around(1, num_v)
    add_around(1, num_v)

    @pl.when(member < ROWS - 1)
    def _():
        edge_send[1, 0] = num_v[top, :].astype(LOW)
        edge_copy(1, 0).start()

    @pl.when(member > 0)
    def _():
        edge_send[1, 1] = num_v[low, :].astype(LOW)
        edge_copy(1, 1).start()

    sent(1)
    start(2)

    @pl.when(member > 0)
    def _():
        edge_copy(1, 0).wait_recv()
        num_v[low, :] = num_v[low, :] + edge_recv[1, 0].astype(F32)

    @pl.when(member < ROWS - 1)
    def _():
        edge_copy(1, 1).wait_recv()
        num_v[top, :] = num_v[top, :] + edge_recv[1, 1].astype(F32)

    for q in range(groups):
        for i in range(6):
            value = scale_v[...] * num_v[rows_of(6 * q + i), :]
            num_v[rows_of(6 * q + i), :] = value
            send_v[2, q, rows_of(i), :] = value.astype(LOW)
    next_r[member] = send_v[2, member]
    sent(2)
    start(3)

    arrived(1)
    arrived(2)
    for q in range(groups):
        for i in range(6):
            rows = rows_of(6 * q + i)
            forcing = forcing_r[q, rows_of(i), :].astype(F32)
            psi_v[rows, :] = scale_v[...] * (forcing + mult_v[...] * num_v[rows, :])

    norm = jnp.where(mode_ids == 0, 1.0 / (3.0 * modes), 0.5 / (3.0 * modes)).astype(F32)
    for p in range(2):
        lateral = []
        for c in range(3):
            psi = field(psi_v, 2 * c + p)
            other = field(psi_v, 2 * c + 1 - p)
            grads = jnp.dot(bwd_mat, psi.astype(LOW), preferred_element_type=F32)
            set_field(
                num_v,
                2 * c + p,
                wide(quad_v[...]) * ((1.0 - time_step * viscosity * wave * wave) * psi)
                + time_step * grads[2 * NODES :],
            )
            turn = -wave if p == 0 else wave
            lateral.append((grads[:NODES], grads[NODES : 2 * NODES], wide(quad_v[...]) * (turn * other)))
        for q, (left, right) in enumerate(pair_order):
            cot = lateral[right][left] + lateral[left][right]
            cot_v[p, rows_of(q), :] = (norm * cot).astype(LOW)

    for p in range(2):
        spread_v[p] = jnp.dot(cot_v[p], synth_v[p], preferred_element_type=F32)
    for c in range(3):
        even = jnp.zeros((NODES, even_v.shape[1]), F32)
        odd = jnp.zeros((NODES, even_v.shape[1]), F32)
        for d in range(3):
            se = spread_v[0, rows_of(pair_index[c][d]), :]
            so = spread_v[1, rows_of(pair_index[c][d]), :]
            ed, od = even_v[rows_of(d), :], odd_v[rows_of(d), :]
            even = even + (se * ed + so * od)
            odd = odd + (se * od + so * ed)
        pcot_v[0, rows_of(c), :] = even.astype(LOW)
        pcot_v[1, rows_of(c), :] = odd.astype(LOW)
    gain = jnp.where(mode_ids == 0, 3.0 * modes * time_step, 6.0 * modes * time_step).astype(F32)
    for p in range(2):
        back = jnp.dot(pcot_v[p], anal_v[p], preferred_element_type=F32)
        for c in range(3):
            low = (
                field(num_v, 2 * c + p) + gain * back[c * NODES : (c + 1) * NODES]
            ).astype(LOW)
            for q in range(groups):
                send_v[3, q, rows_of(2 * c + p), :] = low[:, q * 128 : (q + 1) * 128]
    start_r[member] = send_v[3, member]
    sent(3)
    start(4)

    around_sent(0)
    around_sent(1)

    @pl.when(member < ROWS - 1)
    def _():
        edge_copy(1, 0).wait_send()

    @pl.when(member > 0)
    def _():
        edge_copy(1, 1).wait_send()

    for phase, rows, target in ((3, next_r, next_o), (4, start_r, start_o)):
        arrived(phase)
        for j in range(ROWS):
            target[j] = rows[slots[j]].astype(F32).reshape(3, 2, NODES, 128)
    sent(4)


def store_kernel(next_v, start_v, next_ref, start_ref, sem):
    stores = [
        pltpu.make_async_copy(source.at[j], target.at[j], sem.at[which, j])
        for which, (source, target) in enumerate(((next_v, next_ref), (start_v, start_ref)))
        for j in range(ROWS)
    ]
    for store in stores:
        store.start()
    for store in stores:
        store.wait()


def on_device(state, adjoint_end, observed, spacing, radial_slot):
    groups = lax.axis_size("modes")
    slabs = lax.axis_size("elems")
    modes = groups * state.shape[4]
    half = 3 * modes // 2
    synth, analysis = half_tables(modes, 3 * modes)
    fwd, bwd, w2 = node_tables()
    any_spec = pl.BlockSpec(memory_space=pltpu.HBM)
    vmem_spec = pl.BlockSpec(memory_space=pltpu.VMEM)
    local = state.shape
    block = (6 * NODES, 128)
    vm = pltpu.VMEM
    sem = pltpu.SemaphoreType.DMA

    def run(*args):
        step_kernel(groups, slabs, *args)

    held_out = pltpu.VMEM(local, F32)

    def held(array):
        return pltpu.with_memory_space_constraint(array, pltpu.HBM)

    next_v, start_v = pl.pallas_call(
        run,
        out_shape=(held_out, held_out),
        in_specs=[any_spec] * 10,
        out_specs=(vmem_spec, vmem_spec),
        scratch_shapes=[
            pltpu.SMEM((2, ROWS), F32), pltpu.SMEM((1, ROWS), jnp.int32),
            vm(local, F32), vm(local, F32), vm(local, LOW),
            vm((2, modes, half), LOW), vm((2, half, modes), LOW),
            vm((2, NODES, 3 * NODES), F32), vm((2, 3 * NODES, NODES), F32), vm((NODES, 128), F32),
            vm((4, ROWS) + block, LOW), *[vm((ROWS,) + block, LOW)] * 4,
            vm((NODES, 128), F32), vm((NODES, 128), F32), vm((NODES, 128), F32),
            vm((3 * NODES, half), F32), vm((3 * NODES, half), F32),
            vm((2, 6 * NODES, half), LOW), vm((2, 6 * NODES, modes), LOW),
            vm((6 * NODES * groups, 128), F32), vm((6 * NODES * groups, 128), F32),
            vm((2, 6 * NODES, modes), LOW), vm((2, 6 * NODES, half), F32),
            vm((2, 3 * NODES, half), LOW),
            vm((2, 4, 6 * GLL * groups, 128), LOW), vm((2, 4, 6 * GLL * groups, 128), LOW),
            vm((2, GLL, 128), F32), vm((2, GLL, 128), F32),
            sem((9 + ROWS,)), sem((5, ROWS)), sem((5, ROWS)), sem((2, 4)), sem((2, 4)),
            sem((2,)), sem((2,)),
        ],
        compiler_params=pltpu.CompilerParams(
            collective_id=0, has_side_effects=True, vmem_limit_bytes=48 * 1024 * 1024
        ),
        cost_estimate=pl.CostEstimate(
            flops=1900000000, bytes_accessed=7000000, transcendentals=0
        ),
    )(
        held(state), held(adjoint_end), held(observed), held(spacing.T), held(radial_slot),
        held(jnp.asarray(synth, F32).astype(LOW)), held(jnp.asarray(analysis, F32).astype(LOW)),
        held(jnp.asarray(fwd, F32)), held(jnp.asarray(bwd, F32)),
        held(jnp.asarray(np.broadcast_to(w2[:, None], (NODES, 128)), F32)),
    )
    return pl.pallas_call(
        store_kernel,
        out_shape=(jax.ShapeDtypeStruct(local, F32), jax.ShapeDtypeStruct(local, F32)),
        in_specs=[pl.BlockSpec(memory_space=pl.ANY)] * 2,
        out_specs=(any_spec, any_spec),
        scratch_shapes=[sem((2, ROWS))],
        compiler_params=pltpu.CompilerParams(vmem_limit_bytes=1024 * 1024),
    )(next_v, start_v)


def solution(mesh):
    in_specs = (
        P("elems", None, None, None, "modes"),
        P("elems", None, None, None, "modes"),
        P("elems", None, None, None, "modes"),
        P("elems", None),
        P("elems", None),
    )
    out_specs = (P("elems", None, None, None, "modes"), P("elems", None, None, None, "modes"))
    return jax.shard_map(
        on_device, mesh=mesh, in_specs=in_specs, out_specs=out_specs, check_vma=False
    )
```

```python
import jax
import jax.numpy as jnp
import numpy as np
from jax import lax
from jax.experimental import pallas as pl
from jax.experimental.pallas import tpu as pltpu
from jax.sharding import PartitionSpec as P

GLL = 8
NODES = GLL * GLL
ROWS = 4
time_step = 0.01
viscosity = 0.05
wave_scale = 4.0
pair_order = ((0, 0), (0, 1), (0, 2), (1, 1), (1, 2), (2, 2))
pair_index = ((0, 1, 2), (1, 3, 4), (2, 4, 5))
F32 = jnp.float32
LOW = jnp.bfloat16
MESH = pl.DeviceIdType.MESH


def legendre_table(points, quad_count):
    columns = [points * 0.0 + 1.0, points]
    for degree in range(2, quad_count):
        columns.append(
            ((2 * degree - 1) * points * columns[-1] - (degree - 1) * columns[-2]) / degree
        )
    return np.stack(columns, axis=1)


def gll_tables(quad_count):
    degree = quad_count - 1
    points = -np.cos(np.pi * np.arange(quad_count) / degree)
    for repeat in range(60):
        vander = legendre_table(points, quad_count)
        points = points - (points * vander[:, degree] - vander[:, degree - 1]) / (
            quad_count * vander[:, degree]
        )
    vander = legendre_table(points, quad_count)
    edge_value = vander[:, degree]
    weights = 2.0 / (degree * quad_count * edge_value * edge_value)
    diagonal_mask = np.arange(quad_count)[:, None] == np.arange(quad_count)[None, :]
    differ = np.where(diagonal_mask, 1.0, points[:, None] - points[None, :])
    derivative = np.where(diagonal_mask, 0.0, edge_value[:, None] / (edge_value[None, :] * differ))
    derivative[0, 0] = -degree * quad_count / 4.0
    derivative[degree, degree] = degree * quad_count / 4.0
    return (weights, derivative)


def half_tables(modes, planes):
    half = planes // 2
    turns = np.outer(np.arange(modes), 2 * np.arange(half) + 1) % (2 * planes)
    angles = np.pi * turns / planes
    factor = np.where(np.arange(modes) == 0, 1.0, 2.0)[:, None]
    synth = np.stack((factor * np.cos(angles), -factor * np.sin(angles)))
    analysis = np.stack((np.cos(angles), -np.sin(angles))) * (2.0 / planes)
    return synth, np.transpose(analysis, (0, 2, 1))


def node_tables():
    weights, deriv = gll_tables(GLL)
    wdiag = np.diag(weights)
    back = deriv.T @ wdiag
    ahead = wdiag @ deriv
    stiff = deriv.T @ wdiag @ deriv
    zero = np.zeros((NODES, NODES))
    fwd = (
        np.concatenate((np.kron(back, wdiag), np.kron(wdiag, back), np.kron(stiff, wdiag)), 1),
        np.concatenate((zero, zero, np.kron(wdiag, stiff)), 1),
    )
    adj = (
        np.concatenate((np.kron(ahead, wdiag), np.kron(wdiag, ahead), np.kron(stiff, wdiag)), 0),
        np.concatenate((zero, zero, np.kron(wdiag, stiff)), 0),
    )
    return np.stack(fwd), np.stack(adj), np.kron(weights, weights)


def step_kernel(
    groups,
    slabs,
    state_ref, adj_ref, obs_ref, spacing_h, slot_h, synth_ref, anal_ref, fwd_ref, bwd_ref, w2_ref,
    next_o, start_o,
    spacing_ref, slot_ref, state_v, adj_v, obs_v, synth_v, anal_v, fwd_v, bwd_v, w2_v,
    send_v, state_r, forcing_r, next_r, start_r, quad_v, scale_v, mult_v,
    even_v, odd_v, prod_v, modal_v, num_v, psi_v, cot_v, spread_v, pcot_v,
    edge_send, edge_recv, mass_send, mass_recv,
    load_sem, send_sem, recv_sem, esend_sem, erecv_sem, msend_sem, mrecv_sem,
):
    member = lax.axis_index("modes")
    slab = lax.axis_index("elems")
    low_slab = lax.rem(slab + slabs - 1, slabs)
    high_slab = lax.rem(slab + 1, slabs)
    partners = (lax.rem(member + 2, 4), 3 - member, member + 1 - 2 * lax.rem(member, 2))
    modes = groups * 128
    recv = (state_r, forcing_r, next_r, start_r)

    loads = [
        pltpu.make_async_copy(src, dst, load_sem.at[i])
        for i, (src, dst) in enumerate(
            [(slot_h, slot_ref), (spacing_h, spacing_ref)]
            + [(state_ref.at[j], state_v.at[j]) for j in range(ROWS)]
            + [
                (adj_ref, adj_v), (obs_ref, obs_v), (w2_ref, w2_v),
                (fwd_ref, fwd_v), (synth_ref, synth_v), (anal_ref, anal_v), (bwd_ref, bwd_v),
            ]
        )
    ]
    adj_load, obs_load, w2_load, fwd_load, synth_load, anal_load, bwd_load = loads[2 + ROWS :]
    for load in loads:
        load.start()

    barrier = pltpu.get_barrier_semaphore()
    for partner in partners:
        pl.semaphore_signal(barrier, inc=1, device_id={"modes": partner}, device_id_type=MESH)

    def greet(near):
        pl.semaphore_signal(barrier, inc=1, device_id={"elems": near}, device_id_type=MESH)

    first = slab == 0
    last = slab == slabs - 1

    @pl.when(jnp.logical_not(first))
    def _():
        greet(low_slab)

    @pl.when(jnp.logical_not(last))
    def _():
        greet(high_slab)

    loads[0].wait()
    loads[1].wait()
    slots = [slot_ref[0, j] for j in range(ROWS)]

    def rows_of(index, count=NODES):
        return pl.ds(index * count, count)

    def flat(block):
        return block.reshape(6 * NODES, 128)

    def elem_of(row):
        place = jnp.int32(0)
        for j in range(1, ROWS):
            place = jnp.where(slots[j] == row, j, place)
        return place

    whole = (0, 6 * NODES)
    inner = NODES - 2 * GLL
    edges = 6 * inner
    phases = (
        (0,) + whole,
        (1, 0, 4 * inner), (1, 4 * inner, edges), (1, edges, 6 * NODES),
        (2, 0, edges), (2, edges, 6 * NODES),
        (3,) + whole,
    )

    def pack_inner(which, slot, i, value):
        send_v[which, slot, pl.ds(i * inner, inner), :] = value.astype(LOW)

    def pack_edges(which, slot, i, low_edge, high_edge):
        send_v[which, slot, pl.ds(edges + i * 2 * GLL, 2 * GLL), :] = jnp.concatenate(
            [low_edge, high_edge], axis=0
        ).astype(LOW)

    def unpack(block, i):
        sides = block[edges + i * 2 * GLL : edges + (i + 1) * 2 * GLL]
        middle = block[i * inner : (i + 1) * inner]
        return jnp.concatenate([sides[:GLL], middle, sides[GLL:]], axis=0)

    def swap(phase, partner, arrival=False):
        which, begin, end = phases[phase]
        rows = pl.ds(begin, end - begin)
        slot = partner if arrival else member
        return pltpu.make_async_remote_copy(
            src_ref=send_v.at[which, partner, rows],
            dst_ref=recv[which].at[slot, rows],
            send_sem=send_sem.at[phase, partner],
            recv_sem=recv_sem.at[phase, slot],
            device_id={"modes": partner},
            device_id_type=MESH,
        )

    def start(phase):
        for partner in partners:
            swap(phase, partner).start()

    def sent(phase):
        for partner in partners:
            swap(phase, partner).wait_send()

    def arrived(phase):
        for partner in partners:
            swap(phase, partner, arrival=True).wait_recv()

    for load in loads[2 : 2 + ROWS]:
        load.wait()
    for row in range(ROWS):
        send_v[0, row] = flat(state_v[elem_of(row)]).astype(LOW)

    @pl.when(first)
    def _():
        pl.semaphore_wait(barrier, 4)
        greet(low_slab)

    @pl.when(jnp.logical_not(first))
    def _():
        pl.semaphore_wait(barrier, 5)

    @pl.when(last)
    def _():
        greet(high_slab)

    start(0)
    state_r[member] = send_v[0, member]

    w2_load.wait()
    own = elem_of(member)
    above = elem_of(jnp.minimum(member + 1, ROWS - 1))
    below = elem_of(jnp.maximum(member - 1, 0))

    def area(elem):
        return spacing_ref[0, elem] * spacing_ref[1, elem] * 0.25

    side_x = spacing_ref[0, own]
    side_y = spacing_ref[1, own]
    full = (NODES, 128)
    layer = lax.rem(lax.broadcasted_iota(jnp.int32, full, 0), GLL)
    has_above = jnp.logical_and(layer == GLL - 1, member < ROWS - 1)
    has_below = jnp.logical_and(layer == 0, member > 0)
    w2 = w2_v[...]
    quad = w2 * area(own)
    quad_v[...] = quad
    mass = quad + jnp.where(has_above, w2 * area(above), 0.0)
    mass = mass + jnp.where(has_below, w2 * area(below), 0.0)
    at_wall = jnp.logical_and(layer == 0, member == 0)
    keep = jnp.where(at_wall, 0.0, 1.0)
    scale_v[...] = keep / mass
    mass_send[0] = mass[NODES - GLL :]
    mass_send[1] = mass[:GLL]

    def mass_copy(way):
        return pltpu.make_async_remote_copy(
            src_ref=mass_send.at[way],
            dst_ref=mass_recv.at[way],
            send_sem=msend_sem.at[way],
            recv_sem=mrecv_sem.at[way],
            device_id={"elems": (high_slab, low_slab)[way]},
            device_id_type=MESH,
        )

    copies = jnp.where(jnp.logical_or(has_above, has_below), 2.0, 1.0).astype(F32)
    node_a = lax.broadcasted_iota(jnp.int32, full, 0) // GLL
    mult_v[...] = jnp.where(jnp.logical_or(node_a == 0, node_a == GLL - 1), 2.0 * copies, copies)

    edge_rows = 6 * GLL * groups
    top = pl.ds(GLL - 1, edge_rows, stride=GLL)
    low = pl.ds(0, edge_rows, stride=GLL)

    def edge_copy(which, way):
        if way == 0:
            target = {"modes": jnp.minimum(member + 1, ROWS - 1)}
        elif way == 1:
            target = {"modes": jnp.maximum(member - 1, 0)}
        else:
            target = {"elems": (high_slab, low_slab)[way - 2]}
        return pltpu.make_async_remote_copy(
            src_ref=edge_send.at[which, way],
            dst_ref=edge_recv.at[which, way],
            send_sem=esend_sem.at[which, way],
            recv_sem=erecv_sem.at[which, way],
            device_id=target,
            device_id_type=MESH,
        )

    def pack_around(which, buf):
        for way, begin in ((2, NODES - GLL), (3, 0)):
            edge_send[which, way] = jnp.concatenate(
                [buf[pl.ds(i * NODES + begin, GLL), :] for i in range(6 * groups)], axis=0
            ).astype(LOW)

    def add_around(which, buf):
        for way, begin in ((2, 0), (3, NODES - GLL)):
            edge_copy(which, way).wait_recv()
            came = edge_recv[which, way].astype(F32)
            for i in range(6 * groups):
                rows = pl.ds(i * NODES + begin, GLL)
                buf[rows, :] = buf[rows, :] + came[i * GLL : (i + 1) * GLL]

    def around_sent(which):
        for way in (2, 3):
            edge_copy(which, way).wait_send()

    adj_load.wait()
    obs_load.wait()
    for row in range(ROWS):
        elem = elem_of(row)
        psi_v[rows_of(row, 6 * NODES), :] = flat(adj_v[elem] - obs_v[elem].astype(F32))
    for row in range(ROWS - 1):
        lower = pl.ds(row * 6 * NODES + GLL - 1, 6 * GLL, stride=GLL)
        upper = pl.ds((row + 1) * 6 * NODES, 6 * GLL, stride=GLL)
        both = psi_v[lower, :] + psi_v[upper, :]
        psi_v[lower, :] = both
        psi_v[upper, :] = both
    pack_around(0, psi_v)
    mass_copy(0).start()
    edge_copy(0, 2).start()

    def send_back():
        mass_copy(1).start()
        edge_copy(0, 3).start()

    @pl.when(jnp.logical_not(first))
    def _():
        send_back()

    for row in range(ROWS):
        for i in range(6):
            rows = pl.ds((6 * row + i) * NODES + GLL, inner)
            pack_inner(1, row, i, psi_v[rows, :])
    forcing_r[member, pl.ds(0, edges), :] = send_v[1, member, pl.ds(0, edges), :]
    sent(0)
    start(1)

    fwd_load.wait()
    bwd_load.wait()
    lane = lax.broadcasted_iota(jnp.int32, (NODES, 3 * NODES), 1)
    ratio = jnp.full((NODES, 3 * NODES), side_y) / jnp.full((NODES, 3 * NODES), side_x)
    coef = jnp.where(
        lane < NODES, 0.5 * side_y, jnp.where(lane < 2 * NODES, 0.5 * side_x, -viscosity * ratio)
    )
    fwd_mat = (time_step * (fwd_v[0] * coef - fwd_v[1] * (viscosity / ratio))).astype(LOW)
    line = lax.broadcasted_iota(jnp.int32, (3 * NODES, NODES), 0)
    ratio = jnp.full((3 * NODES, NODES), side_y) / jnp.full((3 * NODES, NODES), side_x)
    coef = jnp.where(
        line < NODES, 0.5 * side_y, jnp.where(line < 2 * NODES, 0.5 * side_x, -viscosity * ratio)
    )
    bwd_mat = (bwd_v[0] * coef - bwd_v[1] * (viscosity / ratio)).astype(LOW)

    arrived(0)

    def gathered(phase, i):
        return jnp.concatenate([recv[phase][q, rows_of(i), :] for q in range(groups)], axis=1)

    def wide(block):
        return jnp.concatenate([block] * groups, axis=1)

    def field(buf, i):
        return jnp.concatenate([buf[rows_of(6 * q + i), :] for q in range(groups)], axis=1)

    def set_field(buf, i, value):
        for q in range(groups):
            buf[rows_of(6 * q + i), :] = value[:, q * 128 : (q + 1) * 128]

    mode_ids = lax.broadcasted_iota(jnp.int32, (NODES, modes), 1)
    wave = mode_ids.astype(F32) * (wave_scale / modes)

    synth_load.wait()
    even_v[...] = jnp.dot(
        jnp.concatenate([gathered(0, 2 * c) for c in range(3)], axis=0),
        synth_v[0],
        preferred_element_type=F32,
    )
    odd_v[...] = jnp.dot(
        jnp.concatenate([gathered(0, 2 * c + 1) for c in range(3)], axis=0),
        synth_v[1],
        preferred_element_type=F32,
    )

    for q, (left, right) in enumerate(pair_order):
        el, ol = even_v[rows_of(left), :], odd_v[rows_of(left), :]
        er, orr = even_v[rows_of(right), :], odd_v[rows_of(right), :]
        prod_v[0, rows_of(q), :] = (el * er + ol * orr).astype(LOW)
        prod_v[1, rows_of(q), :] = (el * orr + ol * er).astype(LOW)
    anal_load.wait()
    for p in range(2):
        modal_v[p] = jnp.dot(prod_v[p], anal_v[p], preferred_element_type=F32).astype(LOW)

    for c in range(3):
        for p in range(2):
            values = gathered(0, 2 * c + p)
            stack = jnp.concatenate(
                [
                    modal_v[p, rows_of(pair_index[0][c]), :],
                    modal_v[p, rows_of(pair_index[1][c]), :],
                    values,
                ],
                axis=0,
            )
            flux_z = modal_v[1 - p, rows_of(pair_index[2][c]), :].astype(F32)
            turn = (-time_step if p == 1 else time_step) * wave
            local = (1.0 - time_step * viscosity * wave * wave) * values.astype(F32)
            set_field(
                num_v,
                2 * c + p,
                jnp.dot(fwd_mat, stack, preferred_element_type=F32)
                + wide(quad_v[...]) * (local + turn * flux_z),
            )

    @pl.when(member < ROWS - 1)
    def _():
        edge_send[1, 0] = num_v[top, :].astype(LOW)
        edge_copy(1, 0).start()

    @pl.when(member > 0)
    def _():
        edge_send[1, 1] = num_v[low, :].astype(LOW)
        edge_copy(1, 1).start()

    start(2)

    @pl.when(first)
    def _():
        pl.semaphore_wait(barrier, 1)
        send_back()

    mass_copy(0).wait()
    mass_copy(1).wait()
    scale_v[:GLL, :] = keep[:GLL] / (mass_send[1] + mass_recv[0])
    scale_v[NODES - GLL :, :] = keep[NODES - GLL :] / (mass_send[0] + mass_recv[1])
    add_around(0, psi_v)
    for row in range(ROWS):
        for i in range(6):
            base = (6 * row + i) * NODES
            pack_edges(
                1, row, i, psi_v[pl.ds(base, GLL), :], psi_v[pl.ds(base + NODES - GLL, GLL), :]
            )
    forcing_r[member, pl.ds(edges, 12 * GLL), :] = send_v[1, member, pl.ds(edges, 12 * GLL), :]
    start(3)

    @pl.when(member > 0)
    def _():
        edge_copy(1, 0).wait_recv()
        num_v[low, :] = num_v[low, :] + edge_recv[1, 0].astype(F32)

    @pl.when(member < ROWS - 1)
    def _():
        edge_copy(1, 1).wait_recv()
        num_v[top, :] = num_v[top, :] + edge_recv[1, 1].astype(F32)

    pack_around(1, num_v)
    edge_copy(1, 2).start()
    edge_copy(1, 3).start()
    for q in range(groups):
        for i in range(6):
            rows = pl.ds((6 * q + i) * NODES + GLL, inner)
            value = scale_v[GLL : NODES - GLL, :] * num_v[rows, :]
            num_v[rows, :] = value
            pack_inner(2, q, i, value)
    next_r[member, pl.ds(0, edges), :] = send_v[2, member, pl.ds(0, edges), :]
    sent(1)
    sent(2)
    sent(3)
    start(4)
    add_around(1, num_v)
    for q in range(groups):
        for i in range(6):
            base = (6 * q + i) * NODES
            low_edge = scale_v[:GLL, :] * num_v[pl.ds(base, GLL), :]
            num_v[pl.ds(base, GLL), :] = low_edge
            high_edge = scale_v[NODES - GLL :, :] * num_v[pl.ds(base + NODES - GLL, GLL), :]
            num_v[pl.ds(base + NODES - GLL, GLL), :] = high_edge
            pack_edges(2, q, i, low_edge, high_edge)
    next_r[member, pl.ds(edges, 12 * GLL), :] = send_v[2, member, pl.ds(edges, 12 * GLL), :]
    start(5)

    arrived(1)
    arrived(2)
    arrived(3)
    for q in range(groups):
        block = forcing_r[q].astype(F32)
        for i in range(6):
            rows = rows_of(6 * q + i)
            psi_v[rows, :] = scale_v[...] * (unpack(block, i) + mult_v[...] * num_v[rows, :])

    norm = jnp.where(mode_ids == 0, 1.0 / (3.0 * modes), 0.5 / (3.0 * modes)).astype(F32)
    for p in range(2):
        lateral = []
        for c in range(3):
            psi = field(psi_v, 2 * c + p)
            other = field(psi_v, 2 * c + 1 - p)
            grads = jnp.dot(bwd_mat, psi.astype(LOW), preferred_element_type=F32)
            set_field(
                num_v,
                2 * c + p,
                wide(quad_v[...]) * ((1.0 - time_step * viscosity * wave * wave) * psi)
                + time_step * grads[2 * NODES :],
            )
            turn = -wave if p == 0 else wave
            lateral.append((grads[:NODES], grads[NODES : 2 * NODES], wide(quad_v[...]) * (turn * other)))
        for q, (left, right) in enumerate(pair_order):
            cot = lateral[right][left] + lateral[left][right]
            cot_v[p, rows_of(q), :] = (norm * cot).astype(LOW)

    for p in range(2):
        spread_v[p] = jnp.dot(cot_v[p], synth_v[p], preferred_element_type=F32)
    for c in range(3):
        even = jnp.zeros((NODES, even_v.shape[1]), F32)
        odd = jnp.zeros((NODES, even_v.shape[1]), F32)
        for d in range(3):
            se = spread_v[0, rows_of(pair_index[c][d]), :]
            so = spread_v[1, rows_of(pair_index[c][d]), :]
            ed, od = even_v[rows_of(d), :], odd_v[rows_of(d), :]
            even = even + (se * ed + so * od)
            odd = odd + (se * od + so * ed)
        pcot_v[0, rows_of(c), :] = even.astype(LOW)
        pcot_v[1, rows_of(c), :] = odd.astype(LOW)
    gain = jnp.where(mode_ids == 0, 3.0 * modes * time_step, 6.0 * modes * time_step).astype(F32)
    for p in range(2):
        back = jnp.dot(pcot_v[p], anal_v[p], preferred_element_type=F32)
        for c in range(3):
            low = (
                field(num_v, 2 * c + p) + gain * back[c * NODES : (c + 1) * NODES]
            ).astype(LOW)
            for q in range(groups):
                send_v[3, q, rows_of(2 * c + p), :] = low[:, q * 128 : (q + 1) * 128]
    start_r[member] = send_v[3, member]
    sent(4)
    sent(5)
    start(6)

    around_sent(0)
    around_sent(1)

    @pl.when(member < ROWS - 1)
    def _():
        edge_copy(1, 0).wait_send()

    @pl.when(member > 0)
    def _():
        edge_copy(1, 1).wait_send()

    arrived(4)
    arrived(5)
    for j in range(ROWS):
        block = next_r[slots[j]].astype(F32)
        for i in range(6):
            next_o[j, i // 2, i % 2] = unpack(block, i)
    arrived(6)
    for j in range(ROWS):
        start_o[j] = start_r[slots[j]].astype(F32).reshape(3, 2, NODES, 128)
    sent(6)


def store_kernel(next_v, start_v, next_ref, start_ref, sem):
    stores = [
        pltpu.make_async_copy(source.at[j], target.at[j], sem.at[which, j])
        for which, (source, target) in enumerate(((next_v, next_ref), (start_v, start_ref)))
        for j in range(ROWS)
    ]
    for store in stores:
        store.start()
    for store in stores:
        store.wait()


def on_device(state, adjoint_end, observed, spacing, radial_slot):
    groups = lax.axis_size("modes")
    slabs = lax.axis_size("elems")
    modes = groups * state.shape[4]
    half = 3 * modes // 2
    synth, analysis = half_tables(modes, 3 * modes)
    fwd, bwd, w2 = node_tables()
    any_spec = pl.BlockSpec(memory_space=pltpu.HBM)
    vmem_spec = pl.BlockSpec(memory_space=pltpu.VMEM)
    local = state.shape
    block = (6 * NODES, 128)
    vm = pltpu.VMEM
    sem = pltpu.SemaphoreType.DMA

    def run(*args):
        step_kernel(groups, slabs, *args)

    held_out = pltpu.VMEM(local, F32)

    def held(array):
        return pltpu.with_memory_space_constraint(array, pltpu.HBM)

    next_v, start_v = pl.pallas_call(
        run,
        out_shape=(held_out, held_out),
        in_specs=[any_spec] * 10,
        out_specs=(vmem_spec, vmem_spec),
        scratch_shapes=[
            pltpu.SMEM((2, ROWS), F32), pltpu.SMEM((1, ROWS), jnp.int32),
            vm(local, F32), vm(local, F32), vm(local, LOW),
            vm((2, modes, half), LOW), vm((2, half, modes), LOW),
            vm((2, NODES, 3 * NODES), F32), vm((2, 3 * NODES, NODES), F32), vm((NODES, 128), F32),
            vm((4, ROWS) + block, LOW), *[vm((ROWS,) + block, LOW)] * 4,
            vm((NODES, 128), F32), vm((NODES, 128), F32), vm((NODES, 128), F32),
            vm((3 * NODES, half), F32), vm((3 * NODES, half), F32),
            vm((2, 6 * NODES, half), LOW), vm((2, 6 * NODES, modes), LOW),
            vm((6 * NODES * groups, 128), F32), vm((6 * NODES * groups, 128), F32),
            vm((2, 6 * NODES, modes), LOW), vm((2, 6 * NODES, half), F32),
            vm((2, 3 * NODES, half), LOW),
            vm((2, 4, 6 * GLL * groups, 128), LOW), vm((2, 4, 6 * GLL * groups, 128), LOW),
            vm((2, GLL, 128), F32), vm((2, GLL, 128), F32),
            sem((9 + ROWS,)), sem((7, ROWS)), sem((7, ROWS)), sem((2, 4)), sem((2, 4)),
            sem((2,)), sem((2,)),
        ],
        compiler_params=pltpu.CompilerParams(
            collective_id=0, has_side_effects=True, vmem_limit_bytes=48 * 1024 * 1024
        ),
        cost_estimate=pl.CostEstimate(
            flops=1900000000, bytes_accessed=7000000, transcendentals=0
        ),
    )(
        held(state), held(adjoint_end), held(observed), held(spacing.T), held(radial_slot),
        held(jnp.asarray(synth, F32).astype(LOW)), held(jnp.asarray(analysis, F32).astype(LOW)),
        held(jnp.asarray(fwd, F32)), held(jnp.asarray(bwd, F32)),
        held(jnp.asarray(np.broadcast_to(w2[:, None], (NODES, 128)), F32)),
    )
    return pl.pallas_call(
        store_kernel,
        out_shape=(jax.ShapeDtypeStruct(local, F32), jax.ShapeDtypeStruct(local, F32)),
        in_specs=[pl.BlockSpec(memory_space=pl.ANY)] * 2,
        out_specs=(any_spec, any_spec),
        scratch_shapes=[sem((2, ROWS))],
        compiler_params=pltpu.CompilerParams(vmem_limit_bytes=1024 * 1024),
    )(next_v, start_v)


def solution(mesh):
    in_specs = (
        P("elems", None, None, None, "modes"),
        P("elems", None, None, None, "modes"),
        P("elems", None, None, None, "modes"),
        P("elems", None),
        P("elems", None),
    )
    out_specs = (P("elems", None, None, None, "modes"), P("elems", None, None, None, "modes"))
    return jax.shard_map(
        on_device, mesh=mesh, in_specs=in_specs, out_specs=out_specs, check_vma=False
    )
```

```python
import jax
import jax.numpy as jnp
import numpy as np
from jax import lax
from jax.experimental import pallas as pl
from jax.experimental.pallas import tpu as pltpu
from jax.sharding import PartitionSpec as P

GLL = 8
NODES = GLL * GLL
ROWS = 4
CHIP_ROW = 8
time_step = 0.01
viscosity = 0.05
wave_scale = 4.0
pair_order = ((0, 0), (0, 1), (0, 2), (1, 1), (1, 2), (2, 2))
pair_index = ((0, 1, 2), (1, 3, 4), (2, 4, 5))
F32 = jnp.float32
LOW = jnp.bfloat16
MESH = pl.DeviceIdType.MESH


def legendre_table(points, quad_count):
    columns = [points * 0.0 + 1.0, points]
    for degree in range(2, quad_count):
        columns.append(
            ((2 * degree - 1) * points * columns[-1] - (degree - 1) * columns[-2]) / degree
        )
    return np.stack(columns, axis=1)


def gll_tables(quad_count):
    degree = quad_count - 1
    points = -np.cos(np.pi * np.arange(quad_count) / degree)
    for repeat in range(60):
        vander = legendre_table(points, quad_count)
        points = points - (points * vander[:, degree] - vander[:, degree - 1]) / (
            quad_count * vander[:, degree]
        )
    vander = legendre_table(points, quad_count)
    edge_value = vander[:, degree]
    weights = 2.0 / (degree * quad_count * edge_value * edge_value)
    diagonal_mask = np.arange(quad_count)[:, None] == np.arange(quad_count)[None, :]
    differ = np.where(diagonal_mask, 1.0, points[:, None] - points[None, :])
    derivative = np.where(diagonal_mask, 0.0, edge_value[:, None] / (edge_value[None, :] * differ))
    derivative[0, 0] = -degree * quad_count / 4.0
    derivative[degree, degree] = degree * quad_count / 4.0
    return (weights, derivative)


def half_tables(modes, planes):
    half = planes // 2
    turns = np.outer(np.arange(modes), 2 * np.arange(half) + 1) % (2 * planes)
    angles = np.pi * turns / planes
    factor = np.where(np.arange(modes) == 0, 1.0, 2.0)[:, None]
    synth = np.stack((factor * np.cos(angles), -factor * np.sin(angles)))
    analysis = np.stack((np.cos(angles), -np.sin(angles))) * (2.0 / planes)
    return synth, np.transpose(analysis, (0, 2, 1))


def node_tables():
    weights, deriv = gll_tables(GLL)
    wdiag = np.diag(weights)
    back = deriv.T @ wdiag
    ahead = wdiag @ deriv
    stiff = deriv.T @ wdiag @ deriv
    zero = np.zeros((NODES, NODES))
    fwd = (
        np.concatenate((np.kron(back, wdiag), np.kron(wdiag, back), np.kron(stiff, wdiag)), 1),
        np.concatenate((zero, zero, np.kron(wdiag, stiff)), 1),
    )
    adj = (
        np.concatenate((np.kron(ahead, wdiag), np.kron(wdiag, ahead), np.kron(stiff, wdiag)), 0),
        np.concatenate((zero, zero, np.kron(wdiag, stiff)), 0),
    )
    return np.stack(fwd), np.stack(adj), np.kron(weights, weights)


def step_kernel(
    groups,
    slabs,
    state_ref, adj_ref, obs_ref, spacing_h, slot_h, synth_ref, anal_ref, fwd_ref, bwd_ref, w2_ref,
    next_o, start_o,
    spacing_ref, slot_ref, state_v, adj_v, obs_v, synth_v, anal_v, fwd_v, bwd_v, w2_v,
    send_v, state_r, forcing_r, next_r, start_r, quad_v, scale_v, mult_v,
    even_v, odd_v, prod_v, modal_v, num_v, psi_v, cot_v, spread_v, pcot_v,
    edge_send, edge_recv, stage_v, full_v, mass_send, mass_recv,
    load_sem, send_sem, recv_sem, esend_sem, erecv_sem, msend_sem, mrecv_sem,
):
    member = lax.axis_index("modes")
    slab = lax.axis_index("elems")
    low_slab = lax.rem(slab + slabs - 1, slabs)
    high_slab = lax.rem(slab + 1, slabs)
    partners = (lax.rem(member + 2, 4), 3 - member, member + 1 - 2 * lax.rem(member, 2))
    modes = groups * 128
    recv = (state_r, forcing_r, next_r, start_r)

    loads = [
        pltpu.make_async_copy(src, dst, load_sem.at[i])
        for i, (src, dst) in enumerate(
            [(slot_h, slot_ref), (spacing_h, spacing_ref)]
            + [(state_ref.at[j], state_v.at[j]) for j in range(ROWS)]
            + [
                (adj_ref, adj_v), (obs_ref, obs_v), (w2_ref, w2_v),
                (fwd_ref, fwd_v), (synth_ref, synth_v), (anal_ref, anal_v), (bwd_ref, bwd_v),
            ]
        )
    ]
    adj_load, obs_load, w2_load, fwd_load, synth_load, anal_load, bwd_load = loads[2 + ROWS :]
    for load in loads:
        load.start()

    barrier = pltpu.get_barrier_semaphore()
    for partner in partners:
        pl.semaphore_signal(barrier, inc=1, device_id={"modes": partner}, device_id_type=MESH)

    place = lax.rem(slab, 2 * CHIP_ROW)
    early_low = place == 0
    early_high = place == CHIP_ROW - 1
    across_low = jnp.logical_or(early_low, place == CHIP_ROW)
    across_high = jnp.logical_or(early_high, place == 2 * CHIP_ROW - 1)
    early = jnp.logical_or(early_low, early_high)
    greet_low_now = jnp.logical_not(across_low)
    greet_high_now = jnp.logical_not(across_high)

    mirrored = place >= CHIP_ROW

    def flip(index):
        return jnp.where(mirrored, ROWS - 1 - index, index)

    row_here = flip(member)

    def around(way):
        across = (across_high, across_low)[way]
        return {
            "modes": jnp.where(across, ROWS - 1 - member, member),
            "elems": (high_slab, low_slab)[way],
        }

    def greet(way):
        pl.semaphore_signal(barrier, inc=1, device_id=around(way), device_id_type=MESH)

    @pl.when(greet_low_now)
    def _():
        greet(1)

    @pl.when(greet_high_now)
    def _():
        greet(0)

    loads[0].wait()
    loads[1].wait()
    slots = [slot_ref[0, j] for j in range(ROWS)]

    def rows_of(index, count=NODES):
        return pl.ds(index * count, count)

    def flat(block):
        return block.reshape(6 * NODES, 128)

    def elem_of(row):
        place = jnp.int32(0)
        for j in range(1, ROWS):
            place = jnp.where(slots[j] == row, j, place)
        return place

    whole = (0, 6 * NODES)
    inner = NODES - 2 * GLL
    edges = 12 * GLL
    spare = 4
    kept = 6 * inner - spare * GLL
    phases = (
        (0,) + whole,
        (1, 0, edges + inner), (1, edges + inner, 6 * NODES),
        (2, 0, kept), (2, kept, kept + 6 * GLL),
        (3,) + whole,
        (2, kept + 6 * GLL, kept + 12 * GLL),
    )

    def unpack(block, i):
        sides = block[i * 2 * GLL : (i + 1) * 2 * GLL]
        middle = block[edges + i * inner : edges + (i + 1) * inner]
        return jnp.concatenate([sides[:GLL], middle, sides[GLL:]], axis=0)

    def swap(phase, partner, arrival=False):
        which, begin, end = phases[phase]
        rows = pl.ds(begin, end - begin)
        slot = partner if arrival else member
        return pltpu.make_async_remote_copy(
            src_ref=send_v.at[which, partner, rows],
            dst_ref=recv[which].at[slot, rows],
            send_sem=send_sem.at[phase, partner],
            recv_sem=recv_sem.at[phase, slot],
            device_id={"modes": partner},
            device_id_type=MESH,
        )

    def start(phase):
        for partner in partners:
            swap(phase, partner).start()

    def sent(phase):
        for partner in partners:
            swap(phase, partner).wait_send()

    def arrived(phase):
        for partner in partners:
            swap(phase, partner, arrival=True).wait_recv()

    for load in loads[2 : 2 + ROWS]:
        load.wait()
    for device in range(ROWS):
        send_v[0, device] = flat(state_v[elem_of(flip(device))]).astype(LOW)

    @pl.when(early)
    def _():
        pl.semaphore_wait(barrier, 4)

    @pl.when(jnp.logical_not(early))
    def _():
        pl.semaphore_wait(barrier, 5)

    @pl.when(jnp.logical_not(greet_low_now))
    def _():
        greet(1)

    @pl.when(jnp.logical_not(greet_high_now))
    def _():
        greet(0)

    start(0)
    state_r[member] = send_v[0, member]

    w2_load.wait()
    own = elem_of(row_here)
    row_above = jnp.minimum(row_here + 1, ROWS - 1)
    row_below = jnp.maximum(row_here - 1, 0)
    above = elem_of(row_above)
    below = elem_of(row_below)

    def area(elem):
        return spacing_ref[0, elem] * spacing_ref[1, elem] * 0.25

    side_x = spacing_ref[0, own]
    side_y = spacing_ref[1, own]
    full = (NODES, 128)
    layer = lax.rem(lax.broadcasted_iota(jnp.int32, full, 0), GLL)
    has_above = jnp.logical_and(layer == GLL - 1, row_here < ROWS - 1)
    has_below = jnp.logical_and(layer == 0, row_here > 0)
    w2 = w2_v[...]
    quad = w2 * area(own)
    quad_v[...] = quad
    mass = quad + jnp.where(has_above, w2 * area(above), 0.0)
    mass = mass + jnp.where(has_below, w2 * area(below), 0.0)
    at_wall = jnp.logical_and(layer == 0, row_here == 0)
    keep = jnp.where(at_wall, 0.0, 1.0)
    scale_v[...] = keep / mass
    mass_send[0] = mass[NODES - GLL :]
    mass_send[1] = mass[:GLL]

    def mass_copy(way):
        return pltpu.make_async_remote_copy(
            src_ref=mass_send.at[way],
            dst_ref=mass_recv.at[way],
            send_sem=msend_sem.at[way],
            recv_sem=mrecv_sem.at[way],
            device_id=around(way),
            device_id_type=MESH,
        )

    copies = jnp.where(jnp.logical_or(has_above, has_below), 2.0, 1.0).astype(F32)
    node_a = lax.broadcasted_iota(jnp.int32, full, 0) // GLL
    mult_v[...] = jnp.where(jnp.logical_or(node_a == 0, node_a == GLL - 1), 2.0 * copies, copies)

    edge_rows = 6 * GLL * groups
    top = pl.ds(GLL - 1, edge_rows, stride=GLL)
    low = pl.ds(0, edge_rows, stride=GLL)

    def edge_copy(which, way):
        if way == 0:
            target = {"modes": flip(row_above)}
        elif way == 1:
            target = {"modes": flip(row_below)}
        else:
            target = around(way - 2)
        return pltpu.make_async_remote_copy(
            src_ref=edge_send.at[which, way],
            dst_ref=edge_recv.at[which, way],
            send_sem=esend_sem.at[which, way],
            recv_sem=erecv_sem.at[which, way],
            device_id=target,
            device_id_type=MESH,
        )

    def pack_around(which, buf):
        for way, begin in ((2, NODES - GLL), (3, 0)):
            edge_send[which, way] = jnp.concatenate(
                [buf[pl.ds(i * NODES + begin, GLL), :] for i in range(6 * groups)], axis=0
            ).astype(LOW)

    def add_around(which, buf):
        for way, begin in ((2, 0), (3, NODES - GLL)):
            edge_copy(which, way).wait_recv()
            came = edge_recv[which, way].astype(F32)
            for i in range(6 * groups):
                rows = pl.ds(i * NODES + begin, GLL)
                buf[rows, :] = buf[rows, :] + came[i * GLL : (i + 1) * GLL]

    def around_sent(which):
        for way in (2, 3):
            edge_copy(which, way).wait_send()

    adj_load.wait()
    obs_load.wait()
    for row in range(ROWS):
        elem = elem_of(row)
        psi_v[rows_of(row, 6 * NODES), :] = flat(adj_v[elem] - obs_v[elem].astype(F32))
    for row in range(ROWS - 1):
        lower = pl.ds(row * 6 * NODES + GLL - 1, 6 * GLL, stride=GLL)
        upper = pl.ds((row + 1) * 6 * NODES, 6 * GLL, stride=GLL)
        both = psi_v[lower, :] + psi_v[upper, :]
        psi_v[lower, :] = both
        psi_v[upper, :] = both
    for row in range(ROWS):
        device = flip(row)
        for i in range(6):
            base = (6 * row + i) * NODES
            send_v[1, device, pl.ds(i * 2 * GLL, 2 * GLL), :] = jnp.concatenate(
                [psi_v[pl.ds(base, GLL), :], psi_v[pl.ds(base + NODES - GLL, GLL), :]], axis=0
            ).astype(LOW)
            send_v[1, device, pl.ds(edges + i * inner, inner), :] = psi_v[
                pl.ds(base + GLL, inner), :
            ].astype(LOW)
    forcing_r[member] = send_v[1, member]
    sent(0)
    start(1)

    fwd_load.wait()
    bwd_load.wait()
    lane = lax.broadcasted_iota(jnp.int32, (NODES, 3 * NODES), 1)
    ratio = jnp.full((NODES, 3 * NODES), side_y) / jnp.full((NODES, 3 * NODES), side_x)
    coef = jnp.where(
        lane < NODES, 0.5 * side_y, jnp.where(lane < 2 * NODES, 0.5 * side_x, -viscosity * ratio)
    )
    fwd_mat = (time_step * (fwd_v[0] * coef - fwd_v[1] * (viscosity / ratio))).astype(LOW)
    line = lax.broadcasted_iota(jnp.int32, (3 * NODES, NODES), 0)
    ratio = jnp.full((3 * NODES, NODES), side_y) / jnp.full((3 * NODES, NODES), side_x)
    coef = jnp.where(
        line < NODES, 0.5 * side_y, jnp.where(line < 2 * NODES, 0.5 * side_x, -viscosity * ratio)
    )
    bwd_mat = (bwd_v[0] * coef - bwd_v[1] * (viscosity / ratio)).astype(LOW)

    arrived(0)

    def gathered(phase, i):
        return jnp.concatenate([recv[phase][q, rows_of(i), :] for q in range(groups)], axis=1)

    def wide(block):
        return jnp.concatenate([block] * groups, axis=1)

    def field(buf, i):
        return jnp.concatenate([buf[rows_of(6 * q + i), :] for q in range(groups)], axis=1)

    def set_field(buf, i, value):
        for q in range(groups):
            buf[rows_of(6 * q + i), :] = value[:, q * 128 : (q + 1) * 128]

    mode_ids = lax.broadcasted_iota(jnp.int32, (NODES, modes), 1)
    wave = mode_ids.astype(F32) * (wave_scale / modes)

    synth_load.wait()
    even_v[...] = jnp.dot(
        jnp.concatenate([gathered(0, 2 * c) for c in range(3)], axis=0),
        synth_v[0],
        preferred_element_type=F32,
    )
    odd_v[...] = jnp.dot(
        jnp.concatenate([gathered(0, 2 * c + 1) for c in range(3)], axis=0),
        synth_v[1],
        preferred_element_type=F32,
    )

    for q, (left, right) in enumerate(pair_order):
        el, ol = even_v[rows_of(left), :], odd_v[rows_of(left), :]
        er, orr = even_v[rows_of(right), :], odd_v[rows_of(right), :]
        prod_v[0, rows_of(q), :] = (el * er + ol * orr).astype(LOW)
        prod_v[1, rows_of(q), :] = (el * orr + ol * er).astype(LOW)
    anal_load.wait()
    for p in range(2):
        modal_v[p] = jnp.dot(prod_v[p], anal_v[p], preferred_element_type=F32).astype(LOW)

    for c in range(3):
        for p in range(2):
            values = gathered(0, 2 * c + p)
            stack = jnp.concatenate(
                [
                    modal_v[p, rows_of(pair_index[0][c]), :],
                    modal_v[p, rows_of(pair_index[1][c]), :],
                    values,
                ],
                axis=0,
            )
            flux_z = modal_v[1 - p, rows_of(pair_index[2][c]), :].astype(F32)
            turn = (-time_step if p == 1 else time_step) * wave
            local = (1.0 - time_step * viscosity * wave * wave) * values.astype(F32)
            set_field(
                num_v,
                2 * c + p,
                jnp.dot(fwd_mat, stack, preferred_element_type=F32)
                + wide(quad_v[...]) * (local + turn * flux_z),
            )

    @pl.when(row_here < ROWS - 1)
    def _():
        edge_send[1, 0] = num_v[top, :].astype(LOW)
        edge_copy(1, 0).start()

    @pl.when(row_here > 0)
    def _():
        edge_send[1, 1] = num_v[low, :].astype(LOW)
        edge_copy(1, 1).start()

    start(2)

    @pl.when(early)
    def _():
        pl.semaphore_wait(barrier, 1)

    mass_copy(0).start()
    mass_copy(1).start()
    arrived(1)
    for q in range(groups):
        block = forcing_r[q, pl.ds(0, edges), :].astype(F32)
        for way, begin in ((2, GLL), (3, 0)):
            edge_send[0, way, pl.ds(q * 6 * GLL, 6 * GLL), :] = jnp.concatenate(
                [block[i * 2 * GLL + begin : i * 2 * GLL + begin + GLL] for i in range(6)], axis=0
            ).astype(LOW)
    edge_copy(0, 2).start()
    edge_copy(0, 3).start()

    @pl.when(row_here > 0)
    def _():
        edge_copy(1, 0).wait_recv()
        num_v[low, :] = num_v[low, :] + edge_recv[1, 0].astype(F32)

    @pl.when(row_here < ROWS - 1)
    def _():
        edge_copy(1, 1).wait_recv()
        num_v[top, :] = num_v[top, :] + edge_recv[1, 1].astype(F32)

    pack_around(1, num_v)
    edge_copy(1, 2).start()
    edge_copy(1, 3).start()
    for q in range(groups):
        for i in range(6):
            rows = pl.ds((6 * q + i) * NODES + GLL, inner)
            value = scale_v[GLL : NODES - GLL, :] * num_v[rows, :]
            num_v[rows, :] = value
            if i < 5:
                stage_v[q, pl.ds(i * inner, inner), :] = value
            else:
                stage_v[q, pl.ds(i * inner, inner - spare * GLL), :] = value[: inner - spare * GLL]
                for k in range(spare):
                    tile = value[inner - (spare - k) * GLL : inner - (spare - k - 1) * GLL]
                    stage_v[q, pl.ds(k * GLL * GLL, GLL, stride=GLL), :] = tile
        send_v[2, q, pl.ds(0, kept), :] = stage_v[q].astype(LOW)
    next_r[member, pl.ds(0, kept), :] = send_v[2, member, pl.ds(0, kept), :]
    sent(1)
    sent(2)
    start(3)
    mass_copy(0).wait()
    mass_copy(1).wait()
    scale_v[:GLL, :] = keep[:GLL] / (mass_send[1] + mass_recv[0])
    scale_v[NODES - GLL :, :] = keep[NODES - GLL :] / (mass_send[0] + mass_recv[1])
    add_around(1, num_v)
    for q in range(groups):
        for i in range(6):
            base = (6 * q + i) * NODES
            low_edge = scale_v[:GLL, :] * num_v[pl.ds(base, GLL), :]
            num_v[pl.ds(base, GLL), :] = low_edge
            high_edge = scale_v[NODES - GLL :, :] * num_v[pl.ds(base + NODES - GLL, GLL), :]
            num_v[pl.ds(base + NODES - GLL, GLL), :] = high_edge
            stage_v[q, pl.ds(i * GLL, GLL), :] = low_edge
            stage_v[q, pl.ds((6 + i) * GLL, GLL), :] = high_edge
        send_v[2, q, pl.ds(kept, 12 * GLL), :] = stage_v[q, pl.ds(0, 12 * GLL), :].astype(LOW)
    next_r[member, pl.ds(kept, 12 * GLL), :] = send_v[2, member, pl.ds(kept, 12 * GLL), :]
    start(4)

    @pl.when(across_high)
    def _():
        start(6)

    arrived(2)
    for q in range(groups):
        block = forcing_r[q].astype(F32)
        for i in range(6):
            rows = rows_of(6 * q + i)
            psi_v[rows, :] = unpack(block, i)
    add_around(0, psi_v)
    for i in range(6 * groups):
        rows = rows_of(i)
        psi_v[rows, :] = scale_v[...] * (psi_v[rows, :] + mult_v[...] * num_v[rows, :])

    norm = jnp.where(mode_ids == 0, 1.0 / (3.0 * modes), 0.5 / (3.0 * modes)).astype(F32)
    for p in range(2):
        lateral = []
        for c in range(3):
            psi = field(psi_v, 2 * c + p)
            other = field(psi_v, 2 * c + 1 - p)
            grads = jnp.dot(bwd_mat, psi.astype(LOW), preferred_element_type=F32)
            set_field(
                num_v,
                2 * c + p,
                wide(quad_v[...]) * ((1.0 - time_step * viscosity * wave * wave) * psi)
                + time_step * grads[2 * NODES :],
            )
            turn = -wave if p == 0 else wave
            lateral.append((grads[:NODES], grads[NODES : 2 * NODES], wide(quad_v[...]) * (turn * other)))
        for q, (left, right) in enumerate(pair_order):
            cot = lateral[right][left] + lateral[left][right]
            cot_v[p, rows_of(q), :] = (norm * cot).astype(LOW)

    for p in range(2):
        spread_v[p] = jnp.dot(cot_v[p], synth_v[p], preferred_element_type=F32)
    for c in range(3):
        even = jnp.zeros((NODES, even_v.shape[1]), F32)
        odd = jnp.zeros((NODES, even_v.shape[1]), F32)
        for d in range(3):
            se = spread_v[0, rows_of(pair_index[c][d]), :]
            so = spread_v[1, rows_of(pair_index[c][d]), :]
            ed, od = even_v[rows_of(d), :], odd_v[rows_of(d), :]
            even = even + (se * ed + so * od)
            odd = odd + (se * od + so * ed)
        pcot_v[0, rows_of(c), :] = even.astype(LOW)
        pcot_v[1, rows_of(c), :] = odd.astype(LOW)
    gain = jnp.where(mode_ids == 0, 3.0 * modes * time_step, 6.0 * modes * time_step).astype(F32)
    for p in range(2):
        back = jnp.dot(pcot_v[p], anal_v[p], preferred_element_type=F32)
        for c in range(3):
            low = (
                field(num_v, 2 * c + p) + gain * back[c * NODES : (c + 1) * NODES]
            ).astype(LOW)
            for q in range(groups):
                send_v[3, q, rows_of(2 * c + p), :] = low[:, q * 128 : (q + 1) * 128]
    start_r[member] = send_v[3, member]
    sent(3)
    sent(4)

    @pl.when(across_high)
    def _():
        sent(6)

    start(5)

    around_sent(0)
    around_sent(1)

    @pl.when(row_here < ROWS - 1)
    def _():
        edge_copy(1, 0).wait_send()

    @pl.when(row_here > 0)
    def _():
        edge_copy(1, 1).wait_send()

    arrived(3)
    arrived(4)
    for row in range(ROWS):
        edge_send[0, 0, pl.ds(row * 6 * GLL, 6 * GLL), :] = next_r[
            flip(row), pl.ds(kept, 6 * GLL), :
        ]
    side_copy = pltpu.make_async_remote_copy(
        src_ref=edge_send.at[0, 0],
        dst_ref=edge_recv.at[0, 0],
        send_sem=esend_sem.at[0, 0],
        recv_sem=erecv_sem.at[0, 0],
        device_id={"elems": low_slab},
        device_id_type=MESH,
    )

    @pl.when(jnp.logical_not(across_low))
    def _():
        side_copy.start()

    for row in range(ROWS):
        block = next_r[flip(row), pl.ds(0, kept + 6 * GLL), :].astype(F32)
        stage_v[row] = block[:kept]
        for i in range(6):
            full_v[row, pl.ds(i * NODES, GLL), :] = block[kept + i * GLL : kept + (i + 1) * GLL]
            count = inner if i < 5 else inner - spare * GLL
            full_v[row, pl.ds(i * NODES + GLL, count), :] = block[i * inner : i * inner + count]
        for k in range(spare):
            tile = stage_v[row, pl.ds(k * GLL * GLL, GLL, stride=GLL), :]
            full_v[row, pl.ds(6 * NODES - (spare - k + 1) * GLL, GLL), :] = tile

    @pl.when(jnp.logical_not(across_low))
    def _():
        side_copy.wait_send()

    @pl.when(jnp.logical_not(across_high))
    def _():
        side_copy.wait_recv()

    @pl.when(across_high)
    def _():
        arrived(6)
        for row in range(ROWS):
            edge_recv[0, 0, pl.ds(row * 6 * GLL, 6 * GLL), :] = next_r[
                flip(row), pl.ds(kept + 6 * GLL, 6 * GLL), :
            ]

    for row in range(ROWS):
        side = edge_recv[0, 0, pl.ds(row * 6 * GLL, 6 * GLL), :].astype(F32)
        for i in range(6):
            full_v[row, pl.ds((i + 1) * NODES - GLL, GLL), :] = side[i * GLL : (i + 1) * GLL]
        if row == 0:
            shared = jnp.zeros((6 * GLL, 128), F32)
        else:
            shared = full_v[row - 1, pl.ds(GLL - 1, 6 * GLL, stride=GLL), :]
        full_v[row, pl.ds(0, 6 * GLL, stride=GLL), :] = shared
    for j in range(ROWS):
        next_o[j] = full_v[slots[j]].reshape(3, 2, NODES, 128)
    arrived(5)
    for j in range(ROWS):
        start_o[j] = start_r[flip(slots[j])].astype(F32).reshape(3, 2, NODES, 128)
    sent(5)


def store_kernel(next_v, start_v, next_ref, start_ref, sem):
    stores = [
        pltpu.make_async_copy(source.at[j], target.at[j], sem.at[which, j])
        for which, (source, target) in enumerate(((next_v, next_ref), (start_v, start_ref)))
        for j in range(ROWS)
    ]
    for store in stores:
        store.start()
    for store in stores:
        store.wait()


def on_device(state, adjoint_end, observed, spacing, radial_slot):
    groups = lax.axis_size("modes")
    slabs = lax.axis_size("elems")
    modes = groups * state.shape[4]
    half = 3 * modes // 2
    synth, analysis = half_tables(modes, 3 * modes)
    fwd, bwd, w2 = node_tables()
    any_spec = pl.BlockSpec(memory_space=pltpu.HBM)
    vmem_spec = pl.BlockSpec(memory_space=pltpu.VMEM)
    local = state.shape
    block = (6 * NODES, 128)
    vm = pltpu.VMEM
    sem = pltpu.SemaphoreType.DMA

    def run(*args):
        step_kernel(groups, slabs, *args)

    held_out = pltpu.VMEM(local, F32)

    def held(array):
        return pltpu.with_memory_space_constraint(array, pltpu.HBM)

    next_v, start_v = pl.pallas_call(
        run,
        out_shape=(held_out, held_out),
        in_specs=[any_spec] * 10,
        out_specs=(vmem_spec, vmem_spec),
        scratch_shapes=[
            pltpu.SMEM((2, ROWS), F32), pltpu.SMEM((1, ROWS), jnp.int32),
            vm(local, F32), vm(local, F32), vm(local, LOW),
            vm((2, modes, half), LOW), vm((2, half, modes), LOW),
            vm((2, NODES, 3 * NODES), F32), vm((2, 3 * NODES, NODES), F32), vm((NODES, 128), F32),
            vm((4, ROWS) + block, LOW), *[vm((ROWS,) + block, LOW)] * 4,
            vm((NODES, 128), F32), vm((NODES, 128), F32), vm((NODES, 128), F32),
            vm((3 * NODES, half), F32), vm((3 * NODES, half), F32),
            vm((2, 6 * NODES, half), LOW), vm((2, 6 * NODES, modes), LOW),
            vm((6 * NODES * groups, 128), F32), vm((6 * NODES * groups, 128), F32),
            vm((2, 6 * NODES, modes), LOW), vm((2, 6 * NODES, half), F32),
            vm((2, 3 * NODES, half), LOW),
            vm((2, 4, 6 * GLL * groups, 128), LOW), vm((2, 4, 6 * GLL * groups, 128), LOW),
            vm((ROWS, 256, 128), F32), vm((ROWS,) + block, F32),
            vm((2, GLL, 128), F32), vm((2, GLL, 128), F32),
            sem((9 + ROWS,)), sem((7, ROWS)), sem((7, ROWS)), sem((2, 4)), sem((2, 4)),
            sem((2,)), sem((2,)),
        ],
        compiler_params=pltpu.CompilerParams(
            collective_id=0, has_side_effects=True, vmem_limit_bytes=48 * 1024 * 1024
        ),
        cost_estimate=pl.CostEstimate(
            flops=1900000000, bytes_accessed=7000000, transcendentals=0
        ),
    )(
        held(state), held(adjoint_end), held(observed), held(spacing.T), held(radial_slot),
        held(jnp.asarray(synth, F32).astype(LOW)), held(jnp.asarray(analysis, F32).astype(LOW)),
        held(jnp.asarray(fwd, F32)), held(jnp.asarray(bwd, F32)),
        held(jnp.asarray(np.broadcast_to(w2[:, None], (NODES, 128)), F32)),
    )
    return pl.pallas_call(
        store_kernel,
        out_shape=(jax.ShapeDtypeStruct(local, F32), jax.ShapeDtypeStruct(local, F32)),
        in_specs=[pl.BlockSpec(memory_space=pl.ANY)] * 2,
        out_specs=(any_spec, any_spec),
        scratch_shapes=[sem((2, ROWS))],
        compiler_params=pltpu.CompilerParams(vmem_limit_bytes=1024 * 1024),
    )(next_v, start_v)


def solution(mesh):
    in_specs = (
        P("elems", None, None, None, "modes"),
        P("elems", None, None, None, "modes"),
        P("elems", None, None, None, "modes"),
        P("elems", None),
        P("elems", None),
    )
    out_specs = (P("elems", None, None, None, "modes"), P("elems", None, None, None, "modes"))
    return jax.shard_map(
        on_device, mesh=mesh, in_specs=in_specs, out_specs=out_specs, check_vma=False
    )
```

```python
import jax
import jax.numpy as jnp
import numpy as np
from jax import lax
from jax.experimental import pallas as pl
from jax.experimental.pallas import tpu as pltpu
from jax.sharding import PartitionSpec as P

GLL = 8
NODES = GLL * GLL
ROWS = 4
CHIP_ROW = 8
time_step = 0.01
viscosity = 0.05
wave_scale = 4.0
pair_order = ((0, 0), (0, 1), (0, 2), (1, 1), (1, 2), (2, 2))
pair_index = ((0, 1, 2), (1, 3, 4), (2, 4, 5))
F32 = jnp.float32
LOW = jnp.bfloat16
MESH = pl.DeviceIdType.MESH


def legendre_table(points, quad_count):
    columns = [points * 0.0 + 1.0, points]
    for degree in range(2, quad_count):
        columns.append(
            ((2 * degree - 1) * points * columns[-1] - (degree - 1) * columns[-2]) / degree
        )
    return np.stack(columns, axis=1)


def gll_tables(quad_count):
    degree = quad_count - 1
    points = -np.cos(np.pi * np.arange(quad_count) / degree)
    for repeat in range(60):
        vander = legendre_table(points, quad_count)
        points = points - (points * vander[:, degree] - vander[:, degree - 1]) / (
            quad_count * vander[:, degree]
        )
    vander = legendre_table(points, quad_count)
    edge_value = vander[:, degree]
    weights = 2.0 / (degree * quad_count * edge_value * edge_value)
    diagonal_mask = np.arange(quad_count)[:, None] == np.arange(quad_count)[None, :]
    differ = np.where(diagonal_mask, 1.0, points[:, None] - points[None, :])
    derivative = np.where(diagonal_mask, 0.0, edge_value[:, None] / (edge_value[None, :] * differ))
    derivative[0, 0] = -degree * quad_count / 4.0
    derivative[degree, degree] = degree * quad_count / 4.0
    return (weights, derivative)


def half_tables(modes, planes):
    half = planes // 2
    turns = np.outer(np.arange(modes), 2 * np.arange(half) + 1) % (2 * planes)
    angles = np.pi * turns / planes
    factor = np.where(np.arange(modes) == 0, 1.0, 2.0)[:, None]
    synth = np.stack((factor * np.cos(angles), -factor * np.sin(angles)))
    analysis = np.stack((np.cos(angles), -np.sin(angles))) * (2.0 / planes)
    return synth, np.transpose(analysis, (0, 2, 1))


def node_tables():
    weights, deriv = gll_tables(GLL)
    wdiag = np.diag(weights)
    back = deriv.T @ wdiag
    ahead = wdiag @ deriv
    stiff = deriv.T @ wdiag @ deriv
    zero = np.zeros((NODES, NODES))
    fwd = (
        np.concatenate((np.kron(back, wdiag), np.kron(wdiag, back), np.kron(stiff, wdiag)), 1),
        np.concatenate((zero, zero, np.kron(wdiag, stiff)), 1),
    )
    adj = (
        np.concatenate((np.kron(ahead, wdiag), np.kron(wdiag, ahead), np.kron(stiff, wdiag)), 0),
        np.concatenate((zero, zero, np.kron(wdiag, stiff)), 0),
    )
    return np.stack(fwd), np.stack(adj), np.kron(weights, weights)


def step_kernel(
    groups,
    slabs,
    state_ref, adj_ref, obs_ref, spacing_h, slot_h, synth_ref, anal_ref, fwd_ref, bwd_ref, w2_ref,
    next_o, start_o,
    spacing_ref, slot_ref, state_v, adj_v, obs_v, synth_v, anal_v, fwd_v, bwd_v, w2_v,
    send_v, state_r, forcing_r, next_r, start_r, quad_v, scale_v, mult_v,
    even_v, odd_v, prod_v, modal_v, num_v, psi_v, cot_v, spread_v, pcot_v,
    edge_send, edge_recv, stage_v, full_v, mass_send, mass_recv,
    load_sem, send_sem, recv_sem, esend_sem, erecv_sem, msend_sem, mrecv_sem,
):
    member = lax.axis_index("modes")
    slab = lax.axis_index("elems")
    low_slab = lax.rem(slab + slabs - 1, slabs)
    high_slab = lax.rem(slab + 1, slabs)
    partners = (lax.rem(member + 2, 4), 3 - member, member + 1 - 2 * lax.rem(member, 2))
    modes = groups * 128
    recv = (state_r, forcing_r, next_r, start_r)

    loads = [
        pltpu.make_async_copy(src, dst, load_sem.at[i])
        for i, (src, dst) in enumerate(
            [(slot_h, slot_ref), (spacing_h, spacing_ref)]
            + [(state_ref.at[j], state_v.at[j]) for j in range(ROWS)]
            + [
                (adj_ref, adj_v), (obs_ref, obs_v), (w2_ref, w2_v),
                (fwd_ref, fwd_v), (synth_ref, synth_v), (anal_ref, anal_v), (bwd_ref, bwd_v),
            ]
        )
    ]
    adj_load, obs_load, w2_load, fwd_load, synth_load, anal_load, bwd_load = loads[2 + ROWS :]
    for load in loads:
        load.start()

    barrier = pltpu.get_barrier_semaphore()
    for partner in partners:
        pl.semaphore_signal(barrier, inc=1, device_id={"modes": partner}, device_id_type=MESH)

    place = lax.rem(slab, 2 * CHIP_ROW)
    early_low = place == 0
    early_high = place == CHIP_ROW - 1
    across_low = jnp.logical_or(early_low, place == CHIP_ROW)
    across_high = jnp.logical_or(early_high, place == 2 * CHIP_ROW - 1)
    early = jnp.logical_or(early_low, early_high)
    greet_low_now = jnp.logical_not(across_low)
    greet_high_now = jnp.logical_not(across_high)

    mirrored = place >= CHIP_ROW

    def flip(index):
        return jnp.where(mirrored, ROWS - 1 - index, index)

    row_here = flip(member)

    def around(way):
        across = (across_high, across_low)[way]
        return {
            "modes": jnp.where(across, ROWS - 1 - member, member),
            "elems": (high_slab, low_slab)[way],
        }

    def greet(way):
        pl.semaphore_signal(barrier, inc=1, device_id=around(way), device_id_type=MESH)

    @pl.when(greet_low_now)
    def _():
        greet(1)

    @pl.when(greet_high_now)
    def _():
        greet(0)

    loads[0].wait()
    loads[1].wait()
    slots = [slot_ref[0, j] for j in range(ROWS)]

    def rows_of(index, count=NODES):
        return pl.ds(index * count, count)

    def flat(block):
        return block.reshape(6 * NODES, 128)

    def elem_of(row):
        place = jnp.int32(0)
        for j in range(1, ROWS):
            place = jnp.where(slots[j] == row, j, place)
        return place

    part = NODES // 2
    halves = ((0, 6 * part), (6 * part, 12 * part))
    inner = NODES - 2 * GLL
    edges = 12 * GLL
    spare = 4
    kept = 6 * inner - spare * GLL
    phases = (
        (0,) + halves[0],
        (1, 0, edges + inner), (1, edges + inner, 6 * NODES),
        (2, 0, kept), (2, kept, kept + 6 * GLL),
        (3,) + halves[0],
        (2, kept + 6 * GLL, kept + 12 * GLL),
        (0,) + halves[1],
        (3,) + halves[1],
    )

    def unpack(block, i):
        sides = block[i * 2 * GLL : (i + 1) * 2 * GLL]
        middle = block[edges + i * inner : edges + (i + 1) * inner]
        return jnp.concatenate([sides[:GLL], middle, sides[GLL:]], axis=0)

    def swap(phase, partner, arrival=False):
        which, begin, end = phases[phase]
        rows = pl.ds(begin, end - begin)
        slot = partner if arrival else member
        return pltpu.make_async_remote_copy(
            src_ref=send_v.at[which, partner, rows],
            dst_ref=recv[which].at[slot, rows],
            send_sem=send_sem.at[phase, partner],
            recv_sem=recv_sem.at[phase, slot],
            device_id={"modes": partner},
            device_id_type=MESH,
        )

    def start(phase):
        for partner in partners:
            swap(phase, partner).start()

    def sent(phase):
        for partner in partners:
            swap(phase, partner).wait_send()

    def arrived(phase):
        for partner in partners:
            swap(phase, partner, arrival=True).wait_recv()

    for load in loads[2 : 2 + ROWS]:
        load.wait()
    for device in range(ROWS):
        block = flat(state_v[elem_of(flip(device))]).astype(LOW)
        for h in range(2):
            for i in range(6):
                begin = i * NODES + h * part
                send_v[0, device, rows_of(6 * h + i, part), :] = block[begin : begin + part]

    @pl.when(early)
    def _():
        pl.semaphore_wait(barrier, 4)

    @pl.when(jnp.logical_not(early))
    def _():
        pl.semaphore_wait(barrier, 5)

    @pl.when(jnp.logical_not(greet_low_now))
    def _():
        greet(1)

    @pl.when(jnp.logical_not(greet_high_now))
    def _():
        greet(0)

    start(0)
    start(7)
    state_r[member] = send_v[0, member]

    w2_load.wait()
    own = elem_of(row_here)
    row_above = jnp.minimum(row_here + 1, ROWS - 1)
    row_below = jnp.maximum(row_here - 1, 0)
    above = elem_of(row_above)
    below = elem_of(row_below)

    def area(elem):
        return spacing_ref[0, elem] * spacing_ref[1, elem] * 0.25

    side_x = spacing_ref[0, own]
    side_y = spacing_ref[1, own]
    full = (NODES, 128)
    layer = lax.rem(lax.broadcasted_iota(jnp.int32, full, 0), GLL)
    has_above = jnp.logical_and(layer == GLL - 1, row_here < ROWS - 1)
    has_below = jnp.logical_and(layer == 0, row_here > 0)
    w2 = w2_v[...]
    quad = w2 * area(own)
    quad_v[...] = quad
    mass = quad + jnp.where(has_above, w2 * area(above), 0.0)
    mass = mass + jnp.where(has_below, w2 * area(below), 0.0)
    at_wall = jnp.logical_and(layer == 0, row_here == 0)
    keep = jnp.where(at_wall, 0.0, 1.0)
    scale_v[...] = keep / mass
    mass_send[0] = mass[NODES - GLL :]
    mass_send[1] = mass[:GLL]

    def mass_copy(way):
        return pltpu.make_async_remote_copy(
            src_ref=mass_send.at[way],
            dst_ref=mass_recv.at[way],
            send_sem=msend_sem.at[way],
            recv_sem=mrecv_sem.at[way],
            device_id=around(way),
            device_id_type=MESH,
        )

    copies = jnp.where(jnp.logical_or(has_above, has_below), 2.0, 1.0).astype(F32)
    node_a = lax.broadcasted_iota(jnp.int32, full, 0) // GLL
    mult_v[...] = jnp.where(jnp.logical_or(node_a == 0, node_a == GLL - 1), 2.0 * copies, copies)

    edge_rows = 6 * GLL * groups
    top = pl.ds(GLL - 1, edge_rows, stride=GLL)
    low = pl.ds(0, edge_rows, stride=GLL)

    def edge_copy(which, way):
        if way == 0:
            target = {"modes": flip(row_above)}
        elif way == 1:
            target = {"modes": flip(row_below)}
        else:
            target = around(way - 2)
        return pltpu.make_async_remote_copy(
            src_ref=edge_send.at[which, way],
            dst_ref=edge_recv.at[which, way],
            send_sem=esend_sem.at[which, way],
            recv_sem=erecv_sem.at[which, way],
            device_id=target,
            device_id_type=MESH,
        )

    def pack_around(which, buf):
        for way, begin in ((2, NODES - GLL), (3, 0)):
            edge_send[which, way] = jnp.concatenate(
                [buf[pl.ds(i * NODES + begin, GLL), :] for i in range(6 * groups)], axis=0
            ).astype(LOW)

    def add_around(which, buf):
        for way, begin in ((2, 0), (3, NODES - GLL)):
            edge_copy(which, way).wait_recv()
            came = edge_recv[which, way].astype(F32)
            for i in range(6 * groups):
                rows = pl.ds(i * NODES + begin, GLL)
                buf[rows, :] = buf[rows, :] + came[i * GLL : (i + 1) * GLL]

    def around_sent(which):
        for way in (2, 3):
            edge_copy(which, way).wait_send()

    adj_load.wait()
    obs_load.wait()
    for row in range(ROWS):
        elem = elem_of(row)
        psi_v[rows_of(row, 6 * NODES), :] = flat(adj_v[elem] - obs_v[elem].astype(F32))
    for row in range(ROWS - 1):
        lower = pl.ds(row * 6 * NODES + GLL - 1, 6 * GLL, stride=GLL)
        upper = pl.ds((row + 1) * 6 * NODES, 6 * GLL, stride=GLL)
        both = psi_v[lower, :] + psi_v[upper, :]
        psi_v[lower, :] = both
        psi_v[upper, :] = both
    for row in range(ROWS):
        device = flip(row)
        for i in range(6):
            base = (6 * row + i) * NODES
            send_v[1, device, pl.ds(i * 2 * GLL, 2 * GLL), :] = jnp.concatenate(
                [psi_v[pl.ds(base, GLL), :], psi_v[pl.ds(base + NODES - GLL, GLL), :]], axis=0
            ).astype(LOW)
            send_v[1, device, pl.ds(edges + i * inner, inner), :] = psi_v[
                pl.ds(base + GLL, inner), :
            ].astype(LOW)
    forcing_r[member] = send_v[1, member]
    fwd_load.wait()
    bwd_load.wait()
    lane = lax.broadcasted_iota(jnp.int32, (NODES, 3 * NODES), 1)
    ratio = jnp.full((NODES, 3 * NODES), side_y) / jnp.full((NODES, 3 * NODES), side_x)
    coef = jnp.where(
        lane < NODES, 0.5 * side_y, jnp.where(lane < 2 * NODES, 0.5 * side_x, -viscosity * ratio)
    )
    fwd_mat = (time_step * (fwd_v[0] * coef - fwd_v[1] * (viscosity / ratio))).astype(LOW)
    line = lax.broadcasted_iota(jnp.int32, (3 * NODES, NODES), 0)
    ratio = jnp.full((3 * NODES, NODES), side_y) / jnp.full((3 * NODES, NODES), side_x)
    coef = jnp.where(
        line < NODES, 0.5 * side_y, jnp.where(line < 2 * NODES, 0.5 * side_x, -viscosity * ratio)
    )
    bwd_mat = (bwd_v[0] * coef - bwd_v[1] * (viscosity / ratio)).astype(LOW)

    def state_part(h, i):
        rows = rows_of(6 * h + i, part)
        return jnp.concatenate([state_r[q, rows, :] for q in range(groups)], axis=1)

    def wide(block):
        return jnp.concatenate([block] * groups, axis=1)

    def field(buf, i):
        return jnp.concatenate([buf[rows_of(6 * q + i), :] for q in range(groups)], axis=1)

    def set_field(buf, i, value):
        for q in range(groups):
            buf[rows_of(6 * q + i), :] = value[:, q * 128 : (q + 1) * 128]

    mode_ids = lax.broadcasted_iota(jnp.int32, (NODES, modes), 1)
    wave = mode_ids.astype(F32) * (wave_scale / modes)

    synth_load.wait()
    anal_load.wait()

    def half_rows(index, h):
        return pl.ds(index * NODES + h * part, part)

    for h in range(2):
        if h == 0:
            arrived(0)
        else:
            sent(0)
            sent(7)
            start(1)
            arrived(7)
        for p, planes in ((0, even_v), (1, odd_v)):
            values = jnp.dot(
                jnp.concatenate([state_part(h, 2 * c + p) for c in range(3)], axis=0),
                synth_v[p],
                preferred_element_type=F32,
            )
            for c in range(3):
                planes[half_rows(c, h), :] = values[c * part : (c + 1) * part]
        for q, (left, right) in enumerate(pair_order):
            el, ol = even_v[half_rows(left, h), :], odd_v[half_rows(left, h), :]
            er, orr = even_v[half_rows(right, h), :], odd_v[half_rows(right, h), :]
            prod_v[0, rows_of(6 * h + q, part), :] = (el * er + ol * orr).astype(LOW)
            prod_v[1, rows_of(6 * h + q, part), :] = (el * orr + ol * er).astype(LOW)
        for p in range(2):
            values = jnp.dot(
                prod_v[p, rows_of(h, 6 * part), :], anal_v[p], preferred_element_type=F32
            ).astype(LOW)
            for q in range(6):
                modal_v[p, half_rows(q, h), :] = values[q * part : (q + 1) * part]

    for c in range(3):
        for p in range(2):
            values = jnp.concatenate([state_part(h, 2 * c + p) for h in range(2)], axis=0)
            stack = jnp.concatenate(
                [
                    modal_v[p, rows_of(pair_index[0][c]), :],
                    modal_v[p, rows_of(pair_index[1][c]), :],
                    values,
                ],
                axis=0,
            )
            flux_z = modal_v[1 - p, rows_of(pair_index[2][c]), :].astype(F32)
            turn = (-time_step if p == 1 else time_step) * wave
            local = (1.0 - time_step * viscosity * wave * wave) * values.astype(F32)
            set_field(
                num_v,
                2 * c + p,
                jnp.dot(fwd_mat, stack, preferred_element_type=F32)
                + wide(quad_v[...]) * (local + turn * flux_z),
            )

    @pl.when(row_here < ROWS - 1)
    def _():
        edge_send[1, 0] = num_v[top, :].astype(LOW)
        edge_copy(1, 0).start()

    @pl.when(row_here > 0)
    def _():
        edge_send[1, 1] = num_v[low, :].astype(LOW)
        edge_copy(1, 1).start()

    start(2)

    @pl.when(early)
    def _():
        pl.semaphore_wait(barrier, 1)

    mass_copy(0).start()
    mass_copy(1).start()
    arrived(1)
    for q in range(groups):
        block = forcing_r[q, pl.ds(0, edges), :].astype(F32)
        for way, begin in ((2, GLL), (3, 0)):
            edge_send[0, way, pl.ds(q * 6 * GLL, 6 * GLL), :] = jnp.concatenate(
                [block[i * 2 * GLL + begin : i * 2 * GLL + begin + GLL] for i in range(6)], axis=0
            ).astype(LOW)
    edge_copy(0, 2).start()
    edge_copy(0, 3).start()

    @pl.when(row_here > 0)
    def _():
        edge_copy(1, 0).wait_recv()
        num_v[low, :] = num_v[low, :] + edge_recv[1, 0].astype(F32)

    @pl.when(row_here < ROWS - 1)
    def _():
        edge_copy(1, 1).wait_recv()
        num_v[top, :] = num_v[top, :] + edge_recv[1, 1].astype(F32)

    pack_around(1, num_v)
    edge_copy(1, 2).start()
    edge_copy(1, 3).start()
    for q in range(groups):
        for i in range(6):
            rows = pl.ds((6 * q + i) * NODES + GLL, inner)
            value = scale_v[GLL : NODES - GLL, :] * num_v[rows, :]
            num_v[rows, :] = value
            if i < 5:
                stage_v[q, pl.ds(i * inner, inner), :] = value
            else:
                stage_v[q, pl.ds(i * inner, inner - spare * GLL), :] = value[: inner - spare * GLL]
                for k in range(spare):
                    tile = value[inner - (spare - k) * GLL : inner - (spare - k - 1) * GLL]
                    stage_v[q, pl.ds(k * GLL * GLL, GLL, stride=GLL), :] = tile
        send_v[2, q, pl.ds(0, kept), :] = stage_v[q].astype(LOW)
    next_r[member, pl.ds(0, kept), :] = send_v[2, member, pl.ds(0, kept), :]
    sent(1)
    sent(2)
    start(3)
    mass_copy(0).wait()
    mass_copy(1).wait()
    scale_v[:GLL, :] = keep[:GLL] / (mass_send[1] + mass_recv[0])
    scale_v[NODES - GLL :, :] = keep[NODES - GLL :] / (mass_send[0] + mass_recv[1])
    add_around(1, num_v)
    for q in range(groups):
        for i in range(6):
            base = (6 * q + i) * NODES
            low_edge = scale_v[:GLL, :] * num_v[pl.ds(base, GLL), :]
            num_v[pl.ds(base, GLL), :] = low_edge
            high_edge = scale_v[NODES - GLL :, :] * num_v[pl.ds(base + NODES - GLL, GLL), :]
            num_v[pl.ds(base + NODES - GLL, GLL), :] = high_edge
            stage_v[q, pl.ds(i * GLL, GLL), :] = low_edge
            stage_v[q, pl.ds((6 + i) * GLL, GLL), :] = high_edge
        send_v[2, q, pl.ds(kept, 12 * GLL), :] = stage_v[q, pl.ds(0, 12 * GLL), :].astype(LOW)
    next_r[member, pl.ds(kept, 12 * GLL), :] = send_v[2, member, pl.ds(kept, 12 * GLL), :]
    start(4)

    @pl.when(across_high)
    def _():
        start(6)

    arrived(2)
    for q in range(groups):
        block = forcing_r[q].astype(F32)
        for i in range(6):
            rows = rows_of(6 * q + i)
            psi_v[rows, :] = unpack(block, i)
    add_around(0, psi_v)
    for i in range(6 * groups):
        rows = rows_of(i)
        psi_v[rows, :] = scale_v[...] * (psi_v[rows, :] + mult_v[...] * num_v[rows, :])

    norm = jnp.where(mode_ids == 0, 1.0 / (3.0 * modes), 0.5 / (3.0 * modes)).astype(F32)
    for p in range(2):
        lateral = []
        for c in range(3):
            psi = field(psi_v, 2 * c + p)
            other = field(psi_v, 2 * c + 1 - p)
            grads = jnp.dot(bwd_mat, psi.astype(LOW), preferred_element_type=F32)
            set_field(
                num_v,
                2 * c + p,
                wide(quad_v[...]) * ((1.0 - time_step * viscosity * wave * wave) * psi)
                + time_step * grads[2 * NODES :],
            )
            turn = -wave if p == 0 else wave
            lateral.append((grads[:NODES], grads[NODES : 2 * NODES], wide(quad_v[...]) * (turn * other)))
        for q, (left, right) in enumerate(pair_order):
            cot = lateral[right][left] + lateral[left][right]
            cot = (norm * cot).astype(LOW)
            for h in range(2):
                cot_v[p, rows_of(6 * h + q, part), :] = cot[h * part : (h + 1) * part]

    gain = jnp.where(mode_ids == 0, 3.0 * modes * time_step, 6.0 * modes * time_step).astype(F32)
    gain = gain[:part]
    for h in range(2):
        for p in range(2):
            spread_v[p] = jnp.dot(
                cot_v[p, rows_of(h, 6 * part), :], synth_v[p], preferred_element_type=F32
            )
        for c in range(3):
            even = jnp.zeros((part, even_v.shape[1]), F32)
            odd = jnp.zeros((part, even_v.shape[1]), F32)
            for d in range(3):
                se = spread_v[0, rows_of(pair_index[c][d], part), :]
                so = spread_v[1, rows_of(pair_index[c][d], part), :]
                ed, od = even_v[half_rows(d, h), :], odd_v[half_rows(d, h), :]
                even = even + (se * ed + so * od)
                odd = odd + (se * od + so * ed)
            pcot_v[0, rows_of(c, part), :] = even.astype(LOW)
            pcot_v[1, rows_of(c, part), :] = odd.astype(LOW)
        for p in range(2):
            back = jnp.dot(pcot_v[p], anal_v[p], preferred_element_type=F32)
            for c in range(3):
                i = 2 * c + p
                near = gain * back[c * part : (c + 1) * part]
                for q in range(groups):
                    rest = num_v[half_rows(6 * q + i, h), :]
                    send_v[3, q, rows_of(6 * h + i, part), :] = (
                        rest + near[:, q * 128 : (q + 1) * 128]
                    ).astype(LOW)
        if h == 0:
            sent(3)
            sent(4)

            @pl.when(across_high)
            def _():
                sent(6)

        start((5, 8)[h])
    start_r[member] = send_v[3, member]

    around_sent(0)
    around_sent(1)

    @pl.when(row_here < ROWS - 1)
    def _():
        edge_copy(1, 0).wait_send()

    @pl.when(row_here > 0)
    def _():
        edge_copy(1, 1).wait_send()

    arrived(3)
    arrived(4)
    for row in range(ROWS):
        edge_send[0, 0, pl.ds(row * 6 * GLL, 6 * GLL), :] = next_r[
            flip(row), pl.ds(kept, 6 * GLL), :
        ]
    side_copy = pltpu.make_async_remote_copy(
        src_ref=edge_send.at[0, 0],
        dst_ref=edge_recv.at[0, 0],
        send_sem=esend_sem.at[0, 0],
        recv_sem=erecv_sem.at[0, 0],
        device_id={"elems": low_slab},
        device_id_type=MESH,
    )

    @pl.when(jnp.logical_not(across_low))
    def _():
        side_copy.start()

    for row in range(ROWS):
        block = next_r[flip(row), pl.ds(0, kept + 6 * GLL), :].astype(F32)
        stage_v[row] = block[:kept]
        for i in range(6):
            full_v[row, pl.ds(i * NODES, GLL), :] = block[kept + i * GLL : kept + (i + 1) * GLL]
            count = inner if i < 5 else inner - spare * GLL
            full_v[row, pl.ds(i * NODES + GLL, count), :] = block[i * inner : i * inner + count]
        for k in range(spare):
            tile = stage_v[row, pl.ds(k * GLL * GLL, GLL, stride=GLL), :]
            full_v[row, pl.ds(6 * NODES - (spare - k + 1) * GLL, GLL), :] = tile

    @pl.when(jnp.logical_not(across_low))
    def _():
        side_copy.wait_send()

    @pl.when(jnp.logical_not(across_high))
    def _():
        side_copy.wait_recv()

    @pl.when(across_high)
    def _():
        arrived(6)
        for row in range(ROWS):
            edge_recv[0, 0, pl.ds(row * 6 * GLL, 6 * GLL), :] = next_r[
                flip(row), pl.ds(kept + 6 * GLL, 6 * GLL), :
            ]

    for row in range(ROWS):
        side = edge_recv[0, 0, pl.ds(row * 6 * GLL, 6 * GLL), :].astype(F32)
        for i in range(6):
            full_v[row, pl.ds((i + 1) * NODES - GLL, GLL), :] = side[i * GLL : (i + 1) * GLL]
        if row == 0:
            shared = jnp.zeros((6 * GLL, 128), F32)
        else:
            shared = full_v[row - 1, pl.ds(GLL - 1, 6 * GLL, stride=GLL), :]
        full_v[row, pl.ds(0, 6 * GLL, stride=GLL), :] = shared
    for j in range(ROWS):
        next_o[j] = full_v[slots[j]].reshape(3, 2, NODES, 128)
    arrived(5)
    arrived(8)
    for j in range(ROWS):
        block = start_r[flip(slots[j])].astype(F32)
        for h in range(2):
            for i in range(6):
                begin = (6 * h + i) * part
                start_o[j, i // 2, i % 2, rows_of(h, part), :] = block[begin : begin + part]
    sent(5)
    sent(8)


def store_kernel(next_v, start_v, next_ref, start_ref, sem):
    stores = [
        pltpu.make_async_copy(source.at[j], target.at[j], sem.at[which, j])
        for which, (source, target) in enumerate(((next_v, next_ref), (start_v, start_ref)))
        for j in range(ROWS)
    ]
    for store in stores:
        store.start()
    for store in stores:
        store.wait()


def on_device(state, adjoint_end, observed, spacing, radial_slot):
    groups = lax.axis_size("modes")
    slabs = lax.axis_size("elems")
    modes = groups * state.shape[4]
    half = 3 * modes // 2
    synth, analysis = half_tables(modes, 3 * modes)
    fwd, bwd, w2 = node_tables()
    any_spec = pl.BlockSpec(memory_space=pltpu.HBM)
    vmem_spec = pl.BlockSpec(memory_space=pltpu.VMEM)
    local = state.shape
    block = (6 * NODES, 128)
    vm = pltpu.VMEM
    sem = pltpu.SemaphoreType.DMA

    def run(*args):
        step_kernel(groups, slabs, *args)

    held_out = pltpu.VMEM(local, F32)

    def held(array):
        return pltpu.with_memory_space_constraint(array, pltpu.HBM)

    next_v, start_v = pl.pallas_call(
        run,
        out_shape=(held_out, held_out),
        in_specs=[any_spec] * 10,
        out_specs=(vmem_spec, vmem_spec),
        scratch_shapes=[
            pltpu.SMEM((2, ROWS), F32), pltpu.SMEM((1, ROWS), jnp.int32),
            vm(local, F32), vm(local, F32), vm(local, LOW),
            vm((2, modes, half), LOW), vm((2, half, modes), LOW),
            vm((2, NODES, 3 * NODES), F32), vm((2, 3 * NODES, NODES), F32), vm((NODES, 128), F32),
            vm((4, ROWS) + block, LOW), *[vm((ROWS,) + block, LOW)] * 4,
            vm((NODES, 128), F32), vm((NODES, 128), F32), vm((NODES, 128), F32),
            vm((3 * NODES, half), F32), vm((3 * NODES, half), F32),
            vm((2, 6 * NODES, half), LOW), vm((2, 6 * NODES, modes), LOW),
            vm((6 * NODES * groups, 128), F32), vm((6 * NODES * groups, 128), F32),
            vm((2, 6 * NODES, modes), LOW), vm((2, 3 * NODES, half), F32),
            vm((2, 3 * NODES // 2, half), LOW),
            vm((2, 4, 6 * GLL * groups, 128), LOW), vm((2, 4, 6 * GLL * groups, 128), LOW),
            vm((ROWS, 256, 128), F32), vm((ROWS,) + block, F32),
            vm((2, GLL, 128), F32), vm((2, GLL, 128), F32),
            sem((9 + ROWS,)), sem((9, ROWS)), sem((9, ROWS)), sem((2, 4)), sem((2, 4)),
            sem((2,)), sem((2,)),
        ],
        compiler_params=pltpu.CompilerParams(
            collective_id=0, has_side_effects=True, vmem_limit_bytes=48 * 1024 * 1024
        ),
        cost_estimate=pl.CostEstimate(
            flops=1900000000, bytes_accessed=7000000, transcendentals=0
        ),
    )(
        held(state), held(adjoint_end), held(observed), held(spacing.T), held(radial_slot),
        held(jnp.asarray(synth, F32).astype(LOW)), held(jnp.asarray(analysis, F32).astype(LOW)),
        held(jnp.asarray(fwd, F32)), held(jnp.asarray(bwd, F32)),
        held(jnp.asarray(np.broadcast_to(w2[:, None], (NODES, 128)), F32)),
    )
    return pl.pallas_call(
        store_kernel,
        out_shape=(jax.ShapeDtypeStruct(local, F32), jax.ShapeDtypeStruct(local, F32)),
        in_specs=[pl.BlockSpec(memory_space=pl.ANY)] * 2,
        out_specs=(any_spec, any_spec),
        scratch_shapes=[sem((2, ROWS))],
        compiler_params=pltpu.CompilerParams(vmem_limit_bytes=1024 * 1024),
    )(next_v, start_v)


def solution(mesh):
    in_specs = (
        P("elems", None, None, None, "modes"),
        P("elems", None, None, None, "modes"),
        P("elems", None, None, None, "modes"),
        P("elems", None),
        P("elems", None),
    )
    out_specs = (P("elems", None, None, None, "modes"), P("elems", None, None, None, "modes"))
    return jax.shard_map(
        on_device, mesh=mesh, in_specs=in_specs, out_specs=out_specs, check_vma=False
    )
```

```python
import jax
import jax.numpy as jnp
import numpy as np
from jax import lax
from jax.experimental import pallas as pl
from jax.experimental.pallas import tpu as pltpu
from jax.sharding import PartitionSpec as P

GLL = 8
NODES = GLL * GLL
ROWS = 4
CHIP_ROW = 8
time_step = 0.01
viscosity = 0.05
wave_scale = 4.0
pair_order = ((0, 0), (0, 1), (0, 2), (1, 1), (1, 2), (2, 2))
pair_index = ((0, 1, 2), (1, 3, 4), (2, 4, 5))
F32 = jnp.float32
LOW = jnp.bfloat16
MESH = pl.DeviceIdType.MESH


def legendre_table(points, quad_count):
    columns = [points * 0.0 + 1.0, points]
    for degree in range(2, quad_count):
        columns.append(
            ((2 * degree - 1) * points * columns[-1] - (degree - 1) * columns[-2]) / degree
        )
    return np.stack(columns, axis=1)


def gll_tables(quad_count):
    degree = quad_count - 1
    points = -np.cos(np.pi * np.arange(quad_count) / degree)
    for repeat in range(60):
        vander = legendre_table(points, quad_count)
        points = points - (points * vander[:, degree] - vander[:, degree - 1]) / (
            quad_count * vander[:, degree]
        )
    vander = legendre_table(points, quad_count)
    edge_value = vander[:, degree]
    weights = 2.0 / (degree * quad_count * edge_value * edge_value)
    diagonal_mask = np.arange(quad_count)[:, None] == np.arange(quad_count)[None, :]
    differ = np.where(diagonal_mask, 1.0, points[:, None] - points[None, :])
    derivative = np.where(diagonal_mask, 0.0, edge_value[:, None] / (edge_value[None, :] * differ))
    derivative[0, 0] = -degree * quad_count / 4.0
    derivative[degree, degree] = degree * quad_count / 4.0
    return (weights, derivative)


def half_tables(modes, planes):
    half = planes // 2
    turns = np.outer(np.arange(modes), 2 * np.arange(half) + 1) % (2 * planes)
    angles = np.pi * turns / planes
    factor = np.where(np.arange(modes) == 0, 1.0, 2.0)[:, None]
    synth = np.stack((factor * np.cos(angles), -factor * np.sin(angles)))
    analysis = np.stack((np.cos(angles), -np.sin(angles))) * (2.0 / planes)
    return synth, np.transpose(analysis, (0, 2, 1))


def node_tables():
    weights, deriv = gll_tables(GLL)
    wdiag = np.diag(weights)
    back = deriv.T @ wdiag
    ahead = wdiag @ deriv
    stiff = deriv.T @ wdiag @ deriv
    zero = np.zeros((NODES, NODES))
    fwd = (
        np.concatenate((np.kron(back, wdiag), np.kron(wdiag, back), np.kron(stiff, wdiag)), 1),
        np.concatenate((zero, zero, np.kron(wdiag, stiff)), 1),
    )
    adj = (
        np.concatenate((np.kron(ahead, wdiag), np.kron(wdiag, ahead), np.kron(stiff, wdiag)), 0),
        np.concatenate((zero, zero, np.kron(wdiag, stiff)), 0),
    )
    return np.stack(fwd), np.stack(adj), np.kron(weights, weights)


def step_kernel(
    groups,
    slabs,
    state_ref, adj_ref, obs_ref, spacing_h, slot_h, synth_ref, anal_ref, fwd_ref, bwd_ref, w2_ref,
    next_o, start_o,
    spacing_ref, slot_ref, state_v, adj_v, obs_v, synth_v, anal_v, fwd_v, bwd_v, w2_v,
    send_v, state_r, forcing_r, next_r, start_r, quad_v, scale_v, mult_v,
    even_v, odd_v, prod_v, modal_v, num_v, psi_v, cot_v, spread_v, pcot_v,
    edge_send, edge_recv, stage_v, full_v, mass_send, mass_recv,
    load_sem, send_sem, recv_sem, esend_sem, erecv_sem, msend_sem, mrecv_sem,
):
    member = lax.axis_index("modes")
    slab = lax.axis_index("elems")
    low_slab = lax.rem(slab + slabs - 1, slabs)
    high_slab = lax.rem(slab + 1, slabs)
    partners = (lax.rem(member + 2, 4), 3 - member, member + 1 - 2 * lax.rem(member, 2))
    modes = groups * 128
    recv = (state_r, forcing_r, next_r, start_r)

    loads = [
        pltpu.make_async_copy(src, dst, load_sem.at[i])
        for i, (src, dst) in enumerate(
            [(slot_h, slot_ref), (spacing_h, spacing_ref)]
            + [(state_ref.at[j], state_v.at[j]) for j in range(ROWS)]
            + [
                (adj_ref, adj_v), (obs_ref, obs_v), (w2_ref, w2_v),
                (fwd_ref, fwd_v), (synth_ref, synth_v), (anal_ref, anal_v), (bwd_ref, bwd_v),
            ]
        )
    ]
    adj_load, obs_load, w2_load, fwd_load, synth_load, anal_load, bwd_load = loads[2 + ROWS :]
    for load in loads:
        load.start()

    barrier = pltpu.get_barrier_semaphore()
    for partner in partners:
        pl.semaphore_signal(barrier, inc=1, device_id={"modes": partner}, device_id_type=MESH)

    place = lax.rem(slab, 2 * CHIP_ROW)
    early_low = place == 0
    early_high = place == CHIP_ROW - 1
    across_low = jnp.logical_or(early_low, place == CHIP_ROW)
    across_high = jnp.logical_or(early_high, place == 2 * CHIP_ROW - 1)
    early = jnp.logical_or(early_low, early_high)
    greet_low_now = jnp.logical_not(across_low)
    greet_high_now = jnp.logical_not(across_high)

    mirrored = place >= CHIP_ROW

    def flip(index):
        return jnp.where(mirrored, ROWS - 1 - index, index)

    row_here = flip(member)

    def around(way):
        across = (across_high, across_low)[way]
        return {
            "modes": jnp.where(across, ROWS - 1 - member, member),
            "elems": (high_slab, low_slab)[way],
        }

    def greet(way):
        pl.semaphore_signal(barrier, inc=1, device_id=around(way), device_id_type=MESH)

    @pl.when(greet_low_now)
    def _():
        greet(1)

    @pl.when(greet_high_now)
    def _():
        greet(0)

    loads[0].wait()
    loads[1].wait()
    slots = [slot_ref[0, j] for j in range(ROWS)]

    def rows_of(index, count=NODES):
        return pl.ds(index * count, count)

    def flat(block):
        return block.reshape(6 * NODES, 128)

    def elem_of(row):
        place = jnp.int32(0)
        for j in range(1, ROWS):
            place = jnp.where(slots[j] == row, j, place)
        return place

    part = NODES // 2
    halves = ((0, 6 * part), (6 * part, 12 * part))
    inner = NODES - 2 * GLL
    edges = 6 * GLL
    far = edges + 6 * inner
    spare = 4
    kept = 6 * inner - spare * GLL
    phases = (
        (0,) + halves[0],
        (1, 0, edges), (1, edges, far),
        (2, 0, kept), (2, kept, kept + 6 * GLL),
        (3,) + halves[0],
        (2, kept + 6 * GLL, kept + 12 * GLL),
        (0,) + halves[1],
        (3,) + halves[1],
        (1, far, 6 * NODES),
    )

    def swap(phase, partner, arrival=False):
        which, begin, end = phases[phase]
        rows = pl.ds(begin, end - begin)
        slot = partner if arrival else member
        return pltpu.make_async_remote_copy(
            src_ref=send_v.at[which, partner, rows],
            dst_ref=recv[which].at[slot, rows],
            send_sem=send_sem.at[phase, partner],
            recv_sem=recv_sem.at[phase, slot],
            device_id={"modes": partner},
            device_id_type=MESH,
        )

    def start(phase):
        for partner in partners:
            swap(phase, partner).start()

    def sent(phase):
        for partner in partners:
            swap(phase, partner).wait_send()

    def arrived(phase):
        for partner in partners:
            swap(phase, partner, arrival=True).wait_recv()

    for load in loads[2 : 2 + ROWS]:
        load.wait()
    for device in range(ROWS):
        block = flat(state_v[elem_of(flip(device))]).astype(LOW)
        for h in range(2):
            for i in range(6):
                begin = i * NODES + h * part
                send_v[0, device, rows_of(6 * h + i, part), :] = block[begin : begin + part]

    @pl.when(early)
    def _():
        pl.semaphore_wait(barrier, 4)

    @pl.when(jnp.logical_not(early))
    def _():
        pl.semaphore_wait(barrier, 5)

    @pl.when(jnp.logical_not(greet_low_now))
    def _():
        greet(1)

    @pl.when(jnp.logical_not(greet_high_now))
    def _():
        greet(0)

    start(0)
    start(7)
    state_r[member] = send_v[0, member]

    w2_load.wait()
    own = elem_of(row_here)
    row_above = jnp.minimum(row_here + 1, ROWS - 1)
    row_below = jnp.maximum(row_here - 1, 0)
    above = elem_of(row_above)
    below = elem_of(row_below)

    def area(elem):
        return spacing_ref[0, elem] * spacing_ref[1, elem] * 0.25

    side_x = spacing_ref[0, own]
    side_y = spacing_ref[1, own]
    full = (NODES, 128)
    layer = lax.rem(lax.broadcasted_iota(jnp.int32, full, 0), GLL)
    has_above = jnp.logical_and(layer == GLL - 1, row_here < ROWS - 1)
    has_below = jnp.logical_and(layer == 0, row_here > 0)
    w2 = w2_v[...]
    quad = w2 * area(own)
    quad_v[...] = quad
    mass = quad + jnp.where(has_above, w2 * area(above), 0.0)
    mass = mass + jnp.where(has_below, w2 * area(below), 0.0)
    at_wall = jnp.logical_and(layer == 0, row_here == 0)
    keep = jnp.where(at_wall, 0.0, 1.0)
    scale_v[...] = keep / mass
    mass_send[0] = mass[NODES - GLL :]
    mass_send[1] = mass[:GLL]

    def mass_copy(way):
        return pltpu.make_async_remote_copy(
            src_ref=mass_send.at[way],
            dst_ref=mass_recv.at[way],
            send_sem=msend_sem.at[way],
            recv_sem=mrecv_sem.at[way],
            device_id=around(way),
            device_id_type=MESH,
        )

    copies = jnp.where(jnp.logical_or(has_above, has_below), 2.0, 1.0).astype(F32)
    node_a = lax.broadcasted_iota(jnp.int32, full, 0) // GLL
    mult_v[...] = jnp.where(jnp.logical_or(node_a == 0, node_a == GLL - 1), 2.0 * copies, copies)

    edge_rows = 6 * GLL * groups
    top = pl.ds(GLL - 1, edge_rows, stride=GLL)
    low = pl.ds(0, edge_rows, stride=GLL)

    def edge_copy(which, way):
        if way == 0:
            target = {"modes": flip(row_above)}
        elif way == 1:
            target = {"modes": flip(row_below)}
        else:
            target = around(way - 2)
        return pltpu.make_async_remote_copy(
            src_ref=edge_send.at[which, way],
            dst_ref=edge_recv.at[which, way],
            send_sem=esend_sem.at[which, way],
            recv_sem=erecv_sem.at[which, way],
            device_id=target,
            device_id_type=MESH,
        )

    def pack_around(which, buf):
        for way, begin in ((2, NODES - GLL), (3, 0)):
            edge_send[which, way] = jnp.concatenate(
                [buf[pl.ds(i * NODES + begin, GLL), :] for i in range(6 * groups)], axis=0
            ).astype(LOW)

    def add_around(which, buf):
        for way, begin in ((2, 0), (3, NODES - GLL)):
            edge_copy(which, way).wait_recv()
            came = edge_recv[which, way].astype(F32)
            for i in range(6 * groups):
                rows = pl.ds(i * NODES + begin, GLL)
                buf[rows, :] = buf[rows, :] + came[i * GLL : (i + 1) * GLL]

    def around_sent(which):
        for way in (2, 3):
            edge_copy(which, way).wait_send()

    adj_load.wait()
    obs_load.wait()
    for row in range(ROWS):
        elem = elem_of(row)
        psi_v[rows_of(row, 6 * NODES), :] = flat(adj_v[elem] - obs_v[elem].astype(F32))
    for row in range(ROWS - 1):
        lower = pl.ds(row * 6 * NODES + GLL - 1, 6 * GLL, stride=GLL)
        upper = pl.ds((row + 1) * 6 * NODES, 6 * GLL, stride=GLL)
        both = psi_v[lower, :] + psi_v[upper, :]
        psi_v[lower, :] = both
        psi_v[upper, :] = both
    slab_edge = pltpu.make_async_remote_copy(
        src_ref=edge_send.at[0, 1],
        dst_ref=edge_recv.at[0, 1],
        send_sem=esend_sem.at[0, 1],
        recv_sem=erecv_sem.at[0, 1],
        device_id={"elems": high_slab},
        device_id_type=MESH,
    )
    edge_send[0, 1] = jnp.concatenate(
        [psi_v[pl.ds((i + 1) * NODES - GLL, GLL), :] for i in range(6 * ROWS)], axis=0
    ).astype(LOW)

    @pl.when(jnp.logical_not(across_high))
    def _():
        slab_edge.start()

    for row in range(ROWS):
        device = flip(row)
        for i in range(6):
            base = (6 * row + i) * NODES
            send_v[1, device, pl.ds(edges + i * inner, inner), :] = psi_v[
                pl.ds(base + GLL, inner), :
            ].astype(LOW)

    @pl.when(jnp.logical_not(across_low))
    def _():
        slab_edge.wait_recv()
        came = edge_recv[0, 1].astype(F32)
        for i in range(6 * ROWS):
            rows = pl.ds(i * NODES, GLL)
            psi_v[rows, :] = psi_v[rows, :] + came[i * GLL : (i + 1) * GLL]

    for row in range(ROWS):
        device = flip(row)
        for begin, offset in ((0, 0), (far, NODES - GLL)):
            send_v[1, device, pl.ds(begin, edges), :] = jnp.concatenate(
                [psi_v[pl.ds((6 * row + i) * NODES + offset, GLL), :] for i in range(6)], axis=0
            ).astype(LOW)
    forcing_r[member] = send_v[1, member]
    fwd_load.wait()
    bwd_load.wait()
    lane = lax.broadcasted_iota(jnp.int32, (NODES, 3 * NODES), 1)
    ratio = jnp.full((NODES, 3 * NODES), side_y) / jnp.full((NODES, 3 * NODES), side_x)
    coef = jnp.where(
        lane < NODES, 0.5 * side_y, jnp.where(lane < 2 * NODES, 0.5 * side_x, -viscosity * ratio)
    )
    fwd_mat = (time_step * (fwd_v[0] * coef - fwd_v[1] * (viscosity / ratio))).astype(LOW)
    line = lax.broadcasted_iota(jnp.int32, (3 * NODES, NODES), 0)
    ratio = jnp.full((3 * NODES, NODES), side_y) / jnp.full((3 * NODES, NODES), side_x)
    coef = jnp.where(
        line < NODES, 0.5 * side_y, jnp.where(line < 2 * NODES, 0.5 * side_x, -viscosity * ratio)
    )
    bwd_mat = (bwd_v[0] * coef - bwd_v[1] * (viscosity / ratio)).astype(LOW)

    def state_part(h, i):
        rows = rows_of(6 * h + i, part)
        return jnp.concatenate([state_r[q, rows, :] for q in range(groups)], axis=1)

    def wide(block):
        return jnp.concatenate([block] * groups, axis=1)

    def field(buf, i):
        return jnp.concatenate([buf[rows_of(6 * q + i), :] for q in range(groups)], axis=1)

    def set_field(buf, i, value):
        for q in range(groups):
            buf[rows_of(6 * q + i), :] = value[:, q * 128 : (q + 1) * 128]

    mode_ids = lax.broadcasted_iota(jnp.int32, (NODES, modes), 1)
    wave = mode_ids.astype(F32) * (wave_scale / modes)

    synth_load.wait()
    anal_load.wait()

    def half_rows(index, h):
        return pl.ds(index * NODES + h * part, part)

    for h in range(2):
        if h == 0:
            arrived(0)
        else:
            sent(0)
            sent(7)
            start(1)

            @pl.when(across_high)
            def _():
                start(9)

            arrived(7)
        for p, planes in ((0, even_v), (1, odd_v)):
            values = jnp.dot(
                jnp.concatenate([state_part(h, 2 * c + p) for c in range(3)], axis=0),
                synth_v[p],
                preferred_element_type=F32,
            )
            for c in range(3):
                planes[half_rows(c, h), :] = values[c * part : (c + 1) * part]
        for q, (left, right) in enumerate(pair_order):
            el, ol = even_v[half_rows(left, h), :], odd_v[half_rows(left, h), :]
            er, orr = even_v[half_rows(right, h), :], odd_v[half_rows(right, h), :]
            prod_v[0, rows_of(6 * h + q, part), :] = (el * er + ol * orr).astype(LOW)
            prod_v[1, rows_of(6 * h + q, part), :] = (el * orr + ol * er).astype(LOW)
        for p in range(2):
            values = jnp.dot(
                prod_v[p, rows_of(h, 6 * part), :], anal_v[p], preferred_element_type=F32
            ).astype(LOW)
            for q in range(6):
                modal_v[p, half_rows(q, h), :] = values[q * part : (q + 1) * part]

    for c in range(3):
        for p in range(2):
            values = jnp.concatenate([state_part(h, 2 * c + p) for h in range(2)], axis=0)
            stack = jnp.concatenate(
                [
                    modal_v[p, rows_of(pair_index[0][c]), :],
                    modal_v[p, rows_of(pair_index[1][c]), :],
                    values,
                ],
                axis=0,
            )
            flux_z = modal_v[1 - p, rows_of(pair_index[2][c]), :].astype(F32)
            turn = (-time_step if p == 1 else time_step) * wave
            local = (1.0 - time_step * viscosity * wave * wave) * values.astype(F32)
            set_field(
                num_v,
                2 * c + p,
                jnp.dot(fwd_mat, stack, preferred_element_type=F32)
                + wide(quad_v[...]) * (local + turn * flux_z),
            )

    @pl.when(row_here < ROWS - 1)
    def _():
        edge_send[1, 0] = num_v[top, :].astype(LOW)
        edge_copy(1, 0).start()

    @pl.when(row_here > 0)
    def _():
        edge_send[1, 1] = num_v[low, :].astype(LOW)
        edge_copy(1, 1).start()

    start(2)

    @pl.when(early)
    def _():
        pl.semaphore_wait(barrier, 1)

    mass_copy(0).start()
    mass_copy(1).start()
    arrived(1)
    for q in range(groups):
        edge_send[0, 3, pl.ds(q * edges, edges), :] = forcing_r[q, pl.ds(0, edges), :]
    edge_copy(0, 3).start()

    @pl.when(across_high)
    def _():
        arrived(9)
        for q in range(groups):
            edge_send[0, 2, pl.ds(q * edges, edges), :] = forcing_r[q, pl.ds(far, edges), :]
        edge_copy(0, 2).start()

    @pl.when(jnp.logical_not(across_high))
    def _():
        edge_send[0, 2] = jnp.zeros((edge_rows, 128), LOW)

    @pl.when(row_here > 0)
    def _():
        edge_copy(1, 0).wait_recv()
        num_v[low, :] = num_v[low, :] + edge_recv[1, 0].astype(F32)

    @pl.when(row_here < ROWS - 1)
    def _():
        edge_copy(1, 1).wait_recv()
        num_v[top, :] = num_v[top, :] + edge_recv[1, 1].astype(F32)

    pack_around(1, num_v)
    edge_copy(1, 2).start()
    edge_copy(1, 3).start()
    for q in range(groups):
        for i in range(6):
            rows = pl.ds((6 * q + i) * NODES + GLL, inner)
            value = scale_v[GLL : NODES - GLL, :] * num_v[rows, :]
            num_v[rows, :] = value
            if i < 5:
                stage_v[q, pl.ds(i * inner, inner), :] = value
            else:
                stage_v[q, pl.ds(i * inner, inner - spare * GLL), :] = value[: inner - spare * GLL]
                for k in range(spare):
                    tile = value[inner - (spare - k) * GLL : inner - (spare - k - 1) * GLL]
                    stage_v[q, pl.ds(k * GLL * GLL, GLL, stride=GLL), :] = tile
        send_v[2, q, pl.ds(0, kept), :] = stage_v[q].astype(LOW)
    next_r[member, pl.ds(0, kept), :] = send_v[2, member, pl.ds(0, kept), :]
    start(3)
    mass_copy(0).wait()
    mass_copy(1).wait()
    scale_v[:GLL, :] = keep[:GLL] / (mass_send[1] + mass_recv[0])
    scale_v[NODES - GLL :, :] = keep[NODES - GLL :] / (mass_send[0] + mass_recv[1])
    add_around(1, num_v)
    for q in range(groups):
        for i in range(6):
            base = (6 * q + i) * NODES
            low_edge = scale_v[:GLL, :] * num_v[pl.ds(base, GLL), :]
            num_v[pl.ds(base, GLL), :] = low_edge
            high_edge = scale_v[NODES - GLL :, :] * num_v[pl.ds(base + NODES - GLL, GLL), :]
            num_v[pl.ds(base + NODES - GLL, GLL), :] = high_edge
            stage_v[q, pl.ds(i * GLL, GLL), :] = low_edge
            stage_v[q, pl.ds((6 + i) * GLL, GLL), :] = high_edge
        send_v[2, q, pl.ds(kept, 12 * GLL), :] = stage_v[q, pl.ds(0, 12 * GLL), :].astype(LOW)
    next_r[member, pl.ds(kept, 12 * GLL), :] = send_v[2, member, pl.ds(kept, 12 * GLL), :]
    start(4)

    @pl.when(across_high)
    def _():
        start(6)

    arrived(2)
    for q in range(groups):
        block = forcing_r[q, pl.ds(0, far), :].astype(F32)
        for i in range(6):
            base = (6 * q + i) * NODES
            psi_v[pl.ds(base, GLL), :] = block[i * GLL : (i + 1) * GLL]
            psi_v[pl.ds(base + GLL, inner), :] = block[edges + i * inner : edges + (i + 1) * inner]
    edge_copy(0, 3).wait_recv()
    far_edge = edge_send[0, 2].astype(F32) + edge_recv[0, 3].astype(F32)
    for i in range(6 * groups):
        psi_v[pl.ds((i + 1) * NODES - GLL, GLL), :] = far_edge[i * GLL : (i + 1) * GLL]

    @pl.when(across_low)
    def _():
        edge_copy(0, 2).wait_recv()
        came = edge_recv[0, 2].astype(F32)
        for i in range(6 * groups):
            rows = pl.ds(i * NODES, GLL)
            psi_v[rows, :] = psi_v[rows, :] + came[i * GLL : (i + 1) * GLL]

    for i in range(6 * groups):
        rows = rows_of(i)
        psi_v[rows, :] = scale_v[...] * (psi_v[rows, :] + mult_v[...] * num_v[rows, :])

    norm = jnp.where(mode_ids == 0, 1.0 / (3.0 * modes), 0.5 / (3.0 * modes)).astype(F32)
    for p in range(2):
        lateral = []
        for c in range(3):
            psi = field(psi_v, 2 * c + p)
            other = field(psi_v, 2 * c + 1 - p)
            grads = jnp.dot(bwd_mat, psi.astype(LOW), preferred_element_type=F32)
            set_field(
                num_v,
                2 * c + p,
                wide(quad_v[...]) * ((1.0 - time_step * viscosity * wave * wave) * psi)
                + time_step * grads[2 * NODES :],
            )
            turn = -wave if p == 0 else wave
            lateral.append((grads[:NODES], grads[NODES : 2 * NODES], wide(quad_v[...]) * (turn * other)))
        for q, (left, right) in enumerate(pair_order):
            cot = lateral[right][left] + lateral[left][right]
            cot = (norm * cot).astype(LOW)
            for h in range(2):
                cot_v[p, rows_of(6 * h + q, part), :] = cot[h * part : (h + 1) * part]

    gain = jnp.where(mode_ids == 0, 3.0 * modes * time_step, 6.0 * modes * time_step).astype(F32)
    gain = gain[:part]
    for h in range(2):
        for p in range(2):
            spread_v[p] = jnp.dot(
                cot_v[p, rows_of(h, 6 * part), :], synth_v[p], preferred_element_type=F32
            )
        for c in range(3):
            even = jnp.zeros((part, even_v.shape[1]), F32)
            odd = jnp.zeros((part, even_v.shape[1]), F32)
            for d in range(3):
                se = spread_v[0, rows_of(pair_index[c][d], part), :]
                so = spread_v[1, rows_of(pair_index[c][d], part), :]
                ed, od = even_v[half_rows(d, h), :], odd_v[half_rows(d, h), :]
                even = even + (se * ed + so * od)
                odd = odd + (se * od + so * ed)
            pcot_v[0, rows_of(c, part), :] = even.astype(LOW)
            pcot_v[1, rows_of(c, part), :] = odd.astype(LOW)
        for p in range(2):
            back = jnp.dot(pcot_v[p], anal_v[p], preferred_element_type=F32)
            for c in range(3):
                i = 2 * c + p
                near = gain * back[c * part : (c + 1) * part]
                for q in range(groups):
                    rest = num_v[half_rows(6 * q + i, h), :]
                    send_v[3, q, rows_of(6 * h + i, part), :] = (
                        rest + near[:, q * 128 : (q + 1) * 128]
                    ).astype(LOW)
        start((5, 8)[h])
    start_r[member] = send_v[3, member]

    sent(1)
    sent(2)
    sent(3)
    sent(4)

    @pl.when(across_high)
    def _():
        sent(6)

    edge_copy(0, 3).wait_send()
    around_sent(1)

    @pl.when(across_high)
    def _():
        sent(9)
        edge_copy(0, 2).wait_send()

    @pl.when(jnp.logical_not(across_high))
    def _():
        slab_edge.wait_send()


    @pl.when(row_here < ROWS - 1)
    def _():
        edge_copy(1, 0).wait_send()

    @pl.when(row_here > 0)
    def _():
        edge_copy(1, 1).wait_send()

    arrived(3)
    arrived(4)
    for row in range(ROWS):
        edge_send[0, 0, pl.ds(row * 6 * GLL, 6 * GLL), :] = next_r[
            flip(row), pl.ds(kept, 6 * GLL), :
        ]
    side_copy = pltpu.make_async_remote_copy(
        src_ref=edge_send.at[0, 0],
        dst_ref=edge_recv.at[0, 0],
        send_sem=esend_sem.at[0, 0],
        recv_sem=erecv_sem.at[0, 0],
        device_id={"elems": low_slab},
        device_id_type=MESH,
    )

    @pl.when(jnp.logical_not(across_low))
    def _():
        side_copy.start()

    for row in range(ROWS):
        block = next_r[flip(row), pl.ds(0, kept + 6 * GLL), :].astype(F32)
        stage_v[row] = block[:kept]
        for i in range(6):
            full_v[row, pl.ds(i * NODES, GLL), :] = block[kept + i * GLL : kept + (i + 1) * GLL]
            count = inner if i < 5 else inner - spare * GLL
            full_v[row, pl.ds(i * NODES + GLL, count), :] = block[i * inner : i * inner + count]
        for k in range(spare):
            tile = stage_v[row, pl.ds(k * GLL * GLL, GLL, stride=GLL), :]
            full_v[row, pl.ds(6 * NODES - (spare - k + 1) * GLL, GLL), :] = tile

    @pl.when(jnp.logical_not(across_low))
    def _():
        side_copy.wait_send()

    @pl.when(jnp.logical_not(across_high))
    def _():
        side_copy.wait_recv()

    @pl.when(across_high)
    def _():
        arrived(6)
        for row in range(ROWS):
            edge_recv[0, 0, pl.ds(row * 6 * GLL, 6 * GLL), :] = next_r[
                flip(row), pl.ds(kept + 6 * GLL, 6 * GLL), :
            ]

    for row in range(ROWS):
        side = edge_recv[0, 0, pl.ds(row * 6 * GLL, 6 * GLL), :].astype(F32)
        for i in range(6):
            full_v[row, pl.ds((i + 1) * NODES - GLL, GLL), :] = side[i * GLL : (i + 1) * GLL]
        if row == 0:
            shared = jnp.zeros((6 * GLL, 128), F32)
        else:
            shared = full_v[row - 1, pl.ds(GLL - 1, 6 * GLL, stride=GLL), :]
        full_v[row, pl.ds(0, 6 * GLL, stride=GLL), :] = shared
    for j in range(ROWS):
        next_o[j] = full_v[slots[j]].reshape(3, 2, NODES, 128)
    arrived(5)
    arrived(8)
    for j in range(ROWS):
        block = start_r[flip(slots[j])].astype(F32)
        for h in range(2):
            for i in range(6):
                begin = (6 * h + i) * part
                start_o[j, i // 2, i % 2, rows_of(h, part), :] = block[begin : begin + part]
    sent(5)
    sent(8)


def store_kernel(next_v, start_v, next_ref, start_ref, sem):
    stores = [
        pltpu.make_async_copy(source.at[j], target.at[j], sem.at[which, j])
        for which, (source, target) in enumerate(((next_v, next_ref), (start_v, start_ref)))
        for j in range(ROWS)
    ]
    for store in stores:
        store.start()
    for store in stores:
        store.wait()


def on_device(state, adjoint_end, observed, spacing, radial_slot):
    groups = lax.axis_size("modes")
    slabs = lax.axis_size("elems")
    modes = groups * state.shape[4]
    half = 3 * modes // 2
    synth, analysis = half_tables(modes, 3 * modes)
    fwd, bwd, w2 = node_tables()
    any_spec = pl.BlockSpec(memory_space=pltpu.HBM)
    vmem_spec = pl.BlockSpec(memory_space=pltpu.VMEM)
    local = state.shape
    block = (6 * NODES, 128)
    vm = pltpu.VMEM
    sem = pltpu.SemaphoreType.DMA

    def run(*args):
        step_kernel(groups, slabs, *args)

    held_out = pltpu.VMEM(local, F32)

    def held(array):
        return pltpu.with_memory_space_constraint(array, pltpu.HBM)

    next_v, start_v = pl.pallas_call(
        run,
        out_shape=(held_out, held_out),
        in_specs=[any_spec] * 10,
        out_specs=(vmem_spec, vmem_spec),
        scratch_shapes=[
            pltpu.SMEM((2, ROWS), F32), pltpu.SMEM((1, ROWS), jnp.int32),
            vm(local, F32), vm(local, F32), vm(local, LOW),
            vm((2, modes, half), LOW), vm((2, half, modes), LOW),
            vm((2, NODES, 3 * NODES), F32), vm((2, 3 * NODES, NODES), F32), vm((NODES, 128), F32),
            vm((4, ROWS) + block, LOW), *[vm((ROWS,) + block, LOW)] * 4,
            vm((NODES, 128), F32), vm((NODES, 128), F32), vm((NODES, 128), F32),
            vm((3 * NODES, half), F32), vm((3 * NODES, half), F32),
            vm((2, 6 * NODES, half), LOW), vm((2, 6 * NODES, modes), LOW),
            vm((6 * NODES * groups, 128), F32), vm((6 * NODES * groups, 128), F32),
            vm((2, 6 * NODES, modes), LOW), vm((2, 3 * NODES, half), F32),
            vm((2, 3 * NODES // 2, half), LOW),
            vm((2, 4, 6 * GLL * groups, 128), LOW), vm((2, 4, 6 * GLL * groups, 128), LOW),
            vm((ROWS, 256, 128), F32), vm((ROWS,) + block, F32),
            vm((2, GLL, 128), F32), vm((2, GLL, 128), F32),
            sem((9 + ROWS,)), sem((10, ROWS)), sem((10, ROWS)), sem((2, 4)), sem((2, 4)),
            sem((2,)), sem((2,)),
        ],
        compiler_params=pltpu.CompilerParams(
            collective_id=0, has_side_effects=True, vmem_limit_bytes=48 * 1024 * 1024
        ),
        cost_estimate=pl.CostEstimate(
            flops=1900000000, bytes_accessed=7000000, transcendentals=0
        ),
    )(
        held(state), held(adjoint_end), held(observed), held(spacing.T), held(radial_slot),
        held(jnp.asarray(synth, F32).astype(LOW)), held(jnp.asarray(analysis, F32).astype(LOW)),
        held(jnp.asarray(fwd, F32)), held(jnp.asarray(bwd, F32)),
        held(jnp.asarray(np.broadcast_to(w2[:, None], (NODES, 128)), F32)),
    )
    return pl.pallas_call(
        store_kernel,
        out_shape=(jax.ShapeDtypeStruct(local, F32), jax.ShapeDtypeStruct(local, F32)),
        in_specs=[pl.BlockSpec(memory_space=pl.ANY)] * 2,
        out_specs=(any_spec, any_spec),
        scratch_shapes=[sem((2, ROWS))],
        compiler_params=pltpu.CompilerParams(vmem_limit_bytes=1024 * 1024),
    )(next_v, start_v)


def solution(mesh):
    in_specs = (
        P("elems", None, None, None, "modes"),
        P("elems", None, None, None, "modes"),
        P("elems", None, None, None, "modes"),
        P("elems", None),
        P("elems", None),
    )
    out_specs = (P("elems", None, None, None, "modes"), P("elems", None, None, None, "modes"))
    return jax.shard_map(
        on_device, mesh=mesh, in_specs=in_specs, out_specs=out_specs, check_vma=False
    )
```

```python
import jax
import jax.numpy as jnp
import numpy as np
from jax import lax
from jax.experimental import pallas as pl
from jax.experimental.pallas import tpu as pltpu
from jax.sharding import PartitionSpec as P

GLL = 8
NODES = GLL * GLL
ROWS = 4
CHIP_ROW = 8
time_step = 0.01
viscosity = 0.05
wave_scale = 4.0
pair_order = ((0, 0), (0, 1), (0, 2), (1, 1), (1, 2), (2, 2))
pair_index = ((0, 1, 2), (1, 3, 4), (2, 4, 5))
F32 = jnp.float32
LOW = jnp.bfloat16
MESH = pl.DeviceIdType.MESH


def legendre_table(points, quad_count):
    columns = [points * 0.0 + 1.0, points]
    for degree in range(2, quad_count):
        columns.append(
            ((2 * degree - 1) * points * columns[-1] - (degree - 1) * columns[-2]) / degree
        )
    return np.stack(columns, axis=1)


def gll_tables(quad_count):
    degree = quad_count - 1
    points = -np.cos(np.pi * np.arange(quad_count) / degree)
    for repeat in range(60):
        vander = legendre_table(points, quad_count)
        points = points - (points * vander[:, degree] - vander[:, degree - 1]) / (
            quad_count * vander[:, degree]
        )
    vander = legendre_table(points, quad_count)
    edge_value = vander[:, degree]
    weights = 2.0 / (degree * quad_count * edge_value * edge_value)
    diagonal_mask = np.arange(quad_count)[:, None] == np.arange(quad_count)[None, :]
    differ = np.where(diagonal_mask, 1.0, points[:, None] - points[None, :])
    derivative = np.where(diagonal_mask, 0.0, edge_value[:, None] / (edge_value[None, :] * differ))
    derivative[0, 0] = -degree * quad_count / 4.0
    derivative[degree, degree] = degree * quad_count / 4.0
    return (weights, derivative)


def half_tables(modes, planes):
    half = planes // 2
    turns = np.outer(np.arange(modes), 2 * np.arange(half) + 1) % (2 * planes)
    angles = np.pi * turns / planes
    factor = np.where(np.arange(modes) == 0, 1.0, 2.0)[:, None]
    synth = np.stack((factor * np.cos(angles), -factor * np.sin(angles)))
    analysis = np.stack((np.cos(angles), -np.sin(angles))) * (2.0 / planes)
    return synth, np.transpose(analysis, (0, 2, 1))


def node_tables():
    weights, deriv = gll_tables(GLL)
    wdiag = np.diag(weights)
    back = deriv.T @ wdiag
    ahead = wdiag @ deriv
    stiff = deriv.T @ wdiag @ deriv
    zero = np.zeros((NODES, NODES))
    fwd = (
        np.concatenate((np.kron(back, wdiag), np.kron(wdiag, back), np.kron(stiff, wdiag)), 1),
        np.concatenate((zero, zero, np.kron(wdiag, stiff)), 1),
    )
    adj = (
        np.concatenate((np.kron(ahead, wdiag), np.kron(wdiag, ahead), np.kron(stiff, wdiag)), 0),
        np.concatenate((zero, zero, np.kron(wdiag, stiff)), 0),
    )
    return np.stack(fwd), np.stack(adj), np.kron(weights, weights)


def step_kernel(
    groups,
    slabs,
    state_ref, adj_ref, obs_ref, spacing_h, slot_h, synth_ref, anal_ref, fwd_ref, bwd_ref, w2_ref,
    next_o, start_o,
    spacing_ref, slot_ref, state_v, adj_v, obs_v, synth_v, anal_v, fwd_v, bwd_v, w2_v,
    send_v, state_r, forcing_r, next_r, start_a, start_b, quad_v, scale_v, mult_v,
    even_v, odd_v, prod_v, modal_v, num_v, psi_v, cot_v, spread_v, pcot_v,
    edge_send, edge_recv, stage_v, full_v, mass_send, mass_recv,
    load_sem, send_sem, recv_sem, esend_sem, erecv_sem, msend_sem, mrecv_sem,
):
    member = lax.axis_index("modes")
    slab = lax.axis_index("elems")
    low_slab = lax.rem(slab + slabs - 1, slabs)
    high_slab = lax.rem(slab + 1, slabs)
    partners = (lax.rem(member + 2, 4), 3 - member, member + 1 - 2 * lax.rem(member, 2))
    modes = groups * 128
    recv = (state_r, forcing_r, next_r, start_a)

    loads = [
        pltpu.make_async_copy(src, dst, load_sem.at[i])
        for i, (src, dst) in enumerate(
            [(slot_h, slot_ref), (spacing_h, spacing_ref)]
            + [(state_ref.at[j], state_v.at[j]) for j in range(ROWS)]
            + [
                (adj_ref, adj_v), (obs_ref, obs_v), (w2_ref, w2_v),
                (fwd_ref, fwd_v), (synth_ref, synth_v), (anal_ref, anal_v), (bwd_ref, bwd_v),
            ]
        )
    ]
    adj_load, obs_load, w2_load, fwd_load, synth_load, anal_load, bwd_load = loads[2 + ROWS :]
    for load in loads:
        load.start()

    barrier = pltpu.get_barrier_semaphore()
    for partner in partners:
        pl.semaphore_signal(barrier, inc=1, device_id={"modes": partner}, device_id_type=MESH)

    place = lax.rem(slab, 2 * CHIP_ROW)
    early_low = place == 0
    early_high = place == CHIP_ROW - 1
    across_low = jnp.logical_or(early_low, place == CHIP_ROW)
    across_high = jnp.logical_or(early_high, place == 2 * CHIP_ROW - 1)
    early = jnp.logical_or(early_low, early_high)
    greet_low_now = jnp.logical_not(across_low)
    greet_high_now = jnp.logical_not(across_high)

    mirrored = place >= CHIP_ROW

    def flip(index):
        return jnp.where(mirrored, ROWS - 1 - index, index)

    row_here = flip(member)

    def around(way):
        across = (across_high, across_low)[way]
        return {
            "modes": jnp.where(across, ROWS - 1 - member, member),
            "elems": (high_slab, low_slab)[way],
        }

    def greet(way):
        pl.semaphore_signal(barrier, inc=1, device_id=around(way), device_id_type=MESH)

    @pl.when(greet_low_now)
    def _():
        greet(1)

    @pl.when(greet_high_now)
    def _():
        greet(0)

    loads[0].wait()
    loads[1].wait()
    slots = [slot_ref[0, j] for j in range(ROWS)]

    def rows_of(index, count=NODES):
        return pl.ds(index * count, count)

    def flat(block):
        return block.reshape(6 * NODES, 128)

    def elem_of(row):
        place = jnp.int32(0)
        for j in range(1, ROWS):
            place = jnp.where(slots[j] == row, j, place)
        return place

    part = NODES // 2
    halves = ((0, 6 * part), (6 * part, 12 * part))
    inner = NODES - 2 * GLL
    edges = 6 * GLL
    far = edges + 6 * inner
    spare = 4
    kept = 6 * inner - spare * GLL
    phases = (
        (0,) + halves[0],
        (1, 0, edges), (1, edges, far),
        (2, 0, kept), (2, kept, kept + 6 * GLL),
        (3,) + halves[0],
        (2, kept + 6 * GLL, kept + 12 * GLL),
        (0,) + halves[1],
        (3,) + halves[1],
        (1, far, 6 * NODES),
    )

    def swap(phase, partner, arrival=False):
        which, begin, end = phases[phase]
        rows = pl.ds(begin, end - begin)
        slot = partner if arrival else member
        if phase == 8:
            target = start_b.at[slot]
        elif phase == 5:
            target = start_a.at[slot]
        else:
            target = recv[which].at[slot, rows]
        return pltpu.make_async_remote_copy(
            src_ref=send_v.at[which, partner, rows],
            dst_ref=target,
            send_sem=send_sem.at[phase, partner],
            recv_sem=recv_sem.at[phase, slot],
            device_id={"modes": partner},
            device_id_type=MESH,
        )

    def start(phase):
        for partner in partners:
            swap(phase, partner).start()

    def sent(phase):
        for partner in partners:
            swap(phase, partner).wait_send()

    def arrived(phase):
        for partner in partners:
            swap(phase, partner, arrival=True).wait_recv()

    for load in loads[2 : 2 + ROWS]:
        load.wait()
    for device in range(ROWS):
        block = flat(state_v[elem_of(flip(device))]).astype(LOW)
        for h in range(2):
            for i in range(6):
                begin = i * NODES + h * part
                send_v[0, device, rows_of(6 * h + i, part), :] = block[begin : begin + part]

    @pl.when(early)
    def _():
        pl.semaphore_wait(barrier, 4)

    @pl.when(jnp.logical_not(early))
    def _():
        pl.semaphore_wait(barrier, 5)

    @pl.when(jnp.logical_not(greet_low_now))
    def _():
        greet(1)

    @pl.when(jnp.logical_not(greet_high_now))
    def _():
        greet(0)

    start(0)
    start(7)
    state_r[member] = send_v[0, member]

    w2_load.wait()
    own = elem_of(row_here)
    row_above = jnp.minimum(row_here + 1, ROWS - 1)
    row_below = jnp.maximum(row_here - 1, 0)
    above = elem_of(row_above)
    below = elem_of(row_below)

    def area(elem):
        return spacing_ref[0, elem] * spacing_ref[1, elem] * 0.25

    side_x = spacing_ref[0, own]
    side_y = spacing_ref[1, own]
    full = (NODES, 128)
    layer = lax.rem(lax.broadcasted_iota(jnp.int32, full, 0), GLL)
    has_above = jnp.logical_and(layer == GLL - 1, row_here < ROWS - 1)
    has_below = jnp.logical_and(layer == 0, row_here > 0)
    w2 = w2_v[...]
    quad = w2 * area(own)
    quad_v[...] = quad
    mass = quad + jnp.where(has_above, w2 * area(above), 0.0)
    mass = mass + jnp.where(has_below, w2 * area(below), 0.0)
    at_wall = jnp.logical_and(layer == 0, row_here == 0)
    keep = jnp.where(at_wall, 0.0, 1.0)
    scale_v[...] = keep / mass
    mass_send[0] = mass[NODES - GLL :]
    mass_send[1] = mass[:GLL]

    def mass_copy(way):
        return pltpu.make_async_remote_copy(
            src_ref=mass_send.at[way],
            dst_ref=mass_recv.at[way],
            send_sem=msend_sem.at[way],
            recv_sem=mrecv_sem.at[way],
            device_id=around(way),
            device_id_type=MESH,
        )

    copies = jnp.where(jnp.logical_or(has_above, has_below), 2.0, 1.0).astype(F32)
    node_a = lax.broadcasted_iota(jnp.int32, full, 0) // GLL
    mult_v[...] = jnp.where(jnp.logical_or(node_a == 0, node_a == GLL - 1), 2.0 * copies, copies)

    edge_rows = 6 * GLL * groups
    top = pl.ds(GLL - 1, edge_rows, stride=GLL)
    low = pl.ds(0, edge_rows, stride=GLL)

    def edge_copy(which, way):
        if way == 0:
            target = {"modes": flip(row_above)}
        elif way == 1:
            target = {"modes": flip(row_below)}
        else:
            target = around(way - 2)
        return pltpu.make_async_remote_copy(
            src_ref=edge_send.at[which, way],
            dst_ref=edge_recv.at[which, way],
            send_sem=esend_sem.at[which, way],
            recv_sem=erecv_sem.at[which, way],
            device_id=target,
            device_id_type=MESH,
        )

    def pack_around(which, buf):
        for way, begin in ((2, NODES - GLL), (3, 0)):
            edge_send[which, way] = jnp.concatenate(
                [buf[pl.ds(i * NODES + begin, GLL), :] for i in range(6 * groups)], axis=0
            ).astype(LOW)

    def add_around(which, buf):
        for way, begin in ((2, 0), (3, NODES - GLL)):
            edge_copy(which, way).wait_recv()
            came = edge_recv[which, way].astype(F32)
            for i in range(6 * groups):
                rows = pl.ds(i * NODES + begin, GLL)
                buf[rows, :] = buf[rows, :] + came[i * GLL : (i + 1) * GLL]

    def around_sent(which):
        for way in (2, 3):
            edge_copy(which, way).wait_send()

    adj_load.wait()
    obs_load.wait()
    for row in range(ROWS):
        elem = elem_of(row)
        psi_v[rows_of(row, 6 * NODES), :] = flat(adj_v[elem] - obs_v[elem].astype(F32))
    for row in range(ROWS - 1):
        lower = pl.ds(row * 6 * NODES + GLL - 1, 6 * GLL, stride=GLL)
        upper = pl.ds((row + 1) * 6 * NODES, 6 * GLL, stride=GLL)
        both = psi_v[lower, :] + psi_v[upper, :]
        psi_v[lower, :] = both
        psi_v[upper, :] = both
    slab_edge = pltpu.make_async_remote_copy(
        src_ref=edge_send.at[0, 1],
        dst_ref=edge_recv.at[0, 1],
        send_sem=esend_sem.at[0, 1],
        recv_sem=erecv_sem.at[0, 1],
        device_id={"elems": high_slab},
        device_id_type=MESH,
    )
    edge_send[0, 1] = jnp.concatenate(
        [psi_v[pl.ds((i + 1) * NODES - GLL, GLL), :] for i in range(6 * ROWS)], axis=0
    ).astype(LOW)

    @pl.when(jnp.logical_not(across_high))
    def _():
        slab_edge.start()

    for row in range(ROWS):
        device = flip(row)
        for i in range(6):
            base = (6 * row + i) * NODES
            send_v[1, device, pl.ds(edges + i * inner, inner), :] = psi_v[
                pl.ds(base + GLL, inner), :
            ].astype(LOW)

    @pl.when(jnp.logical_not(across_low))
    def _():
        slab_edge.wait_recv()
        came = edge_recv[0, 1].astype(F32)
        for i in range(6 * ROWS):
            rows = pl.ds(i * NODES, GLL)
            psi_v[rows, :] = psi_v[rows, :] + came[i * GLL : (i + 1) * GLL]

    for row in range(ROWS):
        device = flip(row)
        for begin, offset in ((0, 0), (far, NODES - GLL)):
            send_v[1, device, pl.ds(begin, edges), :] = jnp.concatenate(
                [psi_v[pl.ds((6 * row + i) * NODES + offset, GLL), :] for i in range(6)], axis=0
            ).astype(LOW)
    forcing_r[member] = send_v[1, member]
    fwd_load.wait()
    bwd_load.wait()
    lane = lax.broadcasted_iota(jnp.int32, (NODES, 3 * NODES), 1)
    ratio = jnp.full((NODES, 3 * NODES), side_y) / jnp.full((NODES, 3 * NODES), side_x)
    coef = jnp.where(
        lane < NODES, 0.5 * side_y, jnp.where(lane < 2 * NODES, 0.5 * side_x, -viscosity * ratio)
    )
    fwd_mat = (time_step * (fwd_v[0] * coef - fwd_v[1] * (viscosity / ratio))).astype(LOW)
    line = lax.broadcasted_iota(jnp.int32, (3 * NODES, NODES), 0)
    ratio = jnp.full((3 * NODES, NODES), side_y) / jnp.full((3 * NODES, NODES), side_x)
    coef = jnp.where(
        line < NODES, 0.5 * side_y, jnp.where(line < 2 * NODES, 0.5 * side_x, -viscosity * ratio)
    )
    bwd_mat = (bwd_v[0] * coef - bwd_v[1] * (viscosity / ratio)).astype(LOW)

    def state_part(h, i):
        rows = rows_of(6 * h + i, part)
        return jnp.concatenate([state_r[q, rows, :] for q in range(groups)], axis=1)

    def wide(block):
        return jnp.concatenate([block] * groups, axis=1)

    def field(buf, i):
        return jnp.concatenate([buf[rows_of(6 * q + i), :] for q in range(groups)], axis=1)

    def set_field(buf, i, value):
        for q in range(groups):
            buf[rows_of(6 * q + i), :] = value[:, q * 128 : (q + 1) * 128]

    mode_ids = lax.broadcasted_iota(jnp.int32, (NODES, modes), 1)
    wave = mode_ids.astype(F32) * (wave_scale / modes)

    synth_load.wait()
    anal_load.wait()

    def half_rows(index, h):
        return pl.ds(index * NODES + h * part, part)

    for h in range(2):
        if h == 0:
            arrived(0)
        else:
            sent(0)
            sent(7)
            start(1)

            @pl.when(across_high)
            def _():
                start(9)

            arrived(7)
        for p, planes in ((0, even_v), (1, odd_v)):
            values = jnp.dot(
                jnp.concatenate([state_part(h, 2 * c + p) for c in range(3)], axis=0),
                synth_v[p],
                preferred_element_type=F32,
            )
            for c in range(3):
                planes[half_rows(c, h), :] = values[c * part : (c + 1) * part]
        for q, (left, right) in enumerate(pair_order):
            el, ol = even_v[half_rows(left, h), :], odd_v[half_rows(left, h), :]
            er, orr = even_v[half_rows(right, h), :], odd_v[half_rows(right, h), :]
            prod_v[0, rows_of(6 * h + q, part), :] = (el * er + ol * orr).astype(LOW)
            prod_v[1, rows_of(6 * h + q, part), :] = (el * orr + ol * er).astype(LOW)
        for p in range(2):
            values = jnp.dot(
                prod_v[p, rows_of(h, 6 * part), :], anal_v[p], preferred_element_type=F32
            ).astype(LOW)
            for q in range(6):
                modal_v[p, half_rows(q, h), :] = values[q * part : (q + 1) * part]

    for c in range(3):
        for p in range(2):
            values = jnp.concatenate([state_part(h, 2 * c + p) for h in range(2)], axis=0)
            stack = jnp.concatenate(
                [
                    modal_v[p, rows_of(pair_index[0][c]), :],
                    modal_v[p, rows_of(pair_index[1][c]), :],
                    values,
                ],
                axis=0,
            )
            flux_z = modal_v[1 - p, rows_of(pair_index[2][c]), :].astype(F32)
            turn = (-time_step if p == 1 else time_step) * wave
            local = (1.0 - time_step * viscosity * wave * wave) * values.astype(F32)
            set_field(
                num_v,
                2 * c + p,
                jnp.dot(fwd_mat, stack, preferred_element_type=F32)
                + wide(quad_v[...]) * (local + turn * flux_z),
            )

    @pl.when(row_here < ROWS - 1)
    def _():
        edge_send[1, 0] = num_v[top, :].astype(LOW)
        edge_copy(1, 0).start()

    @pl.when(row_here > 0)
    def _():
        edge_send[1, 1] = num_v[low, :].astype(LOW)
        edge_copy(1, 1).start()

    start(2)

    @pl.when(early)
    def _():
        pl.semaphore_wait(barrier, 1)

    mass_copy(0).start()
    mass_copy(1).start()
    arrived(1)
    for q in range(groups):
        edge_send[0, 3, pl.ds(q * edges, edges), :] = forcing_r[q, pl.ds(0, edges), :]
    edge_copy(0, 3).start()

    @pl.when(across_high)
    def _():
        arrived(9)
        for q in range(groups):
            edge_send[0, 2, pl.ds(q * edges, edges), :] = forcing_r[q, pl.ds(far, edges), :]
        edge_copy(0, 2).start()

    @pl.when(jnp.logical_not(across_high))
    def _():
        edge_send[0, 2] = jnp.zeros((edge_rows, 128), LOW)

    @pl.when(row_here > 0)
    def _():
        edge_copy(1, 0).wait_recv()
        num_v[low, :] = num_v[low, :] + edge_recv[1, 0].astype(F32)

    @pl.when(row_here < ROWS - 1)
    def _():
        edge_copy(1, 1).wait_recv()
        num_v[top, :] = num_v[top, :] + edge_recv[1, 1].astype(F32)

    pack_around(1, num_v)
    edge_copy(1, 2).start()
    edge_copy(1, 3).start()
    for q in range(groups):
        for i in range(6):
            rows = pl.ds((6 * q + i) * NODES + GLL, inner)
            value = scale_v[GLL : NODES - GLL, :] * num_v[rows, :]
            num_v[rows, :] = value
            if i < 5:
                stage_v[q, pl.ds(i * inner, inner), :] = value
            else:
                stage_v[q, pl.ds(i * inner, inner - spare * GLL), :] = value[: inner - spare * GLL]
                for k in range(spare):
                    tile = value[inner - (spare - k) * GLL : inner - (spare - k - 1) * GLL]
                    stage_v[q, pl.ds(k * GLL * GLL, GLL, stride=GLL), :] = tile
        send_v[2, q, pl.ds(0, kept), :] = stage_v[q].astype(LOW)
    next_r[member, pl.ds(0, kept), :] = send_v[2, member, pl.ds(0, kept), :]
    start(3)
    mass_copy(0).wait()
    mass_copy(1).wait()
    scale_v[:GLL, :] = keep[:GLL] / (mass_send[1] + mass_recv[0])
    scale_v[NODES - GLL :, :] = keep[NODES - GLL :] / (mass_send[0] + mass_recv[1])
    add_around(1, num_v)
    for q in range(groups):
        for i in range(6):
            base = (6 * q + i) * NODES
            low_edge = scale_v[:GLL, :] * num_v[pl.ds(base, GLL), :]
            num_v[pl.ds(base, GLL), :] = low_edge
            high_edge = scale_v[NODES - GLL :, :] * num_v[pl.ds(base + NODES - GLL, GLL), :]
            num_v[pl.ds(base + NODES - GLL, GLL), :] = high_edge
            stage_v[q, pl.ds(i * GLL, GLL), :] = low_edge
            stage_v[q, pl.ds((6 + i) * GLL, GLL), :] = high_edge
        send_v[2, q, pl.ds(kept, 12 * GLL), :] = stage_v[q, pl.ds(0, 12 * GLL), :].astype(LOW)
    next_r[member, pl.ds(kept, 12 * GLL), :] = send_v[2, member, pl.ds(kept, 12 * GLL), :]
    start(4)

    @pl.when(across_high)
    def _():
        start(6)

    arrived(2)
    for q in range(groups):
        block = forcing_r[q, pl.ds(0, far), :].astype(F32)
        for i in range(6):
            base = (6 * q + i) * NODES
            psi_v[pl.ds(base, GLL), :] = block[i * GLL : (i + 1) * GLL]
            psi_v[pl.ds(base + GLL, inner), :] = block[edges + i * inner : edges + (i + 1) * inner]
    edge_copy(0, 3).wait_recv()
    far_edge = edge_send[0, 2].astype(F32) + edge_recv[0, 3].astype(F32)
    for i in range(6 * groups):
        psi_v[pl.ds((i + 1) * NODES - GLL, GLL), :] = far_edge[i * GLL : (i + 1) * GLL]

    @pl.when(across_low)
    def _():
        edge_copy(0, 2).wait_recv()
        came = edge_recv[0, 2].astype(F32)
        for i in range(6 * groups):
            rows = pl.ds(i * NODES, GLL)
            psi_v[rows, :] = psi_v[rows, :] + came[i * GLL : (i + 1) * GLL]

    for i in range(6 * groups):
        rows = rows_of(i)
        psi_v[rows, :] = scale_v[...] * (psi_v[rows, :] + mult_v[...] * num_v[rows, :])

    norm = jnp.where(mode_ids == 0, 1.0 / (3.0 * modes), 0.5 / (3.0 * modes)).astype(F32)
    for p in range(2):
        lateral = []
        for c in range(3):
            psi = field(psi_v, 2 * c + p)
            other = field(psi_v, 2 * c + 1 - p)
            grads = jnp.dot(bwd_mat, psi.astype(LOW), preferred_element_type=F32)
            set_field(
                num_v,
                2 * c + p,
                wide(quad_v[...]) * ((1.0 - time_step * viscosity * wave * wave) * psi)
                + time_step * grads[2 * NODES :],
            )
            turn = -wave if p == 0 else wave
            lateral.append((grads[:NODES], grads[NODES : 2 * NODES], wide(quad_v[...]) * (turn * other)))
        for q, (left, right) in enumerate(pair_order):
            cot = lateral[right][left] + lateral[left][right]
            cot = (norm * cot).astype(LOW)
            for h in range(2):
                cot_v[p, rows_of(6 * h + q, part), :] = cot[h * part : (h + 1) * part]

    gain = jnp.where(mode_ids == 0, 3.0 * modes * time_step, 6.0 * modes * time_step).astype(F32)
    gain = gain[:part]
    for h in range(2):
        for p in range(2):
            spread_v[p] = jnp.dot(
                cot_v[p, rows_of(h, 6 * part), :], synth_v[p], preferred_element_type=F32
            )
        for c in range(3):
            even = jnp.zeros((part, even_v.shape[1]), F32)
            odd = jnp.zeros((part, even_v.shape[1]), F32)
            for d in range(3):
                se = spread_v[0, rows_of(pair_index[c][d], part), :]
                so = spread_v[1, rows_of(pair_index[c][d], part), :]
                ed, od = even_v[half_rows(d, h), :], odd_v[half_rows(d, h), :]
                even = even + (se * ed + so * od)
                odd = odd + (se * od + so * ed)
            pcot_v[0, rows_of(c, part), :] = even.astype(LOW)
            pcot_v[1, rows_of(c, part), :] = odd.astype(LOW)
        for p in range(2):
            back = jnp.dot(pcot_v[p], anal_v[p], preferred_element_type=F32)
            for c in range(3):
                i = 2 * c + p
                near = gain * back[c * part : (c + 1) * part]
                for q in range(groups):
                    rest = num_v[half_rows(6 * q + i, h), :]
                    send_v[3, q, rows_of(6 * h + i, part), :] = (
                        rest + near[:, q * 128 : (q + 1) * 128]
                    ).astype(LOW)
        start((5, 8)[h])
    start_a[member] = send_v[3, member, rows_of(0, 6 * part), :]
    start_b[member] = send_v[3, member, rows_of(1, 6 * part), :]

    sent(1)
    sent(2)
    sent(3)
    sent(4)

    @pl.when(across_high)
    def _():
        sent(6)

    edge_copy(0, 3).wait_send()
    around_sent(1)

    @pl.when(across_high)
    def _():
        sent(9)
        edge_copy(0, 2).wait_send()

    @pl.when(jnp.logical_not(across_high))
    def _():
        slab_edge.wait_send()


    @pl.when(row_here < ROWS - 1)
    def _():
        edge_copy(1, 0).wait_send()

    @pl.when(row_here > 0)
    def _():
        edge_copy(1, 1).wait_send()

    arrived(3)
    arrived(4)
    for row in range(ROWS):
        edge_send[0, 0, pl.ds(row * 6 * GLL, 6 * GLL), :] = next_r[
            flip(row), pl.ds(kept, 6 * GLL), :
        ]
    side_copy = pltpu.make_async_remote_copy(
        src_ref=edge_send.at[0, 0],
        dst_ref=edge_recv.at[0, 0],
        send_sem=esend_sem.at[0, 0],
        recv_sem=erecv_sem.at[0, 0],
        device_id={"elems": low_slab},
        device_id_type=MESH,
    )

    @pl.when(jnp.logical_not(across_low))
    def _():
        side_copy.start()

    for row in range(ROWS):
        block = next_r[flip(row), pl.ds(0, kept + 6 * GLL), :].astype(F32)
        stage_v[row] = block[:kept]
        for i in range(6):
            full_v[row, pl.ds(i * NODES, GLL), :] = block[kept + i * GLL : kept + (i + 1) * GLL]
            count = inner if i < 5 else inner - spare * GLL
            full_v[row, pl.ds(i * NODES + GLL, count), :] = block[i * inner : i * inner + count]
        for k in range(spare):
            tile = stage_v[row, pl.ds(k * GLL * GLL, GLL, stride=GLL), :]
            full_v[row, pl.ds(6 * NODES - (spare - k + 1) * GLL, GLL), :] = tile

    @pl.when(jnp.logical_not(across_low))
    def _():
        side_copy.wait_send()

    @pl.when(jnp.logical_not(across_high))
    def _():
        side_copy.wait_recv()

    @pl.when(across_high)
    def _():
        arrived(6)
        for row in range(ROWS):
            edge_recv[0, 0, pl.ds(row * 6 * GLL, 6 * GLL), :] = next_r[
                flip(row), pl.ds(kept + 6 * GLL, 6 * GLL), :
            ]

    for row in range(ROWS):
        side = edge_recv[0, 0, pl.ds(row * 6 * GLL, 6 * GLL), :].astype(F32)
        for i in range(6):
            full_v[row, pl.ds((i + 1) * NODES - GLL, GLL), :] = side[i * GLL : (i + 1) * GLL]
        if row == 0:
            shared = jnp.zeros((6 * GLL, 128), F32)
        else:
            shared = full_v[row - 1, pl.ds(GLL - 1, 6 * GLL, stride=GLL), :]
        full_v[row, pl.ds(0, 6 * GLL, stride=GLL), :] = shared
    for j in range(ROWS):
        next_o[j] = full_v[slots[j]].reshape(3, 2, NODES, 128)
    for h, (phase, rows) in enumerate(((5, start_a), (8, start_b))):
        arrived(phase)
        for j in range(ROWS):
            block = rows[flip(slots[j])].astype(F32)
            for i in range(6):
                start_o[j, i // 2, i % 2, rows_of(h, part), :] = block[i * part : (i + 1) * part]
    sent(5)
    sent(8)


def store_kernel(next_v, start_v, next_ref, start_ref, sem):
    stores = [
        pltpu.make_async_copy(source, target, sem.at[which])
        for which, (source, target) in enumerate(((next_v, next_ref), (start_v, start_ref)))
    ]
    for store in stores:
        store.start()
    for store in stores:
        store.wait()


def on_device(state, adjoint_end, observed, spacing, radial_slot):
    groups = lax.axis_size("modes")
    slabs = lax.axis_size("elems")
    modes = groups * state.shape[4]
    half = 3 * modes // 2
    synth, analysis = half_tables(modes, 3 * modes)
    fwd, bwd, w2 = node_tables()
    any_spec = pl.BlockSpec(memory_space=pltpu.HBM)
    vmem_spec = pl.BlockSpec(memory_space=pltpu.VMEM)
    local = state.shape
    block = (6 * NODES, 128)
    vm = pltpu.VMEM
    sem = pltpu.SemaphoreType.DMA

    def run(*args):
        step_kernel(groups, slabs, *args)

    held_out = pltpu.VMEM(local, F32)

    def held(array):
        return pltpu.with_memory_space_constraint(array, pltpu.HBM)

    next_v, start_v = pl.pallas_call(
        run,
        out_shape=(held_out, held_out),
        in_specs=[any_spec] * 10,
        out_specs=(vmem_spec, vmem_spec),
        scratch_shapes=[
            pltpu.SMEM((2, ROWS), F32), pltpu.SMEM((1, ROWS), jnp.int32),
            vm(local, F32), vm(local, F32), vm(local, LOW),
            vm((2, modes, half), LOW), vm((2, half, modes), LOW),
            vm((2, NODES, 3 * NODES), F32), vm((2, 3 * NODES, NODES), F32), vm((NODES, 128), F32),
            vm((4, ROWS) + block, LOW), *[vm((ROWS,) + block, LOW)] * 3,
            *[vm((ROWS, 3 * NODES, 128), LOW)] * 2,
            vm((NODES, 128), F32), vm((NODES, 128), F32), vm((NODES, 128), F32),
            vm((3 * NODES, half), F32), vm((3 * NODES, half), F32),
            vm((2, 6 * NODES, half), LOW), vm((2, 6 * NODES, modes), LOW),
            vm((6 * NODES * groups, 128), F32), vm((6 * NODES * groups, 128), F32),
            vm((2, 6 * NODES, modes), LOW), vm((2, 3 * NODES, half), F32),
            vm((2, 3 * NODES // 2, half), LOW),
            vm((2, 4, 6 * GLL * groups, 128), LOW), vm((2, 4, 6 * GLL * groups, 128), LOW),
            vm((ROWS, 256, 128), F32), vm((ROWS,) + block, F32),
            vm((2, GLL, 128), F32), vm((2, GLL, 128), F32),
            sem((9 + ROWS,)), sem((10, ROWS)), sem((10, ROWS)), sem((2, 4)), sem((2, 4)),
            sem((2,)), sem((2,)),
        ],
        compiler_params=pltpu.CompilerParams(
            collective_id=0, has_side_effects=True, vmem_limit_bytes=48 * 1024 * 1024
        ),
        cost_estimate=pl.CostEstimate(
            flops=1900000000, bytes_accessed=7000000, transcendentals=0
        ),
    )(
        held(state), held(adjoint_end), held(observed), held(spacing.T), held(radial_slot),
        held(jnp.asarray(synth, F32).astype(LOW)), held(jnp.asarray(analysis, F32).astype(LOW)),
        held(jnp.asarray(fwd, F32)), held(jnp.asarray(bwd, F32)),
        held(jnp.asarray(np.broadcast_to(w2[:, None], (NODES, 128)), F32)),
    )
    return pl.pallas_call(
        store_kernel,
        out_shape=(jax.ShapeDtypeStruct(local, F32), jax.ShapeDtypeStruct(local, F32)),
        in_specs=[pl.BlockSpec(memory_space=pl.ANY)] * 2,
        out_specs=(any_spec, any_spec),
        scratch_shapes=[sem((2,))],
        compiler_params=pltpu.CompilerParams(vmem_limit_bytes=1024 * 1024),
    )(next_v, start_v)


def solution(mesh):
    in_specs = (
        P("elems", None, None, None, "modes"),
        P("elems", None, None, None, "modes"),
        P("elems", None, None, None, "modes"),
        P("elems", None),
        P("elems", None),
    )
    out_specs = (P("elems", None, None, None, "modes"), P("elems", None, None, None, "modes"))
    return jax.shard_map(
        on_device, mesh=mesh, in_specs=in_specs, out_specs=out_specs, check_vma=False
    )
```

```python
import jax
import jax.numpy as jnp
import numpy as np
from jax import lax
from jax.experimental import pallas as pl
from jax.experimental.pallas import tpu as pltpu
from jax.sharding import PartitionSpec as P

GLL = 8
NODES = GLL * GLL
ROWS = 4
CHIP_ROW = 8
time_step = 0.01
viscosity = 0.05
wave_scale = 4.0
pair_order = ((0, 0), (0, 1), (0, 2), (1, 1), (1, 2), (2, 2))
pair_index = ((0, 1, 2), (1, 3, 4), (2, 4, 5))
F32 = jnp.float32
LOW = jnp.bfloat16
MESH = pl.DeviceIdType.MESH


def legendre_table(points, quad_count):
    columns = [points * 0.0 + 1.0, points]
    for degree in range(2, quad_count):
        columns.append(
            ((2 * degree - 1) * points * columns[-1] - (degree - 1) * columns[-2]) / degree
        )
    return np.stack(columns, axis=1)


def gll_tables(quad_count):
    degree = quad_count - 1
    points = -np.cos(np.pi * np.arange(quad_count) / degree)
    for repeat in range(60):
        vander = legendre_table(points, quad_count)
        points = points - (points * vander[:, degree] - vander[:, degree - 1]) / (
            quad_count * vander[:, degree]
        )
    vander = legendre_table(points, quad_count)
    edge_value = vander[:, degree]
    weights = 2.0 / (degree * quad_count * edge_value * edge_value)
    diagonal_mask = np.arange(quad_count)[:, None] == np.arange(quad_count)[None, :]
    differ = np.where(diagonal_mask, 1.0, points[:, None] - points[None, :])
    derivative = np.where(diagonal_mask, 0.0, edge_value[:, None] / (edge_value[None, :] * differ))
    derivative[0, 0] = -degree * quad_count / 4.0
    derivative[degree, degree] = degree * quad_count / 4.0
    return (weights, derivative)


def half_tables(modes, planes):
    half = planes // 2
    turns = np.outer(np.arange(modes), 2 * np.arange(half) + 1) % (2 * planes)
    angles = np.pi * turns / planes
    factor = np.where(np.arange(modes) == 0, 1.0, 2.0)[:, None]
    synth = np.stack((factor * np.cos(angles), -factor * np.sin(angles)))
    analysis = np.stack((np.cos(angles), -np.sin(angles))) * (2.0 / planes)
    return synth, np.transpose(analysis, (0, 2, 1))


def node_tables():
    weights, deriv = gll_tables(GLL)
    wdiag = np.diag(weights)
    back = deriv.T @ wdiag
    ahead = wdiag @ deriv
    stiff = deriv.T @ wdiag @ deriv
    zero = np.zeros((NODES, NODES))
    fwd = (
        np.concatenate((np.kron(back, wdiag), np.kron(wdiag, back), np.kron(stiff, wdiag)), 1),
        np.concatenate((zero, zero, np.kron(wdiag, stiff)), 1),
    )
    adj = (
        np.concatenate((np.kron(ahead, wdiag), np.kron(wdiag, ahead), np.kron(stiff, wdiag)), 0),
        np.concatenate((zero, zero, np.kron(wdiag, stiff)), 0),
    )
    return np.stack(fwd), np.stack(adj), np.kron(weights, weights)


def step_kernel(
    groups,
    slabs,
    state_ref, adj_ref, obs_ref, spacing_h, slot_h, synth_ref, anal_ref, fwd_ref, bwd_ref, w2_ref,
    next_o, start_o,
    spacing_ref, slot_ref, state_v, adj_v, obs_v, synth_v, anal_v, fwd_v, bwd_v, w2_v,
    send_v, state_r, forcing_r, next_r, start_r, quad_v, scale_v, mult_v,
    even_v, odd_v, prod_v, modal_v, num_v, psi_v, cot_v, spread_v, pcot_v,
    edge_send, edge_recv, stage_v, full_v, mass_send, mass_recv,
    load_sem, send_sem, recv_sem, esend_sem, erecv_sem, msend_sem, mrecv_sem,
):
    member = lax.axis_index("modes")
    slab = lax.axis_index("elems")
    low_slab = lax.rem(slab + slabs - 1, slabs)
    high_slab = lax.rem(slab + 1, slabs)
    partners = (lax.rem(member + 2, 4), 3 - member, member + 1 - 2 * lax.rem(member, 2))
    modes = groups * 128
    recv = (state_r, forcing_r, next_r, start_r)

    loads = [
        pltpu.make_async_copy(src, dst, load_sem.at[i])
        for i, (src, dst) in enumerate(
            [(slot_h, slot_ref), (spacing_h, spacing_ref)]
            + [(state_ref.at[j], state_v.at[j]) for j in range(ROWS)]
            + [
                (adj_ref, adj_v), (obs_ref, obs_v), (w2_ref, w2_v),
                (fwd_ref, fwd_v), (synth_ref, synth_v), (anal_ref, anal_v), (bwd_ref, bwd_v),
            ]
        )
    ]
    adj_load, obs_load, w2_load, fwd_load, synth_load, anal_load, bwd_load = loads[2 + ROWS :]
    for load in loads:
        load.start()

    barrier = pltpu.get_barrier_semaphore()
    for partner in partners:
        pl.semaphore_signal(barrier, inc=1, device_id={"modes": partner}, device_id_type=MESH)

    place = lax.rem(slab, 2 * CHIP_ROW)
    early_low = place == 0
    early_high = place == CHIP_ROW - 1
    across_low = jnp.logical_or(early_low, place == CHIP_ROW)
    across_high = jnp.logical_or(early_high, place == 2 * CHIP_ROW - 1)
    early = jnp.logical_or(early_low, early_high)
    greet_low_now = jnp.logical_not(across_low)
    greet_high_now = jnp.logical_not(across_high)

    mirrored = place >= CHIP_ROW

    def flip(index):
        return jnp.where(mirrored, ROWS - 1 - index, index)

    row_here = flip(member)

    def around(way):
        across = (across_high, across_low)[way]
        return {
            "modes": jnp.where(across, ROWS - 1 - member, member),
            "elems": (high_slab, low_slab)[way],
        }

    def greet(way):
        pl.semaphore_signal(barrier, inc=1, device_id=around(way), device_id_type=MESH)

    @pl.when(greet_low_now)
    def _():
        greet(1)

    @pl.when(greet_high_now)
    def _():
        greet(0)

    loads[0].wait()
    loads[1].wait()
    slots = [slot_ref[0, j] for j in range(ROWS)]

    def rows_of(index, count=NODES):
        return pl.ds(index * count, count)

    def flat(block):
        return block.reshape(6 * NODES, 128)

    def elem_of(row):
        place = jnp.int32(0)
        for j in range(1, ROWS):
            place = jnp.where(slots[j] == row, j, place)
        return place

    part = NODES // 2
    halves = ((0, 6 * part), (6 * part, 12 * part))
    inner = NODES - 2 * GLL
    edges = 6 * GLL
    far = edges + 6 * inner
    spare = 4
    kept = 6 * inner - spare * GLL
    phases = (
        (0,) + halves[0],
        (1, 0, edges), (1, edges, far),
        (2, 0, kept), (2, kept, kept + 6 * GLL),
        (3,) + halves[0],
        (2, kept + 6 * GLL, kept + 12 * GLL),
        (0,) + halves[1],
        (3,) + halves[1],
        (1, far, 6 * NODES),
    )

    def swap(phase, partner, arrival=False):
        which, begin, end = phases[phase]
        rows = pl.ds(begin, end - begin)
        slot = partner if arrival else member
        return pltpu.make_async_remote_copy(
            src_ref=send_v.at[which, partner, rows],
            dst_ref=recv[which].at[slot, rows],
            send_sem=send_sem.at[phase, partner],
            recv_sem=recv_sem.at[phase, slot],
            device_id={"modes": partner},
            device_id_type=MESH,
        )

    def start(phase):
        for partner in partners:
            swap(phase, partner).start()

    def sent(phase):
        for partner in partners:
            swap(phase, partner).wait_send()

    def arrived(phase):
        for partner in partners:
            swap(phase, partner, arrival=True).wait_recv()

    for load in loads[2 : 2 + ROWS]:
        load.wait()
    for device in range(ROWS):
        block = flat(state_v[elem_of(flip(device))]).astype(LOW)
        for h in range(2):
            for i in range(6):
                begin = i * NODES + h * part
                send_v[0, device, rows_of(6 * h + i, part), :] = block[begin : begin + part]

    @pl.when(early)
    def _():
        pl.semaphore_wait(barrier, 4)

    @pl.when(jnp.logical_not(early))
    def _():
        pl.semaphore_wait(barrier, 5)

    @pl.when(jnp.logical_not(greet_low_now))
    def _():
        greet(1)

    @pl.when(jnp.logical_not(greet_high_now))
    def _():
        greet(0)

    start(0)
    start(7)
    state_r[member] = send_v[0, member]

    w2_load.wait()
    own = elem_of(row_here)
    row_above = jnp.minimum(row_here + 1, ROWS - 1)
    row_below = jnp.maximum(row_here - 1, 0)
    above = elem_of(row_above)
    below = elem_of(row_below)

    def area(elem):
        return spacing_ref[0, elem] * spacing_ref[1, elem] * 0.25

    side_x = spacing_ref[0, own]
    side_y = spacing_ref[1, own]
    full = (NODES, 128)
    layer = lax.rem(lax.broadcasted_iota(jnp.int32, full, 0), GLL)
    has_above = jnp.logical_and(layer == GLL - 1, row_here < ROWS - 1)
    has_below = jnp.logical_and(layer == 0, row_here > 0)
    w2 = w2_v[...]
    quad = w2 * area(own)
    quad_v[...] = quad
    mass = quad + jnp.where(has_above, w2 * area(above), 0.0)
    mass = mass + jnp.where(has_below, w2 * area(below), 0.0)
    at_wall = jnp.logical_and(layer == 0, row_here == 0)
    keep = jnp.where(at_wall, 0.0, 1.0)
    scale_v[...] = keep / mass
    mass_send[0] = mass[NODES - GLL :]
    mass_send[1] = mass[:GLL]

    def mass_copy(way):
        return pltpu.make_async_remote_copy(
            src_ref=mass_send.at[way],
            dst_ref=mass_recv.at[way],
            send_sem=msend_sem.at[way],
            recv_sem=mrecv_sem.at[way],
            device_id=around(way),
            device_id_type=MESH,
        )

    copies = jnp.where(jnp.logical_or(has_above, has_below), 2.0, 1.0).astype(F32)
    node_a = lax.broadcasted_iota(jnp.int32, full, 0) // GLL
    mult_v[...] = jnp.where(jnp.logical_or(node_a == 0, node_a == GLL - 1), 2.0 * copies, copies)

    edge_rows = 6 * GLL * groups
    top = pl.ds(GLL - 1, edge_rows, stride=GLL)
    low = pl.ds(0, edge_rows, stride=GLL)

    def edge_copy(which, way):
        if way == 0:
            target = {"modes": flip(row_above)}
        elif way == 1:
            target = {"modes": flip(row_below)}
        else:
            target = around(way - 2)
        return pltpu.make_async_remote_copy(
            src_ref=edge_send.at[which, way],
            dst_ref=edge_recv.at[which, way],
            send_sem=esend_sem.at[which, way],
            recv_sem=erecv_sem.at[which, way],
            device_id=target,
            device_id_type=MESH,
        )

    def pack_around(which, buf):
        for way, begin in ((2, NODES - GLL), (3, 0)):
            edge_send[which, way] = jnp.concatenate(
                [buf[pl.ds(i * NODES + begin, GLL), :] for i in range(6 * groups)], axis=0
            ).astype(LOW)

    def add_around(which, buf):
        for way, begin in ((2, 0), (3, NODES - GLL)):
            edge_copy(which, way).wait_recv()
            came = edge_recv[which, way].astype(F32)
            for i in range(6 * groups):
                rows = pl.ds(i * NODES + begin, GLL)
                buf[rows, :] = buf[rows, :] + came[i * GLL : (i + 1) * GLL]

    def around_sent(which):
        for way in (2, 3):
            edge_copy(which, way).wait_send()

    adj_load.wait()
    obs_load.wait()
    for row in range(ROWS):
        elem = elem_of(row)
        psi_v[rows_of(row, 6 * NODES), :] = flat(adj_v[elem] - obs_v[elem].astype(F32))
    for row in range(ROWS - 1):
        lower = pl.ds(row * 6 * NODES + GLL - 1, 6 * GLL, stride=GLL)
        upper = pl.ds((row + 1) * 6 * NODES, 6 * GLL, stride=GLL)
        both = psi_v[lower, :] + psi_v[upper, :]
        psi_v[lower, :] = both
        psi_v[upper, :] = both
    slab_edge = pltpu.make_async_remote_copy(
        src_ref=edge_send.at[0, 1],
        dst_ref=edge_recv.at[0, 1],
        send_sem=esend_sem.at[0, 1],
        recv_sem=erecv_sem.at[0, 1],
        device_id={"elems": high_slab},
        device_id_type=MESH,
    )
    edge_send[0, 1] = jnp.concatenate(
        [psi_v[pl.ds((i + 1) * NODES - GLL, GLL), :] for i in range(6 * ROWS)], axis=0
    ).astype(LOW)

    @pl.when(jnp.logical_not(across_high))
    def _():
        slab_edge.start()

    for row in range(ROWS):
        device = flip(row)
        for i in range(6):
            base = (6 * row + i) * NODES
            send_v[1, device, pl.ds(edges + i * inner, inner), :] = psi_v[
                pl.ds(base + GLL, inner), :
            ].astype(LOW)

    @pl.when(jnp.logical_not(across_low))
    def _():
        slab_edge.wait_recv()
        came = edge_recv[0, 1].astype(F32)
        for i in range(6 * ROWS):
            rows = pl.ds(i * NODES, GLL)
            psi_v[rows, :] = psi_v[rows, :] + came[i * GLL : (i + 1) * GLL]

    for row in range(ROWS):
        device = flip(row)
        for begin, offset in ((0, 0), (far, NODES - GLL)):
            send_v[1, device, pl.ds(begin, edges), :] = jnp.concatenate(
                [psi_v[pl.ds((6 * row + i) * NODES + offset, GLL), :] for i in range(6)], axis=0
            ).astype(LOW)
    forcing_r[member] = send_v[1, member]
    fwd_load.wait()
    bwd_load.wait()
    lane = lax.broadcasted_iota(jnp.int32, (NODES, 3 * NODES), 1)
    ratio = jnp.full((NODES, 3 * NODES), side_y) / jnp.full((NODES, 3 * NODES), side_x)
    coef = jnp.where(
        lane < NODES, 0.5 * side_y, jnp.where(lane < 2 * NODES, 0.5 * side_x, -viscosity * ratio)
    )
    fwd_mat = (time_step * (fwd_v[0] * coef - fwd_v[1] * (viscosity / ratio))).astype(LOW)
    line = lax.broadcasted_iota(jnp.int32, (3 * NODES, NODES), 0)
    ratio = jnp.full((3 * NODES, NODES), side_y) / jnp.full((3 * NODES, NODES), side_x)
    coef = jnp.where(
        line < NODES, 0.5 * side_y, jnp.where(line < 2 * NODES, 0.5 * side_x, -viscosity * ratio)
    )
    bwd_mat = (bwd_v[0] * coef - bwd_v[1] * (viscosity / ratio)).astype(LOW)

    def state_part(h, i):
        rows = rows_of(6 * h + i, part)
        return jnp.concatenate([state_r[q, rows, :] for q in range(groups)], axis=1)

    def wide(block):
        return jnp.concatenate([block] * groups, axis=1)

    def field(buf, i):
        return jnp.concatenate([buf[rows_of(6 * q + i), :] for q in range(groups)], axis=1)

    def set_field(buf, i, value):
        for q in range(groups):
            buf[rows_of(6 * q + i), :] = value[:, q * 128 : (q + 1) * 128]

    mode_ids = lax.broadcasted_iota(jnp.int32, (NODES, modes), 1)
    wave = mode_ids.astype(F32) * (wave_scale / modes)

    synth_load.wait()
    anal_load.wait()

    def half_rows(index, h):
        return pl.ds(index * NODES + h * part, part)

    for h in range(2):
        if h == 0:
            arrived(0)
        else:
            sent(0)
            sent(7)
            start(1)

            @pl.when(across_high)
            def _():
                start(9)

            arrived(7)
        for p, planes in ((0, even_v), (1, odd_v)):
            values = jnp.dot(
                jnp.concatenate([state_part(h, 2 * c + p) for c in range(3)], axis=0),
                synth_v[p],
                preferred_element_type=F32,
            )
            for c in range(3):
                planes[half_rows(c, h), :] = values[c * part : (c + 1) * part]
        for q, (left, right) in enumerate(pair_order):
            el, ol = even_v[half_rows(left, h), :], odd_v[half_rows(left, h), :]
            er, orr = even_v[half_rows(right, h), :], odd_v[half_rows(right, h), :]
            prod_v[0, rows_of(6 * h + q, part), :] = (el * er + ol * orr).astype(LOW)
            prod_v[1, rows_of(6 * h + q, part), :] = (el * orr + ol * er).astype(LOW)
        for p in range(2):
            values = jnp.dot(
                prod_v[p, rows_of(h, 6 * part), :], anal_v[p], preferred_element_type=F32
            ).astype(LOW)
            for q in range(6):
                modal_v[p, half_rows(q, h), :] = values[q * part : (q + 1) * part]

    for c in range(3):
        for p in range(2):
            values = jnp.concatenate([state_part(h, 2 * c + p) for h in range(2)], axis=0)
            stack = jnp.concatenate(
                [
                    modal_v[p, rows_of(pair_index[0][c]), :],
                    modal_v[p, rows_of(pair_index[1][c]), :],
                    values,
                ],
                axis=0,
            )
            flux_z = modal_v[1 - p, rows_of(pair_index[2][c]), :].astype(F32)
            turn = (-time_step if p == 1 else time_step) * wave
            local = (1.0 - time_step * viscosity * wave * wave) * values.astype(F32)
            set_field(
                num_v,
                2 * c + p,
                jnp.dot(fwd_mat, stack, preferred_element_type=F32)
                + wide(quad_v[...]) * (local + turn * flux_z),
            )

    @pl.when(row_here < ROWS - 1)
    def _():
        edge_send[1, 0] = num_v[top, :].astype(LOW)
        edge_copy(1, 0).start()

    @pl.when(row_here > 0)
    def _():
        edge_send[1, 1] = num_v[low, :].astype(LOW)
        edge_copy(1, 1).start()

    start(2)

    @pl.when(early)
    def _():
        pl.semaphore_wait(barrier, 1)

    mass_copy(0).start()
    mass_copy(1).start()
    arrived(1)
    for q in range(groups):
        edge_send[0, 3, pl.ds(q * edges, edges), :] = forcing_r[q, pl.ds(0, edges), :]
    edge_copy(0, 3).start()

    @pl.when(across_high)
    def _():
        arrived(9)
        for q in range(groups):
            edge_send[0, 2, pl.ds(q * edges, edges), :] = forcing_r[q, pl.ds(far, edges), :]
        edge_copy(0, 2).start()

    @pl.when(jnp.logical_not(across_high))
    def _():
        edge_send[0, 2] = jnp.zeros((edge_rows, 128), LOW)

    @pl.when(row_here > 0)
    def _():
        edge_copy(1, 0).wait_recv()
        num_v[low, :] = num_v[low, :] + edge_recv[1, 0].astype(F32)

    @pl.when(row_here < ROWS - 1)
    def _():
        edge_copy(1, 1).wait_recv()
        num_v[top, :] = num_v[top, :] + edge_recv[1, 1].astype(F32)

    pack_around(1, num_v)
    edge_copy(1, 2).start()
    edge_copy(1, 3).start()
    for q in range(groups):
        for i in range(6):
            rows = pl.ds((6 * q + i) * NODES + GLL, inner)
            value = scale_v[GLL : NODES - GLL, :] * num_v[rows, :]
            num_v[rows, :] = value
            if i < 5:
                stage_v[q, pl.ds(i * inner, inner), :] = value
            else:
                stage_v[q, pl.ds(i * inner, inner - spare * GLL), :] = value[: inner - spare * GLL]
                for k in range(spare):
                    tile = value[inner - (spare - k) * GLL : inner - (spare - k - 1) * GLL]
                    stage_v[q, pl.ds(k * GLL * GLL, GLL, stride=GLL), :] = tile
        send_v[2, q, pl.ds(0, kept), :] = stage_v[q].astype(LOW)
    next_r[member, pl.ds(0, kept), :] = send_v[2, member, pl.ds(0, kept), :]
    start(3)
    arrived(2)
    for q in range(groups):
        block = forcing_r[q, pl.ds(edges, 6 * inner), :].astype(F32)
        for i in range(6):
            rows = pl.ds((6 * q + i) * NODES + GLL, inner)
            inside = pl.ds(GLL, inner)
            psi_v[rows, :] = scale_v[inside, :] * (
                block[i * inner : (i + 1) * inner] + mult_v[inside, :] * num_v[rows, :]
            )
    mass_copy(0).wait()
    mass_copy(1).wait()
    scale_v[:GLL, :] = keep[:GLL] / (mass_send[1] + mass_recv[0])
    scale_v[NODES - GLL :, :] = keep[NODES - GLL :] / (mass_send[0] + mass_recv[1])
    add_around(1, num_v)
    for q in range(groups):
        for i in range(6):
            base = (6 * q + i) * NODES
            low_edge = scale_v[:GLL, :] * num_v[pl.ds(base, GLL), :]
            num_v[pl.ds(base, GLL), :] = low_edge
            high_edge = scale_v[NODES - GLL :, :] * num_v[pl.ds(base + NODES - GLL, GLL), :]
            num_v[pl.ds(base + NODES - GLL, GLL), :] = high_edge
            stage_v[q, pl.ds(i * GLL, GLL), :] = low_edge
            stage_v[q, pl.ds((6 + i) * GLL, GLL), :] = high_edge
        send_v[2, q, pl.ds(kept, 12 * GLL), :] = stage_v[q, pl.ds(0, 12 * GLL), :].astype(LOW)
    next_r[member, pl.ds(kept, 12 * GLL), :] = send_v[2, member, pl.ds(kept, 12 * GLL), :]
    start(4)

    @pl.when(across_high)
    def _():
        start(6)

    edge_copy(0, 3).wait_recv()
    far_edge = edge_send[0, 2].astype(F32) + edge_recv[0, 3].astype(F32)
    for q in range(groups):
        near_edge = forcing_r[q, pl.ds(0, edges), :].astype(F32)
        for i in range(6):
            base = (6 * q + i) * NODES
            psi_v[pl.ds(base, GLL), :] = near_edge[i * GLL : (i + 1) * GLL]
            psi_v[pl.ds(base + NODES - GLL, GLL), :] = far_edge[
                (6 * q + i) * GLL : (6 * q + i + 1) * GLL
            ]

    @pl.when(across_low)
    def _():
        edge_copy(0, 2).wait_recv()
        came = edge_recv[0, 2].astype(F32)
        for i in range(6 * groups):
            rows = pl.ds(i * NODES, GLL)
            psi_v[rows, :] = psi_v[rows, :] + came[i * GLL : (i + 1) * GLL]

    for i in range(6 * groups):
        for begin in (0, NODES - GLL):
            side = pl.ds(begin, GLL)
            rows = pl.ds(i * NODES + begin, GLL)
            psi_v[rows, :] = scale_v[side, :] * (psi_v[rows, :] + mult_v[side, :] * num_v[rows, :])

    norm = jnp.where(mode_ids == 0, 1.0 / (3.0 * modes), 0.5 / (3.0 * modes)).astype(F32)
    for p in range(2):
        lateral = []
        for c in range(3):
            psi = field(psi_v, 2 * c + p)
            other = field(psi_v, 2 * c + 1 - p)
            grads = jnp.dot(bwd_mat, psi.astype(LOW), preferred_element_type=F32)
            set_field(
                num_v,
                2 * c + p,
                wide(quad_v[...]) * ((1.0 - time_step * viscosity * wave * wave) * psi)
                + time_step * grads[2 * NODES :],
            )
            turn = -wave if p == 0 else wave
            lateral.append((grads[:NODES], grads[NODES : 2 * NODES], wide(quad_v[...]) * (turn * other)))
        for q, (left, right) in enumerate(pair_order):
            cot = lateral[right][left] + lateral[left][right]
            cot = (norm * cot).astype(LOW)
            for h in range(2):
                cot_v[p, rows_of(6 * h + q, part), :] = cot[h * part : (h + 1) * part]

    gain = jnp.where(mode_ids == 0, 3.0 * modes * time_step, 6.0 * modes * time_step).astype(F32)
    gain = gain[:part]
    for h in range(2):
        for p in range(2):
            spread_v[p] = jnp.dot(
                cot_v[p, rows_of(h, 6 * part), :], synth_v[p], preferred_element_type=F32
            )
        for c in range(3):
            even = jnp.zeros((part, even_v.shape[1]), F32)
            odd = jnp.zeros((part, even_v.shape[1]), F32)
            for d in range(3):
                se = spread_v[0, rows_of(pair_index[c][d], part), :]
                so = spread_v[1, rows_of(pair_index[c][d], part), :]
                ed, od = even_v[half_rows(d, h), :], odd_v[half_rows(d, h), :]
                even = even + (se * ed + so * od)
                odd = odd + (se * od + so * ed)
            pcot_v[0, rows_of(c, part), :] = even.astype(LOW)
            pcot_v[1, rows_of(c, part), :] = odd.astype(LOW)
        for p in range(2):
            back = jnp.dot(pcot_v[p], anal_v[p], preferred_element_type=F32)
            for c in range(3):
                i = 2 * c + p
                near = gain * back[c * part : (c + 1) * part]
                for q in range(groups):
                    rest = num_v[half_rows(6 * q + i, h), :]
                    send_v[3, q, rows_of(6 * h + i, part), :] = (
                        rest + near[:, q * 128 : (q + 1) * 128]
                    ).astype(LOW)
        start((5, 8)[h])
    start_r[member] = send_v[3, member]

    sent(1)
    sent(2)
    sent(3)
    sent(4)

    @pl.when(across_high)
    def _():
        sent(6)

    edge_copy(0, 3).wait_send()
    around_sent(1)

    @pl.when(across_high)
    def _():
        sent(9)
        edge_copy(0, 2).wait_send()

    @pl.when(jnp.logical_not(across_high))
    def _():
        slab_edge.wait_send()


    @pl.when(row_here < ROWS - 1)
    def _():
        edge_copy(1, 0).wait_send()

    @pl.when(row_here > 0)
    def _():
        edge_copy(1, 1).wait_send()

    arrived(3)
    arrived(4)
    for row in range(ROWS):
        edge_send[0, 0, pl.ds(row * 6 * GLL, 6 * GLL), :] = next_r[
            flip(row), pl.ds(kept, 6 * GLL), :
        ]
    side_copy = pltpu.make_async_remote_copy(
        src_ref=edge_send.at[0, 0],
        dst_ref=edge_recv.at[0, 0],
        send_sem=esend_sem.at[0, 0],
        recv_sem=erecv_sem.at[0, 0],
        device_id={"elems": low_slab},
        device_id_type=MESH,
    )

    @pl.when(jnp.logical_not(across_low))
    def _():
        side_copy.start()

    for row in range(ROWS):
        block = next_r[flip(row), pl.ds(0, kept + 6 * GLL), :].astype(F32)
        stage_v[row] = block[:kept]
        for i in range(6):
            full_v[row, pl.ds(i * NODES, GLL), :] = block[kept + i * GLL : kept + (i + 1) * GLL]
            count = inner if i < 5 else inner - spare * GLL
            full_v[row, pl.ds(i * NODES + GLL, count), :] = block[i * inner : i * inner + count]
        for k in range(spare):
            tile = stage_v[row, pl.ds(k * GLL * GLL, GLL, stride=GLL), :]
            full_v[row, pl.ds(6 * NODES - (spare - k + 1) * GLL, GLL), :] = tile

    @pl.when(jnp.logical_not(across_low))
    def _():
        side_copy.wait_send()

    @pl.when(jnp.logical_not(across_high))
    def _():
        side_copy.wait_recv()

    @pl.when(across_high)
    def _():
        arrived(6)
        for row in range(ROWS):
            edge_recv[0, 0, pl.ds(row * 6 * GLL, 6 * GLL), :] = next_r[
                flip(row), pl.ds(kept + 6 * GLL, 6 * GLL), :
            ]

    for row in range(ROWS):
        side = edge_recv[0, 0, pl.ds(row * 6 * GLL, 6 * GLL), :].astype(F32)
        for i in range(6):
            full_v[row, pl.ds((i + 1) * NODES - GLL, GLL), :] = side[i * GLL : (i + 1) * GLL]
        if row == 0:
            shared = jnp.zeros((6 * GLL, 128), F32)
        else:
            shared = full_v[row - 1, pl.ds(GLL - 1, 6 * GLL, stride=GLL), :]
        full_v[row, pl.ds(0, 6 * GLL, stride=GLL), :] = shared
    for j in range(ROWS):
        next_o[j] = full_v[slots[j]].reshape(3, 2, NODES, 128)
    arrived(5)
    arrived(8)
    for j in range(ROWS):
        block = start_r[flip(slots[j])].astype(F32)
        for h in range(2):
            for i in range(6):
                begin = (6 * h + i) * part
                start_o[j, i // 2, i % 2, rows_of(h, part), :] = block[begin : begin + part]
    sent(5)
    sent(8)


def store_kernel(next_v, start_v, next_ref, start_ref, sem):
    stores = [
        pltpu.make_async_copy(source.at[j], target.at[j], sem.at[which, j])
        for which, (source, target) in enumerate(((next_v, next_ref), (start_v, start_ref)))
        for j in range(ROWS)
    ]
    for store in stores:
        store.start()
    for store in stores:
        store.wait()


def on_device(state, adjoint_end, observed, spacing, radial_slot):
    groups = lax.axis_size("modes")
    slabs = lax.axis_size("elems")
    modes = groups * state.shape[4]
    half = 3 * modes // 2
    synth, analysis = half_tables(modes, 3 * modes)
    fwd, bwd, w2 = node_tables()
    any_spec = pl.BlockSpec(memory_space=pltpu.HBM)
    vmem_spec = pl.BlockSpec(memory_space=pltpu.VMEM)
    local = state.shape
    block = (6 * NODES, 128)
    vm = pltpu.VMEM
    sem = pltpu.SemaphoreType.DMA

    def run(*args):
        step_kernel(groups, slabs, *args)

    held_out = pltpu.VMEM(local, F32)

    def held(array):
        return pltpu.with_memory_space_constraint(array, pltpu.HBM)

    next_v, start_v = pl.pallas_call(
        run,
        out_shape=(held_out, held_out),
        in_specs=[any_spec] * 10,
        out_specs=(vmem_spec, vmem_spec),
        scratch_shapes=[
            pltpu.SMEM((2, ROWS), F32), pltpu.SMEM((1, ROWS), jnp.int32),
            vm(local, F32), vm(local, F32), vm(local, LOW),
            vm((2, modes, half), LOW), vm((2, half, modes), LOW),
            vm((2, NODES, 3 * NODES), F32), vm((2, 3 * NODES, NODES), F32), vm((NODES, 128), F32),
            vm((4, ROWS) + block, LOW), *[vm((ROWS,) + block, LOW)] * 4,
            vm((NODES, 128), F32), vm((NODES, 128), F32), vm((NODES, 128), F32),
            vm((3 * NODES, half), F32), vm((3 * NODES, half), F32),
            vm((2, 6 * NODES, half), LOW), vm((2, 6 * NODES, modes), LOW),
            vm((6 * NODES * groups, 128), F32), vm((6 * NODES * groups, 128), F32),
            vm((2, 6 * NODES, modes), LOW), vm((2, 3 * NODES, half), F32),
            vm((2, 3 * NODES // 2, half), LOW),
            vm((2, 4, 6 * GLL * groups, 128), LOW), vm((2, 4, 6 * GLL * groups, 128), LOW),
            vm((ROWS, 256, 128), F32), vm((ROWS,) + block, F32),
            vm((2, GLL, 128), F32), vm((2, GLL, 128), F32),
            sem((9 + ROWS,)), sem((10, ROWS)), sem((10, ROWS)), sem((2, 4)), sem((2, 4)),
            sem((2,)), sem((2,)),
        ],
        compiler_params=pltpu.CompilerParams(
            collective_id=0, has_side_effects=True, vmem_limit_bytes=48 * 1024 * 1024
        ),
        cost_estimate=pl.CostEstimate(
            flops=1900000000, bytes_accessed=7000000, transcendentals=0
        ),
    )(
        held(state), held(adjoint_end), held(observed), held(spacing.T), held(radial_slot),
        held(jnp.asarray(synth, F32).astype(LOW)), held(jnp.asarray(analysis, F32).astype(LOW)),
        held(jnp.asarray(fwd, F32)), held(jnp.asarray(bwd, F32)),
        held(jnp.asarray(np.broadcast_to(w2[:, None], (NODES, 128)), F32)),
    )
    return pl.pallas_call(
        store_kernel,
        out_shape=(jax.ShapeDtypeStruct(local, F32), jax.ShapeDtypeStruct(local, F32)),
        in_specs=[pl.BlockSpec(memory_space=pl.ANY)] * 2,
        out_specs=(any_spec, any_spec),
        scratch_shapes=[sem((2, ROWS))],
        compiler_params=pltpu.CompilerParams(vmem_limit_bytes=1024 * 1024),
    )(next_v, start_v)


def solution(mesh):
    in_specs = (
        P("elems", None, None, None, "modes"),
        P("elems", None, None, None, "modes"),
        P("elems", None, None, None, "modes"),
        P("elems", None),
        P("elems", None),
    )
    out_specs = (P("elems", None, None, None, "modes"), P("elems", None, None, None, "modes"))
    return jax.shard_map(
        on_device, mesh=mesh, in_specs=in_specs, out_specs=out_specs, check_vma=False
    )
```
